256 devices in a mesh: dp: 4 (over x), context: 4 (over y), tensor: 16 (over z, core).
Axes of the slice: x: 4, y: 4, z: 8, core: 2. Of those that a mesh axis runs over, the one named last changes fastest.
Arguments:
- head_inputs: bfloat16 [4, 1024, 16384], P('dp', 'context', 'tensor'), may hold values from -6 to 6
- gate_inputs: bfloat16 [4, 1024, 16384], P('dp', 'context', 'tensor'), may hold values from -6 to 6
- step_raw: float32 [4, 1024, 256], P('dp', 'context', 'tensor'), may hold values from -4 to 4
- state_write: bfloat16 [4, 1024, 1024], P('dp', 'context', 'tensor'), may hold values from -1 to 1
- state_read: bfloat16 [4, 1024, 1024], P('dp', 'context', 'tensor'), may hold values from -1 to 1
- log_rate: float32 [256], P('tensor'), may hold values from -12 to -2
- skip_gain: float32 [256], P('tensor'), may hold values from 0.5 to 1.5
- step_bias: float32 [256], P('tensor'), may hold values from -1 to 1
- grad_gated: bfloat16 [4, 1024, 16384], P('dp', 'context', 'tensor'), may hold values from -6 to 6
Outputs:
- grad_inputs: bfloat16 [4, 1024, 16384], P('dp', 'context', 'tensor')
- grad_gates: bfloat16 [4, 1024, 16384], P('dp', 'context', 'tensor')
- grad_write: float32 [4, 1024, 1024], P('dp', 'context', 'tensor')
- grad_read: float32 [4, 1024, 1024], P('dp', 'context', 'tensor')
- grad_step: float32 [4, 1024, 256], P('dp', 'context', 'tensor')
- grad_rate: float32 [256], P('tensor')
- grad_skip: float32 [256], P('tensor')
- grad_bias: float32 [256], P('tensor')
The draws below stay inside these ranges and needn't reach their ends.
All inputs are finite; a program needn't handle non-finite values.
Results may differ from the reference program's by a relative error of at most 0.015.
Values may be sent and summed in bfloat16 or wider, within the bound.
No kernel may reach another device: no remote copies, remote signals or barrier semaphores. Data moves between devices by JAX's collectives and lax.ppermute only.
A program may use at most 64 MiB of HBM per device.

```python
import math
import jax
import jax.numpy as jnp
from jax import lax

HEADS = 256
HEAD_DIM = 64
GROUPS = 8
STATE = 128
STRETCH = 128
SEQ = 1024
BATCH = 4


def draw_log_rate(key, part):
    key = jax.random.fold_in(key, 7)
    spread = jax.random.uniform(key, (HEADS,), jnp.float32)
    bottom = math.log(0.5 / SEQ)
    upper_end = math.log(0.05)
    return bottom + (upper_end - bottom) * spread


def shard_levels(own_key, shape, shards, least, largest):
    def one(axis_at, blocks):
        draws = jax.random.uniform(jax.random.fold_in(jax.random.fold_in(own_key, 6), axis_at), (blocks,), jnp.float32, least / len(shards), largest / len(shards))
        return jnp.repeat(jnp.exp(draws), shape[axis_at] // blocks).reshape((-1,) + (1,) * (len(shape) - axis_at - 1))

    level = one(*shards[0])
    for cut in shards[1:]:
        level = level * one(*cut)
    return level


def noise(rng, shape, scale, bound, cuts=(), dtype=jnp.bfloat16):
    gain = shard_levels(rng, shape, cuts, -0.22, 0.18) if cuts else 1.0
    drawn = jax.random.normal(rng, shape, jnp.float32) * scale * gain
    return jnp.minimum(jnp.maximum(drawn, -bound), bound).astype(dtype)


def setup_inputs(seed: int = 0) -> dict:
    key_list = jax.random.split(jax.random.key(seed), 10)
    return {
        "head_inputs": noise(key_list[0], (BATCH, SEQ, HEADS * HEAD_DIM), 1.0, 6.0, ((0, 4), (1, 4), (2, 16))),
        "gate_inputs": noise(key_list[1], (BATCH, SEQ, HEADS * HEAD_DIM), 1.0, 6.0, ((0, 4), (1, 4), (2, 16))),
        "step_raw": noise(key_list[2], (BATCH, SEQ, HEADS), 1.0, 4.0, ((0, 4), (1, 4), (2, 16)), jnp.float32),
        "state_write": noise(key_list[3], (BATCH, SEQ, GROUPS * STATE), 0.15, 1.0, ((0, 4), (1, 4), (2, 16))),
        "state_read": noise(key_list[4], (BATCH, SEQ, GROUPS * STATE), 0.15, 1.0, ((0, 4), (1, 4), (2, 16))),
        "log_rate": draw_log_rate(jax.random.fold_in(key_list[9], 71), 0),
        "skip_gain": jnp.clip(0.5 + 1.0 * jax.random.uniform(key_list[6], (HEADS,), jnp.float32) ** shard_levels(key_list[6], (HEADS,), ((0, 16),), -0.2, 0.2), 0.5, 1.5),
        "step_bias": jnp.clip(jax.random.uniform(key_list[7], (HEADS,), jnp.float32, -1.0, 1.0) * shard_levels(key_list[7], (HEADS,), ((0, 16),), -0.4, 0.0), -1.0, 1.0),
        "grad_gated": noise(key_list[8], (BATCH, SEQ, HEADS * HEAD_DIM), 1.0, 6.0, ((0, 4), (1, 4), (2, 16))),
    }


HIGHEST = lax.Precision.HIGHEST

def stretch_step(carried, pieces, decay_rates, skip_gain):
    values, step_sizes, write_keys, read_keys, gate_values = pieces
    value_half = values.astype(jnp.bfloat16)
    write_half = write_keys.astype(jnp.bfloat16)
    log_decay = -decay_rates * step_sizes
    running = jnp.cumsum(log_decay, axis=0)
    closing = running[-1]
    by_head = jnp.moveaxis(running, 0, -1)
    length = running.shape[0]
    causal = lax.broadcasted_iota(jnp.int32, (length, length), 0) >= lax.broadcasted_iota(jnp.int32, (length, length), 1)
    spread = by_head[..., :, None] - by_head[..., None, :]
    damping = jnp.exp(jnp.where(causal, spread, -jnp.inf))
    intersection = jnp.einsum('tgn,sgn->gts', read_keys.astype(jnp.bfloat16), write_half, preferred_element_type=jnp.float32)
    weights = (damping * intersection[:, None] * jnp.moveaxis(step_sizes, 0, -1)[..., None, :]).astype(jnp.bfloat16)
    within = jnp.einsum('gkts,sgkp->tgkp', weights, value_half, preferred_element_type=jnp.float32)
    earlier = jnp.einsum('tgn,gkpn->tgkp', read_keys, carried, precision=HIGHEST) * jnp.exp(running)[..., None]
    output = (within + earlier + skip_gain[..., None] * values) * jax.nn.silu(gate_values)
    leftover = ((jnp.exp(closing[None] - running) * step_sizes)[..., None] * values).astype(jnp.bfloat16)
    updated = jnp.exp(closing)[..., None, None] * carried + jnp.einsum('sgkp,sgn->gkpn', leftover, write_half, preferred_element_type=jnp.float32)
    return (updated, output)

def sequence_forward(head_values, gate_values, raw_steps, write_keys, read_keys, rate_log, skips, bias):
    blocks = SEQ // STRETCH
    per_group = HEADS // GROUPS
    values = head_values.reshape(blocks, STRETCH, GROUPS, per_group, HEAD_DIM)
    gates = gate_values.reshape(blocks, STRETCH, GROUPS, per_group, HEAD_DIM)
    step_sizes = jax.nn.softplus(raw_steps + bias).reshape(blocks, STRETCH, GROUPS, per_group)
    writes = write_keys.reshape(blocks, STRETCH, GROUPS, STATE)
    reads = read_keys.reshape(blocks, STRETCH, GROUPS, STATE)
    decay_rates = jnp.exp(rate_log).reshape(GROUPS, per_group)
    skip_gain = skips.reshape(GROUPS, per_group)

    def advance(carried, pieces):
        return jax.checkpoint(stretch_step)(carried, pieces, decay_rates, skip_gain)
    start = jnp.zeros((GROUPS, per_group, HEAD_DIM, STATE), jnp.float32)
    final, gated = lax.scan(advance, start, (values, step_sizes, writes, reads, gates))
    return gated.reshape(SEQ, HEADS * HEAD_DIM)

def reference(head_inputs, gate_inputs, step_raw, state_write, state_read, log_rate, skip_gain, step_bias, grad_gated):

    def forward(values, gates, raw_steps, writes, reads, rate_log, skips, bias):
        mapped = jax.vmap(sequence_forward, in_axes=(0, 0, 0, 0, 0, None, None, None))
        return mapped(values, gates, raw_steps, writes, reads, rate_log, skips, bias)
    gated, pullback = jax.vjp(forward, head_inputs.astype(jnp.float32), gate_inputs.astype(jnp.float32), step_raw, state_write.astype(jnp.float32), state_read.astype(jnp.float32), log_rate, skip_gain, step_bias)
    grads = pullback(grad_gated.astype(jnp.float32))
    grad_values, grad_gate_part, grad_steps, grad_writes, grad_reads, grad_rates, grad_skips, grad_biases = grads
    return (grad_values.astype(jnp.bfloat16), grad_gate_part.astype(jnp.bfloat16), grad_writes, grad_reads, grad_steps, grad_rates, grad_skips, grad_biases)
```

```python
import functools
import math

import jax
import jax.numpy as jnp
from jax import lax
from jax.experimental import pallas as pl
from jax.experimental.pallas import tpu as pltpu
from jax.sharding import PartitionSpec as P

HEAD_DIM = 64
STATE = 128
BLOCK = 128
LOG2E = math.log2(math.e)
F32 = jnp.float32
BF16 = jnp.bfloat16
TILE = 256


def dot(a, b, dims=((1,), (0,))):
    return lax.dot_general(a, b, (dims, ((), ())), preferred_element_type=F32)


def pieces(v, count):
    out = []
    for _ in range(count):
        part = v.astype(BF16)
        out.append(part)
        v = v - part.astype(F32)
    return out


def split_dot_left(exact, v, count):
    return sum(dot(exact, part) for part in pieces(v, count))


def split_dot_right(v, exact, count):
    return sum(dot(part, exact) for part in pieces(v, count))


def expander(heads, lo, size):
    head = lax.broadcasted_iota(jnp.int32, (heads, size), 0)
    column = lax.broadcasted_iota(jnp.int32, (heads, size), 1) + lo
    return ((column >= head * HEAD_DIM) & (column < (head + 1) * HEAD_DIM)).astype(BF16)


def selector(heads, lo, size):
    head = lax.broadcasted_iota(jnp.int32, (size, heads), 1)
    column = lax.broadcasted_iota(jnp.int32, (size, heads), 0) + lo
    return ((column >= head * HEAD_DIM) & (column < (head + 1) * HEAD_DIM)).astype(BF16)


def triangle(rows, lower):
    i = lax.broadcasted_iota(jnp.int32, (rows, rows), 0)
    j = lax.broadcasted_iota(jnp.int32, (rows, rows), 1)
    return ((i >= j) if lower else (i <= j)).astype(BF16)


def softplus(z):
    return jnp.maximum(z, 0.0) + jnp.log(1.0 + jnp.exp(-jnp.abs(z)))


def both(own_ref, other_ref):
    return jnp.concatenate([own_ref[...], other_ref[...]], axis=1)


def kernel_local(
    x_ref, g_ref, dy_ref, raw_ref, bias_ref, rate_ref, wo_ref, wt_ref, ro_ref, rt_ref,
    up_ref, down_ref, ua_ref, xb_ref, al_ref, be_ref, wide_ref, small_ref,
    al_e, be_e,
):
    rows, cols = x_ref.shape
    heads = raw_ref.shape[1]
    step = softplus(raw_ref[...] + bias_ref[...])
    log2_decay = step * (-LOG2E * jnp.exp(rate_ref[...]))
    run = split_dot_left(triangle(rows, True), log2_decay, 3)
    mid0 = run[BLOCK // 2 - 1 : BLOCK // 2]
    mid1 = run[BLOCK + BLOCK // 2 - 1 : BLOCK + BLOCK // 2]
    end = run[rows - 1 : rows]
    row = lax.broadcasted_iota(jnp.int32, (rows, heads), 0)
    rel = run - jnp.where(row < BLOCK, mid0, mid1)
    al = jnp.exp2(rel)
    be = jnp.exp2(-rel) * step
    al_ref[...] = al
    be_ref[...] = be
    small = jnp.exp2(
        jnp.concatenate([mid0, mid1, end - mid0, end - mid1, mid1 - mid0, end, end, end], axis=0)
    )
    small_ref[...] = small
    for lo in range(0, cols, TILE):
        wide = expander(heads, lo, TILE)
        here = pl.ds(lo, TILE)
        al_e[:, here] = split_dot_right(al, wide, 2)
        be_e[:, here] = split_dot_right(be, wide, 2)
        wide_ref[:, here] = split_dot_right(small, wide, 3)
    writes = both(wo_ref, wt_ref).astype(F32).T.astype(BF16)
    reads = both(ro_ref, rt_ref).astype(F32).T.astype(BF16)
    place = lax.axis_index("context")
    last = lax.axis_size("context") - 1
    tail = pl.ds(cols, 8)
    for lo in range(0, cols, BLOCK):
        here = pl.ds(lo, BLOCK)
        state = None
        adjoint = None
        for b in range(rows // BLOCK):
            at = pl.ds(b * BLOCK, BLOCK)
            g = g_ref[at, here].astype(F32)
            u = dy_ref[at, here].astype(F32) * g / (1.0 + jnp.exp(-g))
            ua = (u * al_e[at, here]).astype(BF16)
            xb = (x_ref[at, here].astype(F32) * be_e[at, here]).astype(BF16)
            ua_ref[at, here] = ua
            xb_ref[at, here] = xb
            s = dot(writes[:, b * BLOCK : (b + 1) * BLOCK], xb) * wide_ref[2 + b : 3 + b, here]
            a = dot(reads[:, b * BLOCK : (b + 1) * BLOCK], ua) * wide_ref[b : b + 1, here]
            state = s if state is None else state + s
            adjoint = a if adjoint is None else adjoint + a
        state = state.astype(BF16)
        adjoint = adjoint.astype(BF16)
        up_ref[here, :] = jnp.where(place == last, adjoint, state)
        down_ref[here, :] = jnp.where(place == 0, state, adjoint)
    total = jnp.concatenate(
        [wide_ref[5:6, pl.ds(lo, BLOCK)] for lo in range(0, cols, BLOCK)], axis=0
    )
    totals = jnp.concatenate([p.astype(F32) for p in pieces(total, 2)], axis=0).astype(BF16)
    up_ref[pl.ds(cols, 16), :] = totals
    down_ref[pl.ds(cols, 16), :] = totals


def kernel_within(
    x_ref, g_ref, dy_ref, skip_ref, wo_ref, wt_ref, ro_ref, rt_ref,
    ua_ref, xb_ref, al_ref, be_ref, wide_ref,
    gate_ref, gate_f_ref, in_ref, in_f_ref, dr_ref, dw_ref, p_ref, q_ref, skip_out_ref,
    al_e, be_e, skip_e,
):
    rows, cols = x_ref.shape
    heads = skip_ref.shape[1]
    for lo in range(0, cols, TILE):
        wide = expander(heads, lo, TILE)
        here = pl.ds(lo, TILE)
        al_e[:, here] = split_dot_right(al_ref[...], wide, 2)
        be_e[:, here] = split_dot_right(be_ref[...], wide, 2)
        skip_e[:, here] = split_dot_right(jnp.broadcast_to(skip_ref[...], (8, heads)), wide, 3)
    writes = both(wo_ref, wt_ref)
    reads = both(ro_ref, rt_ref)
    w = [writes[:BLOCK], writes[BLOCK:]]
    r = [reads[:BLOCK], reads[BLOCK:]]
    i = lax.broadcasted_iota(jnp.int32, (BLOCK, BLOCK), 0)
    j = lax.broadcasted_iota(jnp.int32, (BLOCK, BLOCK), 1)
    nt = ((1,), (1,))
    i00 = jnp.where(i >= j, dot(r[0], w[0], nt), 0.0)
    i11 = jnp.where(i >= j, dot(r[1], w[1], nt), 0.0)
    i10 = dot(r[1], w[0], nt)
    t00, t11, t10 = i00.T.astype(BF16), i11.T.astype(BF16), i10.T.astype(BF16)
    i00, i11, i10 = i00.astype(BF16), i11.astype(BF16), i10.astype(BF16)
    m00 = jnp.zeros((BLOCK, BLOCK), F32)
    m11 = m00
    m10 = m00
    first = pl.ds(0, BLOCK)
    second = pl.ds(BLOCK, BLOCK)
    p = [jnp.zeros((BLOCK, heads), F32)] * 2
    q = [jnp.zeros((BLOCK, heads), F32)] * 2
    skips = jnp.zeros((8, heads), F32)
    for lo in range(0, cols, BLOCK):
        here = pl.ds(lo, BLOCK)
        sel = selector(heads, lo, BLOCK)
        link = wide_ref[4:5, here]
        ua = [ua_ref[first, here], ua_ref[second, here]]
        xb = [xb_ref[first, here], xb_ref[second, here]]
        m00 += dot(ua[0], xb[0], nt)
        m11 += dot(ua[1], xb[1], nt)
        m10 += dot(ua[1], (xb[0].astype(F32) * link).astype(BF16), nt)
        v = [dot(i00, xb[0]), dot(i11, xb[1]) + link * dot(i10, xb[0])]
        z = [dot(t00, ua[0]) + link * dot(t10, ua[1]), dot(t11, ua[1])]
        skip = skip_e[0:1, here]
        for b in range(2):
            at = pl.ds(b * BLOCK, BLOCK)
            p[b] += split_dot_right(ua[b].astype(F32) * v[b], sel, 2)
            q[b] += split_dot_right(xb[b].astype(F32) * z[b], sel, 2)
            g = g_ref[at, here].astype(F32)
            dy = dy_ref[at, here].astype(F32)
            x = x_ref[at, here].astype(F32)
            sig = 1.0 / (1.0 + jnp.exp(-g))
            u = dy * g * sig
            up = dy * sig * (1.0 + g * (1.0 - sig))
            al = al_e[at, here]
            be = be_e[at, here]
            gate_ref[at, here] = (up * (al * v[b] + skip * x)).astype(BF16)
            gate_f_ref[at, here] = (up * al * wide_ref[b : b + 1, here]).astype(BF16)
            in_ref[at, here] = (be * z[b] + skip * u).astype(BF16)
            in_f_ref[at, here] = (be * wide_ref[2 + b : 3 + b, here]).astype(BF16)
            ux = jnp.sum((u * x).reshape(BLOCK // 8, 8, BLOCK), axis=0)
            skips += split_dot_right(ux, sel, 3)
    for b in range(2):
        p_ref[pl.ds(b * BLOCK, BLOCK), :] = p[b]
        q_ref[pl.ds(b * BLOCK, BLOCK), :] = q[b]
    skip_out_ref[...] = skips
    m00 = jnp.where(i >= j, m00, 0.0)
    m11 = jnp.where(i >= j, m11, 0.0)
    n00, n11, n10 = m00.T.astype(BF16), m11.T.astype(BF16), m10.T.astype(BF16)
    m00, m11, m10 = m00.astype(BF16), m11.astype(BF16), m10.astype(BF16)
    dr_ref[first, :] = dot(m00, w[0])
    dr_ref[second, :] = dot(m10, w[0]) + dot(m11, w[1])
    dw_ref[first, :] = dot(n00, r[0]) + dot(n10, r[1])
    dw_ref[second, :] = dot(n11, r[1])


def kernel_steps(
    a_ref, b_ref, c_ref, d_ref, wo_ref, wt_ref, ro_ref, rt_ref, ua_ref, xb_ref, p_ref, q_ref,
    small_ref, raw_ref, bias_ref, rate_ref, skips_ref,
    state_ref, adjoint_ref, step_ref, sums_ref,
):
    rows, cols = ua_ref.shape
    heads = raw_ref.shape[1]
    place = lax.axis_index("context")
    last = lax.axis_size("context") - 1
    writes = both(wo_ref, wt_ref)
    reads = both(ro_ref, rt_ref)
    p = jnp.zeros((rows, heads), F32)
    q = jnp.zeros((rows, heads), F32)
    cross = jnp.zeros((8, heads), F32)

    def total(ref, k):
        hi = ref[pl.ds(cols, 8), :].astype(F32)[k : k + 1]
        lo = ref[pl.ds(cols + 8, 8), :].astype(F32)[k : k + 1]
        return hi + lo

    def masked(keep, v):
        return jnp.where(keep, v, 0.0)

    for k in range(cols // BLOCK):
        here = pl.ds(k * BLOCK, BLOCK)
        ta, tb, tc, td = (total(ref, k) for ref in (a_ref, b_ref, c_ref, d_ref))
        got_a, got_b, got_c, got_d = (
            ref[here, :].astype(F32) for ref in (a_ref, b_ref, c_ref, d_ref)
        )
        state = (
            masked(place >= 1, 1.0) * got_a
            + masked(place >= 2, ta) * got_c
            + masked(place >= 3, ta * tc) * got_b
        )
        adjoint = (
            masked(place <= last - 1, 1.0) * got_b
            + masked(place <= last - 2, tb) * got_d
            + masked(place <= last - 3, tb * td) * got_a
        )
        sel = selector(heads, k * BLOCK, BLOCK)
        both_sum = jnp.sum((state * adjoint).reshape(STATE // 8, 8, BLOCK), axis=0)
        cross += split_dot_right(both_sum, sel, 2)
        state = state.astype(BF16)
        adjoint = adjoint.astype(BF16)
        state_ref[:, here] = state
        adjoint_ref[:, here] = adjoint
        p += split_dot_right(ua_ref[:, here].astype(F32) * dot(reads, state), sel, 2)
        q += split_dot_right(xb_ref[:, here].astype(F32) * dot(writes, adjoint), sel, 2)
    row = lax.broadcasted_iota(jnp.int32, (rows, heads), 0)
    p = p * jnp.where(row < BLOCK, small_ref[0:1], small_ref[1:2])
    q = q * jnp.where(row < BLOCK, small_ref[2:3], small_ref[3:4])
    ends = jnp.sum(q, axis=0, keepdims=True) + small_ref[5:6] * jnp.sum(
        cross, axis=0, keepdims=True
    )
    q = q + q_ref[...]
    flow = split_dot_left(triangle(rows, False), p + p_ref[...] - q, 3) + ends
    z = raw_ref[...] + bias_ref[...]
    step = softplus(z)
    rate = jnp.exp(rate_ref[...])
    grad = (q / step - rate * flow) / (1.0 + jnp.exp(-z))
    step_ref[...] = grad
    sum_rate = jnp.sum(flow * step, axis=0, keepdims=True) * -rate
    sum_bias = jnp.sum(grad, axis=0, keepdims=True)
    sum_skip = jnp.sum(skips_ref[...], axis=0, keepdims=True)
    index = lax.broadcasted_iota(jnp.int32, (8, heads), 0)
    sums_ref[...] = jnp.where(
        index == 0, sum_rate, jnp.where(index == 1, sum_skip, jnp.where(index == 2, sum_bias, 0.0))
    )


def kernel_last(
    state_ref, adjoint_ref, wo_ref, wt_ref, ro_ref, rt_ref, ua_ref, xb_ref, wide_ref,
    gate_ref, gate_f_ref, in_ref, in_f_ref, dr_ref, dw_ref,
    grad_in_ref, grad_gate_ref, keep_w_ref, keep_r_ref, send_ref,
):
    rows, cols = ua_ref.shape
    half = wo_ref.shape[1]
    nt = ((1,), (1,))
    writes = both(wo_ref, wt_ref)
    reads = both(ro_ref, rt_ref)
    for b in range(2):
        at = pl.ds(b * BLOCK, BLOCK)
        dr = dr_ref[at, :]
        dw = dw_ref[at, :]
        for lo in range(0, cols, BLOCK):
            here = pl.ds(lo, BLOCK)
            s = state_ref[:, here]
            a = adjoint_ref[:, here]
            scaled_s = (s.astype(F32) * wide_ref[b : b + 1, here]).astype(BF16)
            scaled_a = (a.astype(F32) * wide_ref[2 + b : 3 + b, here]).astype(BF16)
            dr += dot(ua_ref[at, here], scaled_s, nt)
            dw += dot(xb_ref[at, here], scaled_a, nt)
            v = dot(reads[b * BLOCK : (b + 1) * BLOCK], s)
            z = dot(writes[b * BLOCK : (b + 1) * BLOCK], a)
            grad_gate_ref[at, here] = (
                gate_ref[at, here].astype(F32) + gate_f_ref[at, here].astype(F32) * v
            ).astype(BF16)
            grad_in_ref[at, here] = (
                in_ref[at, here].astype(F32) + in_f_ref[at, here].astype(F32) * z
            ).astype(BF16)
        keep_w_ref[at, :] = dw[:, :half]
        keep_r_ref[at, :] = dr[:, :half]
        send_ref[at, :] = jnp.concatenate([dw[:, half:], dr[:, half:]], axis=1).astype(BF16)


def call(kernel, outs, args, scratch=(), us=3.0):
    shapes = [jax.ShapeDtypeStruct(s, d) for s, d in outs]
    return pl.pallas_call(
        kernel,
        out_shape=shapes,
        in_specs=[pl.BlockSpec(memory_space=pltpu.VMEM)] * len(args),
        out_specs=[pl.BlockSpec(memory_space=pltpu.VMEM)] * len(outs),
        scratch_shapes=list(scratch),
        compiler_params=pltpu.CompilerParams(vmem_limit_bytes=40 * 1024 * 1024),
        cost_estimate=pl.CostEstimate(
            flops=int(us * 1e9), bytes_accessed=int(us * 1e6), transcendentals=0
        ),
    )(*args)


def cycle(array, axis, by):
    count = lax.axis_size(axis)
    return lax.ppermute(array, axis, [(i, (i + by) % count) for i in range(count)])


def swap(array):
    count = lax.axis_size("tensor")
    return lax.ppermute(array, "tensor", [(i, i ^ 1) for i in range(count)])


def all_sum(array, axis):
    count = lax.axis_size(axis)
    return sum([cycle(array, axis, by) for by in range(1, count)], array)


def body(
    head_inputs,
    gate_inputs,
    step_raw,
    state_write,
    state_read,
    log_rate,
    skip_gain,
    step_bias,
    grad_gated,
):
    x, g, dy = head_inputs[0], gate_inputs[0], grad_gated[0]
    raw = step_raw[0]
    rows, cols = x.shape
    heads = raw.shape[1]
    half = state_write.shape[2]
    wo, ro = state_write[0], state_read[0]
    wt, rt = swap(wo), swap(ro)
    rate, skip, bias = (v.reshape(1, heads) for v in (log_rate, skip_gain, step_bias))
    keys = [wo, wt, ro, rt]
    payload = ((cols + 16, STATE), BF16)
    big = ((rows, cols), BF16)
    thin = ((rows, heads), F32)
    up, down, ua, xb, al, be, wide, small = call(
        kernel_local,
        [payload, payload, big, big, thin, thin, ((8, cols), F32), ((8, heads), F32)],
        [x, g, dy, raw, bias, rate] + keys,
        [pltpu.VMEM((rows, cols), F32)] * 2,
    )
    got_a = cycle(up, "context", 1)
    got_b = cycle(down, "context", -1)
    got_c = cycle(got_a, "context", 1)
    got_d = cycle(got_b, "context", -1)
    gate, gate_f, inp, inp_f, dr, dw, p, q, skips = call(
        kernel_within,
        [big] * 4 + [((rows, STATE), F32)] * 2 + [thin] * 2 + [((8, heads), F32)],
        [x, g, dy, skip] + keys + [ua, xb, al, be, wide],
        [pltpu.VMEM((rows, cols), F32)] * 2 + [pltpu.VMEM((8, cols), F32)],
        us=6.0,
    )
    state, adjoint, grad_step, sums = call(
        kernel_steps,
        [((STATE, cols), BF16)] * 2 + [thin, ((8, heads), F32)],
        [got_a, got_b, got_c, got_d] + keys
        + [ua, xb, p, q, small, raw, bias, rate, skips],
    )
    sums = all_sum(all_sum(sums, "context"), "dp")
    grad_in, grad_gate, keep_w, keep_r, send = call(
        kernel_last,
        [big, big, ((rows, half), F32), ((rows, half), F32), ((rows, 2 * half), BF16)],
        [state, adjoint] + keys + [ua, xb, wide, gate, gate_f, inp, inp_f, dr, dw],
    )
    got = swap(send).astype(F32)
    return (
        grad_in[None],
        grad_gate[None],
        (keep_w + got[:, :half])[None],
        (keep_r + got[:, half:])[None],
        grad_step[None],
        sums[0],
        sums[1],
        sums[2],
    )


def solution(mesh):
    wide = P("dp", "context", "tensor")
    head = P("tensor")
    return jax.shard_map(
        body,
        mesh=mesh,
        in_specs=(wide,) * 5 + (head,) * 3 + (wide,),
        out_specs=(wide,) * 5 + (head,) * 3,
        check_vma=False,
    )
```

```python
import functools
import math

import jax
import jax.numpy as jnp
from jax import lax
from jax.experimental import pallas as pl
from jax.experimental.pallas import tpu as pltpu
from jax.sharding import PartitionSpec as P

HEAD_DIM = 64
STATE = 128
BLOCK = 128
LOG2E = math.log2(math.e)
F32 = jnp.float32
BF16 = jnp.bfloat16
TILE = 256


def dot(a, b, dims=((1,), (0,))):
    return lax.dot_general(a, b, (dims, ((), ())), preferred_element_type=F32)


def pieces(v, count):
    out = []
    for _ in range(count):
        part = v.astype(BF16)
        out.append(part)
        v = v - part.astype(F32)
    return out


def split_dot_left(exact, v, count):
    return sum(dot(exact, part) for part in pieces(v, count))


def split_dot_right(v, exact, count):
    return sum(dot(part, exact) for part in pieces(v, count))


def expander(heads, lo, size):
    head = lax.broadcasted_iota(jnp.int32, (heads, size), 0)
    column = lax.broadcasted_iota(jnp.int32, (heads, size), 1) + lo
    return ((column >= head * HEAD_DIM) & (column < (head + 1) * HEAD_DIM)).astype(BF16)


def selector(heads, lo, size):
    head = lax.broadcasted_iota(jnp.int32, (size, heads), 1)
    column = lax.broadcasted_iota(jnp.int32, (size, heads), 0) + lo
    return ((column >= head * HEAD_DIM) & (column < (head + 1) * HEAD_DIM)).astype(BF16)


def triangle(rows, lower):
    i = lax.broadcasted_iota(jnp.int32, (rows, rows), 0)
    j = lax.broadcasted_iota(jnp.int32, (rows, rows), 1)
    return ((i >= j) if lower else (i <= j)).astype(BF16)


def softplus(z):
    return jnp.maximum(z, 0.0) + jnp.log(1.0 + jnp.exp(-jnp.abs(z)))


def at_block(b):
    return pl.ds(b * BLOCK, BLOCK)


def kernel_scale(
    x_in, g_in, dy_in, raw_in, bias_in, rate_in, skip_in, w_in, r_in,
    x_ref, g_ref, dy_ref, w_ref, r_ref, skip_ref, qq_ref, z_ref, rate_ref, al_ref, be_ref,
    wide_ref, small_ref,
    raw_ref, bias_ref, al_e, be_e, sems,
):
    rows, cols = x_ref.shape
    heads = raw_ref.shape[0]
    blocks = rows // BLOCK
    thin = [
        (raw_in, raw_ref), (bias_in, bias_ref), (rate_in, rate_ref),
        (skip_in, skip_ref), (w_in, w_ref), (r_in, r_ref),
    ]
    copies = [pltpu.make_async_copy(s, d, sems.at[i]) for i, (s, d) in enumerate(thin)]
    large = []
    for b in range(blocks):
        large.append([
            pltpu.make_async_copy(s.at[at_block(b)], d.at[at_block(b)], sems.at[6 + 3 * b + i])
            for i, (s, d) in enumerate([(g_in, g_ref), (dy_in, dy_ref), (x_in, x_ref)])
        ])
    for copy in copies[:3] + large[0] + large[1] + copies[3:]:
        copy.start()
    for copy in copies[:3]:
        copy.wait()
    z = raw_ref[...].T + bias_ref[...]
    z_ref[...] = z
    step = softplus(z)
    log2_decay = step * (-LOG2E * jnp.exp(rate_ref[...]))
    run = split_dot_left(triangle(rows, True), log2_decay, 3)
    mid0 = run[BLOCK // 2 - 1 : BLOCK // 2]
    mid1 = run[BLOCK + BLOCK // 2 - 1 : BLOCK + BLOCK // 2]
    end = run[rows - 1 : rows]
    row = lax.broadcasted_iota(jnp.int32, (rows, heads), 0)
    rel = run - jnp.where(row < BLOCK, mid0, mid1)
    al = jnp.exp2(rel)
    be = jnp.exp2(-rel) * step
    al_ref[...] = al
    be_ref[...] = be
    small = jnp.exp2(
        jnp.concatenate([mid0, mid1, end - mid0, end - mid1, mid1 - mid0, end, end, end], axis=0)
    )
    small_ref[...] = small
    for lo in range(0, cols, TILE):
        wide = expander(heads, lo, TILE)
        here = pl.ds(lo, TILE)
        al_e[:, here] = split_dot_right(al, wide, 2)
        be_e[:, here] = split_dot_right(be, wide, 2)
        wide_ref[:, here] = split_dot_right(small, wide, 3)
    for b in range(blocks):
        for copy in large[b]:
            copy.wait()
        at = at_block(b)
        for lo in range(0, cols, BLOCK):
            here = pl.ds(lo, BLOCK)
            g = g_ref[at, here].astype(F32)
            u = dy_ref[at, here].astype(F32) * g / (1.0 + jnp.exp(-g))
            qq_ref[1, at, here] = (u * al_e[at, here]).astype(BF16)
            qq_ref[0, at, here] = (x_ref[at, here].astype(F32) * be_e[at, here]).astype(BF16)
    for copy in copies[3:]:
        copy.wait()


def kernel_states(
    w_ref, wt_ref, r_ref, rt_ref, qq_ref, wide_ref, small_ref, turned_ref, e_ref, f_ref
):
    cols = qq_ref.shape[2]
    blocks = qq_ref.shape[1] // BLOCK
    place = lax.axis_index("context")
    writes = jnp.concatenate([w_ref[...], wt_ref[...]], axis=0)
    reads = jnp.concatenate([r_ref[...], rt_ref[...]], axis=0)
    turned_ref[0] = writes
    turned_ref[1] = reads
    for lo in range(0, cols, BLOCK):
        here = pl.ds(lo, BLOCK)
        state = jnp.zeros((STATE, BLOCK), F32)
        adjoint = state
        for b in range(blocks):
            at = at_block(b)
            part = slice(b * BLOCK, (b + 1) * BLOCK)
            state += dot(writes[:, part], qq_ref[0, at, here]) * wide_ref[2 + b : 3 + b, here]
            adjoint += dot(reads[:, part], qq_ref[1, at, here]) * wide_ref[b : b + 1, here]
        e_ref[here, :] = jnp.where(place < 2, state, adjoint).astype(BF16)
        f_ref[here, :] = jnp.where(lax.rem(place, 2) == 0, state, adjoint).astype(BF16)
    heads = small_ref.shape[1]
    total = jnp.concatenate(
        [small_ref[5:6], jnp.zeros((1, STATE - heads), F32)], axis=1
    )
    parts = [part.astype(F32) for part in pieces(total, 3)]
    totals = jnp.concatenate(parts + [jnp.zeros((13, STATE), F32)], axis=0).astype(BF16)
    e_ref[pl.ds(cols, 16), :] = totals
    f_ref[pl.ds(cols, 16), :] = totals


def kernel_within(
    x_ref, g_ref, dy_ref, skip_ref, turned_ref, qq_ref, al_ref, be_ref, wide_ref,
    gate_ref, gate_f_ref, in_ref, in_f_ref, dr_ref, dw_ref, keys_ref, p_ref, q_ref, skip_out_ref,
    al_e, be_e, skip_e,
):
    rows, cols = x_ref.shape
    heads = skip_ref.shape[1]
    for lo in range(0, cols, TILE):
        wide = expander(heads, lo, TILE)
        here = pl.ds(lo, TILE)
        al_e[:, here] = split_dot_right(al_ref[...], wide, 2)
        be_e[:, here] = split_dot_right(be_ref[...], wide, 2)
        skip_e[:, here] = split_dot_right(jnp.broadcast_to(skip_ref[...], (8, heads)), wide, 3)
    nt = ((1,), (1,))
    wt = [turned_ref[0, :, at_block(b)] for b in range(2)]
    rt = [turned_ref[1, :, at_block(b)] for b in range(2)]
    w = [v.astype(F32).T.astype(BF16) for v in wt]
    r = [v.astype(F32).T.astype(BF16) for v in rt]
    for b in range(2):
        keys_ref[0, at_block(b), :] = w[b]
        keys_ref[1, at_block(b), :] = r[b]
    i = lax.broadcasted_iota(jnp.int32, (BLOCK, BLOCK), 0)
    j = lax.broadcasted_iota(jnp.int32, (BLOCK, BLOCK), 1)
    i00 = jnp.where(i >= j, dot(r[0], wt[0]), 0.0).astype(BF16)
    i11 = jnp.where(i >= j, dot(r[1], wt[1]), 0.0).astype(BF16)
    i10 = dot(r[1], wt[0]).astype(BF16)
    t00 = jnp.where(i <= j, dot(w[0], rt[0]), 0.0).astype(BF16)
    t11 = jnp.where(i <= j, dot(w[1], rt[1]), 0.0).astype(BF16)
    t10 = dot(w[0], rt[1]).astype(BF16)
    m00 = jnp.zeros((BLOCK, BLOCK), F32)
    m11 = m00
    m10 = m00
    p = [jnp.zeros((BLOCK, heads), F32)] * 2
    q = [jnp.zeros((BLOCK, heads), F32)] * 2
    skips = jnp.zeros((8, heads), F32)
    for lo in range(0, cols, BLOCK):
        here = pl.ds(lo, BLOCK)
        sel = selector(heads, lo, BLOCK)
        link = wide_ref[4:5, here]
        xb = [qq_ref[0, at_block(b), here] for b in range(2)]
        ua = [qq_ref[1, at_block(b), here] for b in range(2)]
        m00 += dot(ua[0], xb[0], nt)
        m11 += dot(ua[1], xb[1], nt)
        m10 += dot(ua[1], (xb[0].astype(F32) * link).astype(BF16), nt)
        v = [dot(i00, xb[0]), dot(i11, xb[1]) + link * dot(i10, xb[0])]
        z = [dot(t00, ua[0]) + link * dot(t10, ua[1]), dot(t11, ua[1])]
        skip = skip_e[0:1, here]
        for b in range(2):
            at = at_block(b)
            p[b] += split_dot_right(ua[b].astype(F32) * v[b], sel, 2)
            q[b] += split_dot_right(xb[b].astype(F32) * z[b], sel, 2)
            g = g_ref[at, here].astype(F32)
            dy = dy_ref[at, here].astype(F32)
            x = x_ref[at, here].astype(F32)
            sig = 1.0 / (1.0 + jnp.exp(-g))
            u = dy * g * sig
            up = dy * sig * (1.0 + g * (1.0 - sig))
            al = al_e[at, here]
            be = be_e[at, here]
            gate_ref[at, here] = (up * (al * v[b] + skip * x)).astype(BF16)
            gate_f_ref[at, here] = (up * al * wide_ref[b : b + 1, here]).astype(BF16)
            in_ref[at, here] = (be * z[b] + skip * u).astype(BF16)
            in_f_ref[at, here] = (be * wide_ref[2 + b : 3 + b, here]).astype(BF16)
            ux = jnp.sum((u * x).reshape(BLOCK // 8, 8, BLOCK), axis=0)
            skips += split_dot_right(ux, sel, 3)
    for b in range(2):
        p_ref[at_block(b), :] = p[b]
        q_ref[at_block(b), :] = q[b]
    skip_out_ref[...] = skips
    m00 = jnp.where(i >= j, m00, 0.0).astype(BF16)
    m11 = jnp.where(i >= j, m11, 0.0).astype(BF16)
    m10 = m10.astype(BF16)
    dr_ref[:, at_block(0)] = dot(wt[0], m00, nt)
    dr_ref[:, at_block(1)] = dot(wt[0], m10, nt) + dot(wt[1], m11, nt)
    dw_ref[:, at_block(0)] = dot(rt[0], m00) + dot(rt[1], m10)
    dw_ref[:, at_block(1)] = dot(rt[1], m11)


def kernel_after(first_ref, token_ref, out_ref):
    del first_ref, token_ref, out_ref


def head_sums(buffer_ref, key, weight_ref, index, heads):
    cols = weight_ref.shape[2]
    out = jnp.zeros((key.shape[0], heads), F32)
    for lo in range(0, cols, BLOCK):
        here = pl.ds(lo, BLOCK)
        product = weight_ref[index, :, here].astype(F32) * dot(key, buffer_ref[here, :])
        out += split_dot_right(product, selector(heads, lo, BLOCK), 2)
    return out


def pair_sums(one_ref, two_ref, cols, heads):
    out = jnp.zeros((8, heads), F32)
    for lo in range(0, cols, BLOCK):
        here = pl.ds(lo, BLOCK)
        product = one_ref[here, :].astype(F32) * two_ref[here, :].astype(F32)
        product = jnp.sum(product.reshape(STATE // 8, 8, BLOCK), axis=0)
        out += split_dot_right(product, selector(heads, lo, BLOCK), 2)
    return out


def kernel_early(e_ref, f_ref, keys_ref, qq_ref, small_ref, pe_ref, pf_ref, cross_ref):
    cols = qq_ref.shape[2]
    heads = small_ref.shape[1]
    place = lax.axis_index("context")
    mine = (place >= 2).astype(jnp.int32)
    side = lax.rem(place, 2)
    pe_ref[...] = head_sums(e_ref, keys_ref[mine], qq_ref, mine, heads)
    pf_ref[...] = head_sums(f_ref, keys_ref[side], qq_ref, side, heads)
    cross_ref[...] = pair_sums(e_ref, f_ref, cols, heads)


def total_of(ref, cols, heads):
    parts = ref[pl.ds(cols, 16), :].astype(F32)
    return (parts[0:1] + parts[1:2] + parts[2:3])[:, :heads]


def kernel_steps(
    h_ref, e_ref, f_ref, keys_ref, qq_ref, pe_ref, pf_ref, cross_ref, p_ref, q_ref,
    small_ref, z_ref, rate_ref, skips_ref,
    step_ref, sums_ref,
):
    rows, cols = qq_ref.shape[1:]
    heads = small_ref.shape[1]
    place = lax.axis_index("context")
    mine = (place >= 2).astype(jnp.int32)
    inner = (place == 1) | (place == 2)
    te, tf, th = (total_of(ref, cols, heads) for ref in (e_ref, f_ref, h_ref))
    ph = head_sums(h_ref, keys_ref[mine], qq_ref, mine, heads)
    cross = cross_ref[...] + te * pair_sums(h_ref, f_ref, cols, heads)
    cross = jnp.where(inner, jnp.sum(cross, axis=0, keepdims=True), 0.0)
    pe = pe_ref[...]
    pf = pf_ref[...]
    px = jnp.where(inner, pe + te * ph, pf + tf * (ph + th * pe))
    py = jnp.where(inner, pf, 0.0)
    row = lax.broadcasted_iota(jnp.int32, (rows, heads), 0)
    p = jnp.where(mine == 1, px, py) * jnp.where(row < BLOCK, small_ref[0:1], small_ref[1:2])
    q = jnp.where(mine == 1, py, px) * jnp.where(row < BLOCK, small_ref[2:3], small_ref[3:4])
    ends = jnp.sum(q, axis=0, keepdims=True) + small_ref[5:6] * cross
    q = q + q_ref[...]
    flow = split_dot_left(triangle(rows, False), p + p_ref[...] - q, 3) + ends
    z = z_ref[...]
    step = softplus(z)
    rate = jnp.exp(rate_ref[...])
    grad = (q / step - rate * flow) / (1.0 + jnp.exp(-z))
    step_ref[...] = grad.T
    sum_rate = jnp.sum(flow * step, axis=0, keepdims=True) * -rate
    sum_bias = jnp.sum(grad, axis=0, keepdims=True)
    sum_skip = jnp.sum(skips_ref[...], axis=0, keepdims=True)
    index = lax.broadcasted_iota(jnp.int32, (8, heads), 0)
    sums_ref[...] = jnp.where(
        index == 0, sum_rate, jnp.where(index == 1, sum_skip, jnp.where(index == 2, sum_bias, 0.0))
    )


def kernel_last(
    e_ref, f_ref, h_ref, keys_ref, qq_ref, wide_ref,
    gate_ref, gate_f_ref, in_ref, in_f_ref, dr_ref, dw_ref, after_ref,
    grad_in_ref, grad_gate_ref, keep_ref, send_ref,
    coef_e,
):
    del after_ref
    rows, cols = qq_ref.shape[1:]
    half = STATE // 2
    heads = cols // HEAD_DIM
    nt = ((1,), (1,))
    place = lax.axis_index("context")
    inner = (place == 1) | (place == 2)
    te, tf, th = (total_of(ref, cols, heads) for ref in (e_ref, f_ref, h_ref))
    coef = jnp.concatenate(
        [jnp.where(inner, 1.0, tf * th), jnp.where(inner, te, tf)] + [jnp.zeros_like(te)] * 6,
        axis=0,
    )
    for lo in range(0, cols, TILE):
        coef_e[:, pl.ds(lo, TILE)] = split_dot_right(coef, expander(heads, lo, TILE), 3)
    dr = [dr_ref[:, at_block(b)] for b in range(2)]
    dw = [dw_ref[:, at_block(b)] for b in range(2)]
    for lo in range(0, cols, BLOCK):
        here = pl.ds(lo, BLOCK)
        got_f = f_ref[here, :].astype(F32)
        x = (
            e_ref[here, :].astype(F32) * coef_e[0:1, here]
            + h_ref[here, :].astype(F32) * coef_e[1:2, here]
            + jnp.where(inner, 0.0, got_f)
        )
        y = jnp.where(inner, got_f, 0.0)
        s = jnp.where(place >= 2, x, y)
        a = jnp.where(place >= 2, y, x)
        s_half = s.astype(BF16)
        a_half = a.astype(BF16)
        for b in range(2):
            at = at_block(b)
            scaled_s = (s * wide_ref[b : b + 1, here]).astype(BF16)
            scaled_a = (a * wide_ref[2 + b : 3 + b, here]).astype(BF16)
            dr[b] += dot(scaled_s, qq_ref[1, at, here], nt)
            dw[b] += dot(scaled_a, qq_ref[0, at, here], nt)
            v = dot(keys_ref[1, at, :], s_half)
            z = dot(keys_ref[0, at, :], a_half)
            grad_gate_ref[at, here] = (
                gate_ref[at, here].astype(F32) + gate_f_ref[at, here].astype(F32) * v
            ).astype(BF16)
            grad_in_ref[at, here] = (
                in_ref[at, here].astype(F32) + in_f_ref[at, here].astype(F32) * z
            ).astype(BF16)
    for b in range(2):
        keep_ref[pl.ds(0, half), at_block(b)] = dw[b][:half]
        keep_ref[pl.ds(half, half), at_block(b)] = dr[b][:half]
        send_ref[pl.ds(0, half), at_block(b)] = dw[b][half:].astype(BF16)
        send_ref[pl.ds(half, half), at_block(b)] = dr[b][half:].astype(BF16)


def kernel_add(a_ref, b_ref, c_ref, d_ref, after_ref, out_ref):
    del after_ref
    out_ref[...] = (a_ref[...] + b_ref[...]) + (c_ref[...] + d_ref[...])


def kernel_finish(
    keep_ref, got_ref, a_ref, b_ref, c_ref, d_ref, w_ref, r_ref, rate_ref, skip_ref, bias_ref
):
    half = w_ref.shape[0]
    w_ref[...] = keep_ref[pl.ds(0, half), :] + got_ref[pl.ds(0, half), :].astype(F32)
    r_ref[...] = keep_ref[pl.ds(half, half), :] + got_ref[pl.ds(half, half), :].astype(F32)
    sums = (a_ref[...] + b_ref[...]) + (c_ref[...] + d_ref[...])
    rate_ref[...] = sums[0:1]
    skip_ref[...] = sums[1:2]
    bias_ref[...] = sums[2:3]


V = pltpu.VMEM
ANY = pl.ANY


def call(kernel, outs, args, scratch=(), us=3.0, spaces=None, out_spaces=None, alias=None):
    spaces = spaces or [V] * len(args)
    out_spaces = out_spaces or [V] * len(outs)
    return pl.pallas_call(
        kernel,
        out_shape=[jax.ShapeDtypeStruct(s, d) for s, d in outs],
        in_specs=[pl.BlockSpec(memory_space=s) for s in spaces],
        out_specs=[pl.BlockSpec(memory_space=s) for s in out_spaces],
        scratch_shapes=list(scratch),
        input_output_aliases=alias or {},
        compiler_params=pltpu.CompilerParams(vmem_limit_bytes=36 * 1024 * 1024),
        cost_estimate=pl.CostEstimate(
            flops=int(us * 1e9), bytes_accessed=int(us * 1e6), transcendentals=0
        ),
    )(*args)


def exchange(array, axis, mask):
    count = lax.axis_size(axis)
    pairs = [(i, i ^ mask) for i in range(count) if i ^ mask < count]
    return lax.ppermute(array, axis, pairs)


def body(
    head_inputs,
    gate_inputs,
    step_raw,
    state_write,
    state_read,
    log_rate,
    skip_gain,
    step_bias,
    grad_gated,
):
    x, g, dy = head_inputs[0], gate_inputs[0], grad_gated[0]
    raw = step_raw[0].T
    heads, rows = raw.shape
    cols = x.shape[1]
    half = state_write.shape[2]
    w, r = state_write[0].T, state_read[0].T
    wt, rt = exchange(w, "tensor", 1), exchange(r, "tensor", 1)
    rate, skip, bias = (v.reshape(1, heads) for v in (log_rate, skip_gain, step_bias))
    payload = ((cols + 16, STATE), BF16)
    big = ((rows, cols), BF16)
    pair = ((2, rows, cols), BF16)
    thin = ((rows, heads), F32)
    tiny = ((8, heads), F32)
    one = ((1, heads), F32)
    key = ((half, rows), BF16)
    x, g, dy, w, r, skip, qq, z, rate, al, be, wide, small = call(
        kernel_scale,
        [big, big, big, key, key, one, pair, thin, one, thin, thin, ((8, cols), F32), tiny],
        [
            pltpu.with_memory_space_constraint(v, pltpu.HBM)
            for v in (x, g, dy, raw, bias, rate, skip, w, r)
        ],
        [V((heads, rows), F32), V((1, heads), F32), V((rows, cols), F32), V((rows, cols), F32),
         pltpu.SemaphoreType.DMA((12,))],
        spaces=[pltpu.HBM] * 9,
    )
    turned, send_e, send_f = call(
        kernel_states,
        [((2, STATE, rows), BF16), payload, payload],
        [w, wt, r, rt, qq, wide, small],
    )
    got_e = exchange(send_e, "context", 3)
    got_f = exchange(send_f, "context", 1)
    gate, gate_f, inp, inp_f, dr, dw, keys, p, q, skips = call(
        kernel_within,
        [big] * 4 + [((STATE, rows), F32)] * 2 + [((2, rows, STATE), BF16), thin, thin, tiny],
        [x, g, dy, skip, turned, qq, al, be, wide],
        [V((rows, cols), F32)] * 2 + [V((8, cols), F32)],
        us=4.0,
    )
    (got_e,) = call(
        kernel_after, [payload], [got_e, skips],
        spaces=[ANY, ANY], out_spaces=[ANY], alias={0: 0}, us=0.01,
    )
    got_h = exchange(got_e, "context", 1)
    pe, pf, cross = call(
        kernel_early, [thin, thin, tiny], [got_e, got_f, keys, qq, small], us=2.0
    )
    grad_step, sums = call(
        kernel_steps,
        [((heads, rows), F32), tiny],
        [got_h, got_e, got_f, keys, qq, pe, pf, cross, p, q, small, z, rate, skips],
        us=1.0,
    )
    others = [exchange(sums, "context", mask) for mask in (1, 2, 3)]
    grad_in, grad_gate, keep, send = call(
        kernel_last,
        [big, big, ((STATE, rows), F32), ((STATE, rows), BF16)],
        [got_e, got_f, got_h, keys, qq, wide, gate, gate_f, inp, inp_f, dr, dw, sums],
        [V((8, cols), F32)],
        us=2.0,
        spaces=[V] * 12 + [ANY],
    )
    (sums,) = call(kernel_add, [tiny], [sums] + others + [send], spaces=[V] * 4 + [ANY], us=0.1)
    got = exchange(send, "tensor", 1)
    others = [exchange(sums, "dp", mask) for mask in (1, 2, 3)]
    grad_w, grad_r, sum_rate, sum_skip, sum_bias = call(
        kernel_finish,
        [((half, rows), F32)] * 2 + [one] * 3,
        [keep, got, sums] + others,
        us=0.2,
    )
    return (
        grad_in[None],
        grad_gate[None],
        grad_w.T[None],
        grad_r.T[None],
        grad_step.T[None],
        sum_rate.reshape(heads),
        sum_skip.reshape(heads),
        sum_bias.reshape(heads),
    )


def solution(mesh):
    wide = P("dp", "context", "tensor")
    head = P("tensor")
    return jax.shard_map(
        body,
        mesh=mesh,
        in_specs=(wide,) * 5 + (head,) * 3 + (wide,),
        out_specs=(wide,) * 5 + (head,) * 3,
        check_vma=False,
    )
```

```python
import functools
import math

import jax
import jax.numpy as jnp
from jax import lax
from jax.experimental import pallas as pl
from jax.experimental.pallas import tpu as pltpu
from jax.sharding import PartitionSpec as P

HEAD_DIM = 64
STATE = 128
BLOCK = 128
LOG2E = math.log2(math.e)
F32 = jnp.float32
BF16 = jnp.bfloat16
TILE = 256


def dot(a, b, dims=((1,), (0,))):
    return lax.dot_general(a, b, (dims, ((), ())), preferred_element_type=F32)


def pieces(v, count):
    out = []
    for _ in range(count):
        part = v.astype(BF16)
        out.append(part)
        v = v - part.astype(F32)
    return out


def split_dot_left(exact, v, count):
    return sum(dot(exact, part) for part in pieces(v, count))


def split_dot_right(v, exact, count):
    return sum(dot(part, exact) for part in pieces(v, count))


def expander(heads, lo, size):
    head = lax.broadcasted_iota(jnp.int32, (heads, size), 0)
    column = lax.broadcasted_iota(jnp.int32, (heads, size), 1) + lo
    return ((column >= head * HEAD_DIM) & (column < (head + 1) * HEAD_DIM)).astype(BF16)


def selector(heads, lo, size):
    head = lax.broadcasted_iota(jnp.int32, (size, heads), 1)
    column = lax.broadcasted_iota(jnp.int32, (size, heads), 0) + lo
    return ((column >= head * HEAD_DIM) & (column < (head + 1) * HEAD_DIM)).astype(BF16)


def triangle(rows, lower):
    i = lax.broadcasted_iota(jnp.int32, (rows, rows), 0)
    j = lax.broadcasted_iota(jnp.int32, (rows, rows), 1)
    return ((i >= j) if lower else (i <= j)).astype(BF16)


def softplus(z):
    return jnp.maximum(z, 0.0) + jnp.log(1.0 + jnp.exp(-jnp.abs(z)))


def at_block(b):
    return pl.ds(b * BLOCK, BLOCK)


def kernel_scale(
    x_in, g_in, dy_in, raw_in, bias_in, rate_in, skip_in, w_in, r_in,
    x_ref, g_ref, dy_ref, w_ref, r_ref, skip_ref, qq_ref, z_ref, rate_ref, al_ref, be_ref,
    wide_ref, small_ref,
    raw_ref, bias_ref, al_e, be_e, sems,
):
    rows, cols = x_ref.shape
    heads = raw_ref.shape[0]
    blocks = rows // BLOCK
    thin = [
        (raw_in, raw_ref), (bias_in, bias_ref), (rate_in, rate_ref),
        (skip_in, skip_ref), (w_in, w_ref), (r_in, r_ref),
    ]
    copies = [pltpu.make_async_copy(s, d, sems.at[i]) for i, (s, d) in enumerate(thin)]
    large = []
    for b in range(blocks):
        large.append([
            pltpu.make_async_copy(s.at[at_block(b)], d.at[at_block(b)], sems.at[6 + 3 * b + i])
            for i, (s, d) in enumerate([(g_in, g_ref), (dy_in, dy_ref), (x_in, x_ref)])
        ])
    for copy in copies[:3] + large[0] + large[1] + copies[3:]:
        copy.start()
    for copy in copies[:3]:
        copy.wait()
    z = raw_ref[...].T + bias_ref[...]
    z_ref[...] = z
    step = softplus(z)
    log2_decay = step * (-LOG2E * jnp.exp(rate_ref[...]))
    run = split_dot_left(triangle(rows, True), log2_decay, 3)
    mid0 = run[BLOCK // 2 - 1 : BLOCK // 2]
    mid1 = run[BLOCK + BLOCK // 2 - 1 : BLOCK + BLOCK // 2]
    end = run[rows - 1 : rows]
    row = lax.broadcasted_iota(jnp.int32, (rows, heads), 0)
    rel = run - jnp.where(row < BLOCK, mid0, mid1)
    al = jnp.exp2(rel)
    be = jnp.exp2(-rel) * step
    al_ref[...] = al
    be_ref[...] = be
    small = jnp.exp2(
        jnp.concatenate([mid0, mid1, end - mid0, end - mid1, mid1 - mid0, end, end, end], axis=0)
    )
    small_ref[...] = small
    for lo in range(0, cols, TILE):
        wide = expander(heads, lo, TILE)
        here = pl.ds(lo, TILE)
        al_e[:, here] = split_dot_right(al, wide, 2)
        be_e[:, here] = split_dot_right(be, wide, 2)
        wide_ref[:, here] = split_dot_right(small, wide, 3)
    for b in range(blocks):
        for copy in large[b]:
            copy.wait()
        at = at_block(b)
        for lo in range(0, cols, BLOCK):
            here = pl.ds(lo, BLOCK)
            g = g_ref[at, here].astype(F32)
            u = dy_ref[at, here].astype(F32) * g / (1.0 + jnp.exp(-g))
            qq_ref[1, at, here] = (u * al_e[at, here]).astype(BF16)
            qq_ref[0, at, here] = (x_ref[at, here].astype(F32) * be_e[at, here]).astype(BF16)
    for copy in copies[3:]:
        copy.wait()


def kernel_states(
    w_ref, wt_ref, r_ref, rt_ref, qq_ref, wide_ref, small_ref, turned_ref, e_ref, f_ref
):
    cols = qq_ref.shape[2]
    blocks = qq_ref.shape[1] // BLOCK
    place = lax.axis_index("context")
    writes = jnp.concatenate([w_ref[...], wt_ref[...]], axis=0)
    reads = jnp.concatenate([r_ref[...], rt_ref[...]], axis=0)
    turned_ref[0] = writes
    turned_ref[1] = reads
    for lo in range(0, cols, BLOCK):
        here = pl.ds(lo, BLOCK)
        state = jnp.zeros((STATE, BLOCK), F32)
        adjoint = state
        for b in range(blocks):
            at = at_block(b)
            part = slice(b * BLOCK, (b + 1) * BLOCK)
            state += dot(writes[:, part], qq_ref[0, at, here]) * wide_ref[2 + b : 3 + b, here]
            adjoint += dot(reads[:, part], qq_ref[1, at, here]) * wide_ref[b : b + 1, here]
        e_ref[here, :] = jnp.where(place < 2, state, adjoint).astype(BF16)
        f_ref[here, :] = jnp.where(lax.rem(place, 2) == 0, state, adjoint).astype(BF16)
    heads = small_ref.shape[1]
    total = jnp.concatenate(
        [small_ref[5:6], jnp.zeros((1, STATE - heads), F32)], axis=1
    )
    parts = [part.astype(F32) for part in pieces(total, 3)]
    totals = jnp.concatenate(parts + [jnp.zeros((13, STATE), F32)], axis=0).astype(BF16)
    e_ref[pl.ds(cols, 16), :] = totals
    f_ref[pl.ds(cols, 16), :] = totals


def kernel_within(
    x_ref, g_ref, dy_ref, skip_ref, turned_ref, qq_ref, al_ref, be_ref, wide_ref,
    gate_ref, gate_f_ref, in_ref, in_f_ref, dr_ref, dw_ref, keys_ref, p_ref, q_ref, skip_out_ref,
    al_e, be_e, skip_e,
):
    rows, cols = x_ref.shape
    heads = skip_ref.shape[1]
    for lo in range(0, cols, TILE):
        wide = expander(heads, lo, TILE)
        here = pl.ds(lo, TILE)
        al_e[:, here] = split_dot_right(al_ref[...], wide, 2)
        be_e[:, here] = split_dot_right(be_ref[...], wide, 2)
        skip_e[:, here] = split_dot_right(jnp.broadcast_to(skip_ref[...], (8, heads)), wide, 3)
    nt = ((1,), (1,))
    wt = [turned_ref[0, :, at_block(b)] for b in range(2)]
    rt = [turned_ref[1, :, at_block(b)] for b in range(2)]
    w = [v.astype(F32).T.astype(BF16) for v in wt]
    r = [v.astype(F32).T.astype(BF16) for v in rt]
    for b in range(2):
        keys_ref[0, at_block(b), :] = w[b]
        keys_ref[1, at_block(b), :] = r[b]
    i = lax.broadcasted_iota(jnp.int32, (BLOCK, BLOCK), 0)
    j = lax.broadcasted_iota(jnp.int32, (BLOCK, BLOCK), 1)
    i00 = jnp.where(i >= j, dot(r[0], wt[0]), 0.0).astype(BF16)
    i11 = jnp.where(i >= j, dot(r[1], wt[1]), 0.0).astype(BF16)
    i10 = dot(r[1], wt[0]).astype(BF16)
    t00 = jnp.where(i <= j, dot(w[0], rt[0]), 0.0).astype(BF16)
    t11 = jnp.where(i <= j, dot(w[1], rt[1]), 0.0).astype(BF16)
    t10 = dot(w[0], rt[1]).astype(BF16)
    m00 = jnp.zeros((BLOCK, BLOCK), F32)
    m11 = m00
    m10 = m00
    p = [jnp.zeros((BLOCK, heads), F32)] * 2
    q = [jnp.zeros((BLOCK, heads), F32)] * 2
    skips = jnp.zeros((8, heads), F32)
    for lo in range(0, cols, BLOCK):
        here = pl.ds(lo, BLOCK)
        sel = selector(heads, lo, BLOCK)
        link = wide_ref[4:5, here]
        xb = [qq_ref[0, at_block(b), here] for b in range(2)]
        ua = [qq_ref[1, at_block(b), here] for b in range(2)]
        m00 += dot(ua[0], xb[0], nt)
        m11 += dot(ua[1], xb[1], nt)
        m10 += dot(ua[1], (xb[0].astype(F32) * link).astype(BF16), nt)
        v = [dot(i00, xb[0]), dot(i11, xb[1]) + link * dot(i10, xb[0])]
        z = [dot(t00, ua[0]) + link * dot(t10, ua[1]), dot(t11, ua[1])]
        skip = skip_e[0:1, here]
        for b in range(2):
            at = at_block(b)
            p[b] += split_dot_right(ua[b].astype(F32) * v[b], sel, 2)
            q[b] += split_dot_right(xb[b].astype(F32) * z[b], sel, 2)
            g = g_ref[at, here].astype(F32)
            dy = dy_ref[at, here].astype(F32)
            x = x_ref[at, here].astype(F32)
            sig = 1.0 / (1.0 + jnp.exp(-g))
            u = dy * g * sig
            up = dy * sig * (1.0 + g * (1.0 - sig))
            al = al_e[at, here]
            be = be_e[at, here]
            gate_ref[at, here] = (up * (al * v[b] + skip * x)).astype(BF16)
            gate_f_ref[at, here] = (up * al * wide_ref[b : b + 1, here]).astype(BF16)
            in_ref[at, here] = (be * z[b] + skip * u).astype(BF16)
            in_f_ref[at, here] = (be * wide_ref[2 + b : 3 + b, here]).astype(BF16)
            ux = jnp.sum((u * x).reshape(BLOCK // 8, 8, BLOCK), axis=0)
            skips += split_dot_right(ux, sel, 3)
    for b in range(2):
        p_ref[at_block(b), :] = p[b]
        q_ref[at_block(b), :] = q[b]
    skip_out_ref[...] = skips
    m00 = jnp.where(i >= j, m00, 0.0).astype(BF16)
    m11 = jnp.where(i >= j, m11, 0.0).astype(BF16)
    m10 = m10.astype(BF16)
    dr_ref[:, at_block(0)] = dot(wt[0], m00, nt)
    dr_ref[:, at_block(1)] = dot(wt[0], m10, nt) + dot(wt[1], m11, nt)
    dw_ref[:, at_block(0)] = dot(rt[0], m00) + dot(rt[1], m10)
    dw_ref[:, at_block(1)] = dot(rt[1], m11)


def kernel_after(first_ref, token_ref, out_ref):
    del first_ref, token_ref, out_ref


def head_sums(buffer_ref, key, weight_ref, index, heads):
    cols = weight_ref.shape[2]
    out = jnp.zeros((key.shape[0], heads), F32)
    for lo in range(0, cols, BLOCK):
        here = pl.ds(lo, BLOCK)
        product = weight_ref[index, :, here].astype(F32) * dot(key, buffer_ref[here, :])
        out += split_dot_right(product, selector(heads, lo, BLOCK), 2)
    return out


def pair_sums(one_ref, two_ref, cols, heads):
    out = jnp.zeros((8, heads), F32)
    for lo in range(0, cols, BLOCK):
        here = pl.ds(lo, BLOCK)
        product = one_ref[here, :].astype(F32) * two_ref[here, :].astype(F32)
        product = jnp.sum(product.reshape(STATE // 8, 8, BLOCK), axis=0)
        out += split_dot_right(product, selector(heads, lo, BLOCK), 2)
    return out


def kernel_early(e_ref, f_ref, keys_ref, qq_ref, small_ref, pe_ref, pf_ref, cross_ref):
    cols = qq_ref.shape[2]
    heads = small_ref.shape[1]
    place = lax.axis_index("context")
    mine = (place >= 2).astype(jnp.int32)
    side = lax.rem(place, 2)
    pe_ref[...] = head_sums(e_ref, keys_ref[mine], qq_ref, mine, heads)
    pf_ref[...] = head_sums(f_ref, keys_ref[side], qq_ref, side, heads)
    cross_ref[...] = pair_sums(e_ref, f_ref, cols, heads)


def total_of(ref, cols, heads):
    parts = ref[pl.ds(cols, 16), :].astype(F32)
    return (parts[0:1] + parts[1:2] + parts[2:3])[:, :heads]


def kernel_steps(
    h_ref, e_ref, f_ref, keys_ref, qq_ref, pe_ref, pf_ref, cross_ref, p_ref, q_ref,
    small_ref, z_ref, rate_ref, skips_ref,
    step_ref, sums_ref,
):
    rows, cols = qq_ref.shape[1:]
    heads = small_ref.shape[1]
    place = lax.axis_index("context")
    mine = (place >= 2).astype(jnp.int32)
    inner = (place == 1) | (place == 2)
    te, tf, th = (total_of(ref, cols, heads) for ref in (e_ref, f_ref, h_ref))
    ph = head_sums(h_ref, keys_ref[mine], qq_ref, mine, heads)
    cross = cross_ref[...] + te * pair_sums(h_ref, f_ref, cols, heads)
    cross = jnp.where(inner, jnp.sum(cross, axis=0, keepdims=True), 0.0)
    pe = pe_ref[...]
    pf = pf_ref[...]
    px = jnp.where(inner, pe + te * ph, pf + tf * (ph + th * pe))
    py = jnp.where(inner, pf, 0.0)
    row = lax.broadcasted_iota(jnp.int32, (rows, heads), 0)
    p = jnp.where(mine == 1, px, py) * jnp.where(row < BLOCK, small_ref[0:1], small_ref[1:2])
    q = jnp.where(mine == 1, py, px) * jnp.where(row < BLOCK, small_ref[2:3], small_ref[3:4])
    ends = jnp.sum(q, axis=0, keepdims=True) + small_ref[5:6] * cross
    q = q + q_ref[...]
    flow = split_dot_left(triangle(rows, False), p + p_ref[...] - q, 3) + ends
    z = z_ref[...]
    step = softplus(z)
    rate = jnp.exp(rate_ref[...])
    grad = (q / step - rate * flow) / (1.0 + jnp.exp(-z))
    step_ref[...] = grad.T
    sum_rate = jnp.sum(flow * step, axis=0, keepdims=True) * -rate
    sum_bias = jnp.sum(grad, axis=0, keepdims=True)
    sum_skip = jnp.sum(skips_ref[...], axis=0, keepdims=True)
    index = lax.broadcasted_iota(jnp.int32, (8, heads), 0)
    sums_ref[...] = jnp.where(
        index == 0, sum_rate, jnp.where(index == 1, sum_skip, jnp.where(index == 2, sum_bias, 0.0))
    )


def kernel_last(
    e_ref, f_ref, h_ref, keys_ref, qq_ref, wide_ref,
    gate_ref, gate_f_ref, in_ref, in_f_ref, dr_ref, dw_ref, after_ref,
    grad_in_ref, grad_gate_ref, keep_ref, send_ref,
    coef_e,
):
    del after_ref
    rows, cols = qq_ref.shape[1:]
    half = STATE // 2
    heads = cols // HEAD_DIM
    nt = ((1,), (1,))
    place = lax.axis_index("context")
    inner = (place == 1) | (place == 2)
    te, tf, th = (total_of(ref, cols, heads) for ref in (e_ref, f_ref, h_ref))
    coef = jnp.concatenate(
        [jnp.where(inner, 1.0, tf * th), jnp.where(inner, te, tf)] + [jnp.zeros_like(te)] * 6,
        axis=0,
    )
    for lo in range(0, cols, TILE):
        coef_e[:, pl.ds(lo, TILE)] = split_dot_right(coef, expander(heads, lo, TILE), 3)
    dr = [dr_ref[:, at_block(b)] for b in range(2)]
    dw = [dw_ref[:, at_block(b)] for b in range(2)]
    for lo in range(0, cols, BLOCK):
        here = pl.ds(lo, BLOCK)
        got_f = f_ref[here, :].astype(F32)
        x = (
            e_ref[here, :].astype(F32) * coef_e[0:1, here]
            + h_ref[here, :].astype(F32) * coef_e[1:2, here]
            + jnp.where(inner, 0.0, got_f)
        )
        y = jnp.where(inner, got_f, 0.0)
        s = jnp.where(place >= 2, x, y)
        a = jnp.where(place >= 2, y, x)
        s_half = s.astype(BF16)
        a_half = a.astype(BF16)
        for b in range(2):
            at = at_block(b)
            scaled_s = (s * wide_ref[b : b + 1, here]).astype(BF16)
            scaled_a = (a * wide_ref[2 + b : 3 + b, here]).astype(BF16)
            dr[b] += dot(scaled_s, qq_ref[1, at, here], nt)
            dw[b] += dot(scaled_a, qq_ref[0, at, here], nt)
            v = dot(keys_ref[1, at, :], s_half)
            z = dot(keys_ref[0, at, :], a_half)
            grad_gate_ref[at, here] = (
                gate_ref[at, here].astype(F32) + gate_f_ref[at, here].astype(F32) * v
            ).astype(BF16)
            grad_in_ref[at, here] = (
                in_ref[at, here].astype(F32) + in_f_ref[at, here].astype(F32) * z
            ).astype(BF16)
    for b in range(2):
        keep_ref[pl.ds(0, half), at_block(b)] = dw[b][:half]
        keep_ref[pl.ds(half, half), at_block(b)] = dr[b][:half]
        send_ref[pl.ds(0, half), at_block(b)] = dw[b][half:].astype(BF16)
        send_ref[pl.ds(half, half), at_block(b)] = dr[b][half:].astype(BF16)


def kernel_add(a_ref, b_ref, c_ref, d_ref, out_ref):
    out_ref[...] = (a_ref[...] + b_ref[...]) + (c_ref[...] + d_ref[...])


def kernel_finish(
    keep_ref, got_ref, a_ref, b_ref, c_ref, d_ref, w_ref, r_ref, rate_ref, skip_ref, bias_ref
):
    half = w_ref.shape[0]
    w_ref[...] = keep_ref[pl.ds(0, half), :] + got_ref[pl.ds(0, half), :].astype(F32)
    r_ref[...] = keep_ref[pl.ds(half, half), :] + got_ref[pl.ds(half, half), :].astype(F32)
    sums = (a_ref[...] + b_ref[...]) + (c_ref[...] + d_ref[...])
    rate_ref[...] = sums[0:1]
    skip_ref[...] = sums[1:2]
    bias_ref[...] = sums[2:3]


V = pltpu.VMEM
ANY = pl.ANY


def call(kernel, outs, args, scratch=(), us=3.0, spaces=None, out_spaces=None, alias=None):
    spaces = spaces or [V] * len(args)
    out_spaces = out_spaces or [V] * len(outs)
    return pl.pallas_call(
        kernel,
        out_shape=[jax.ShapeDtypeStruct(s, d) for s, d in outs],
        in_specs=[pl.BlockSpec(memory_space=s) for s in spaces],
        out_specs=[pl.BlockSpec(memory_space=s) for s in out_spaces],
        scratch_shapes=list(scratch),
        input_output_aliases=alias or {},
        compiler_params=pltpu.CompilerParams(vmem_limit_bytes=36 * 1024 * 1024),
        cost_estimate=pl.CostEstimate(
            flops=int(us * 1e9), bytes_accessed=int(us * 1e6), transcendentals=0
        ),
    )(*args)


def exchange(array, axis, mask):
    count = lax.axis_size(axis)
    pairs = [(i, i ^ mask) for i in range(count) if i ^ mask < count]
    return lax.ppermute(array, axis, pairs)


def body(
    head_inputs,
    gate_inputs,
    step_raw,
    state_write,
    state_read,
    log_rate,
    skip_gain,
    step_bias,
    grad_gated,
):
    x, g, dy = head_inputs[0], gate_inputs[0], grad_gated[0]
    raw = step_raw[0].T
    heads, rows = raw.shape
    cols = x.shape[1]
    half = state_write.shape[2]
    w, r = state_write[0].T, state_read[0].T
    wt, rt = exchange(w, "tensor", 1), exchange(r, "tensor", 1)
    rate, skip, bias = (v.reshape(1, heads) for v in (log_rate, skip_gain, step_bias))
    payload = ((cols + 16, STATE), BF16)
    big = ((rows, cols), BF16)
    pair = ((2, rows, cols), BF16)
    thin = ((rows, heads), F32)
    tiny = ((8, heads), F32)
    one = ((1, heads), F32)
    key = ((half, rows), BF16)
    x, g, dy, w, r, skip, qq, z, rate, al, be, wide, small = call(
        kernel_scale,
        [big, big, big, key, key, one, pair, thin, one, thin, thin, ((8, cols), F32), tiny],
        [
            pltpu.with_memory_space_constraint(v, pltpu.HBM)
            for v in (x, g, dy, raw, bias, rate, skip, w, r)
        ],
        [V((heads, rows), F32), V((1, heads), F32), V((rows, cols), F32), V((rows, cols), F32),
         pltpu.SemaphoreType.DMA((12,))],
        spaces=[pltpu.HBM] * 9,
    )
    turned, send_e, send_f = call(
        kernel_states,
        [((2, STATE, rows), BF16), payload, payload],
        [w, wt, r, rt, qq, wide, small],
    )
    got_e = exchange(send_e, "context", 3)
    got_f = exchange(send_f, "context", 1)
    gate, gate_f, inp, inp_f, dr, dw, keys, p, q, skips = call(
        kernel_within,
        [big] * 4 + [((STATE, rows), F32)] * 2 + [((2, rows, STATE), BF16), thin, thin, tiny],
        [x, g, dy, skip, turned, qq, al, be, wide],
        [V((rows, cols), F32)] * 2 + [V((8, cols), F32)],
        us=4.0,
    )
    (got_e,) = call(
        kernel_after, [payload], [got_e, skips],
        spaces=[ANY, ANY], out_spaces=[ANY], alias={0: 0}, us=0.01,
    )
    got_h = exchange(got_e, "context", 1)
    pe, pf, cross = call(
        kernel_early, [thin, thin, tiny], [got_e, got_f, keys, qq, small], us=2.0
    )
    grad_step, sums = call(
        kernel_steps,
        [((heads, rows), F32), tiny],
        [got_h, got_e, got_f, keys, qq, pe, pf, cross, p, q, small, z, rate, skips],
        us=1.0,
    )
    others = [exchange(sums, "context", mask) for mask in (1, 2, 3)]
    grad_in, grad_gate, keep, send = call(
        kernel_last,
        [big, big, ((STATE, rows), F32), ((STATE, rows), BF16)],
        [got_e, got_f, got_h, keys, qq, wide, gate, gate_f, inp, inp_f, dr, dw, others[-1]],
        [V((8, cols), F32)],
        us=2.0,
        spaces=[V] * 12 + [ANY],
    )
    (sums,) = call(kernel_add, [tiny], [sums] + others, us=0.1)
    got = exchange(send, "tensor", 1)
    others = [exchange(sums, "dp", mask) for mask in (1, 2, 3)]
    grad_w, grad_r, sum_rate, sum_skip, sum_bias = call(
        kernel_finish,
        [((half, rows), F32)] * 2 + [one] * 3,
        [keep, got, sums] + others,
        us=0.2,
    )
    return (
        grad_in[None],
        grad_gate[None],
        grad_w.T[None],
        grad_r.T[None],
        grad_step.T[None],
        sum_rate.reshape(heads),
        sum_skip.reshape(heads),
        sum_bias.reshape(heads),
    )


def solution(mesh):
    wide = P("dp", "context", "tensor")
    head = P("tensor")
    return jax.shard_map(
        body,
        mesh=mesh,
        in_specs=(wide,) * 5 + (head,) * 3 + (wide,),
        out_specs=(wide,) * 5 + (head,) * 3,
        check_vma=False,
    )
```

```python
import functools
import math

import jax
import jax.numpy as jnp
from jax import lax
from jax.experimental import pallas as pl
from jax.experimental.pallas import tpu as pltpu
from jax.sharding import PartitionSpec as P

HEAD_DIM = 64
STATE = 128
BLOCK = 128
LOG2E = math.log2(math.e)
F32 = jnp.float32
BF16 = jnp.bfloat16
TILE = 256


def dot(a, b, dims=((1,), (0,))):
    return lax.dot_general(a, b, (dims, ((), ())), preferred_element_type=F32)


def pieces(v, count):
    out = []
    for _ in range(count):
        part = v.astype(BF16)
        out.append(part)
        v = v - part.astype(F32)
    return out


def split_dot_left(exact, v, count):
    return sum(dot(exact, part) for part in pieces(v, count))


def split_dot_right(v, exact, count):
    return sum(dot(part, exact) for part in pieces(v, count))


def expander(heads, lo, size):
    head = lax.broadcasted_iota(jnp.int32, (heads, size), 0)
    column = lax.broadcasted_iota(jnp.int32, (heads, size), 1) + lo
    return ((column >= head * HEAD_DIM) & (column < (head + 1) * HEAD_DIM)).astype(BF16)


def selector(heads, lo, size):
    head = lax.broadcasted_iota(jnp.int32, (size, heads), 1)
    column = lax.broadcasted_iota(jnp.int32, (size, heads), 0) + lo
    return ((column >= head * HEAD_DIM) & (column < (head + 1) * HEAD_DIM)).astype(BF16)


def triangle(rows, lower):
    i = lax.broadcasted_iota(jnp.int32, (rows, rows), 0)
    j = lax.broadcasted_iota(jnp.int32, (rows, rows), 1)
    return ((i >= j) if lower else (i <= j)).astype(BF16)


def softplus(z):
    return jnp.maximum(z, 0.0) + jnp.log(1.0 + jnp.exp(-jnp.abs(z)))


def logistic(v):
    return 0.5 + 0.5 * jnp.tanh(0.5 * v)


def at_block(b):
    return pl.ds(b * BLOCK, BLOCK)


def kernel_scale(
    x_in, g_in, dy_in, raw_in, bias_in, rate_in, skip_in, w_in, r_in,
    x_ref, g_ref, dy_ref, w_ref, r_ref, skip_ref, qq_ref, z_ref, rate_ref, al_ref, be_ref,
    wide_ref, small_ref,
    raw_ref, bias_ref, sems,
):
    rows, cols = x_ref.shape
    heads = raw_ref.shape[0]
    blocks = rows // BLOCK
    thin = [
        (raw_in, raw_ref), (bias_in, bias_ref), (rate_in, rate_ref),
        (skip_in, skip_ref), (w_in, w_ref), (r_in, r_ref),
    ]
    copies = [pltpu.make_async_copy(s, d, sems.at[i]) for i, (s, d) in enumerate(thin)]
    large = []
    for b in range(blocks):
        large.append([
            pltpu.make_async_copy(s.at[at_block(b)], d.at[at_block(b)], sems.at[6 + 3 * b + i])
            for i, (s, d) in enumerate([(g_in, g_ref), (dy_in, dy_ref), (x_in, x_ref)])
        ])
    for copy in copies[:3] + large[0] + large[1] + copies[3:]:
        copy.start()
    for copy in copies[:3]:
        copy.wait()
    z = raw_ref[...].T + bias_ref[...]
    z_ref[...] = z
    step = softplus(z)
    log2_decay = step * (-LOG2E * jnp.exp(rate_ref[...]))
    run = split_dot_left(triangle(rows, True), log2_decay, 3)
    mid0 = run[BLOCK // 2 - 1 : BLOCK // 2]
    mid1 = run[BLOCK + BLOCK // 2 - 1 : BLOCK + BLOCK // 2]
    end = run[rows - 1 : rows]
    row = lax.broadcasted_iota(jnp.int32, (rows, heads), 0)
    rel = run - jnp.where(row < BLOCK, mid0, mid1)
    for copy in large[0]:
        copy.wait()
    al = jnp.exp2(rel)
    be = jnp.exp2(-rel) * step
    al_ref[...] = al
    be_ref[...] = be
    small = jnp.exp2(
        jnp.concatenate([mid0, mid1, end - mid0, end - mid1, mid1 - mid0, end, end, end], axis=0)
    )
    small_ref[...] = small
    small_parts = pieces(small, 3)
    al_parts = pieces(al, 2)
    be_parts = pieces(be, 2)
    for lo in range(0, cols, TILE):
        wide = expander(heads, lo, TILE)
        wide_ref[:, pl.ds(lo, TILE)] = sum(dot(part, wide) for part in small_parts)
    for b in range(blocks):
        if b:
            for copy in large[b]:
                copy.wait()
        at = at_block(b)
        part = slice(b * BLOCK, (b + 1) * BLOCK)
        for lo in range(0, cols, TILE):
            here = pl.ds(lo, TILE)
            wide = expander(heads, lo, TILE)
            al_tile = sum(dot(v[part], wide) for v in al_parts)
            be_tile = sum(dot(v[part], wide) for v in be_parts)
            g = g_ref[at, here].astype(F32)
            u = dy_ref[at, here].astype(F32) * g * logistic(g)
            qq_ref[1, at, here] = (u * al_tile).astype(BF16)
            qq_ref[0, at, here] = (x_ref[at, here].astype(F32) * be_tile).astype(BF16)
    for copy in copies[3:]:
        copy.wait()


def kernel_states(
    w_ref, wt_ref, r_ref, rt_ref, qq_ref, wide_ref, small_ref, turned_ref, e_ref, f_ref
):
    cols = qq_ref.shape[2]
    blocks = qq_ref.shape[1] // BLOCK
    place = lax.axis_index("context")
    writes = jnp.concatenate([w_ref[...], wt_ref[...]], axis=0)
    reads = jnp.concatenate([r_ref[...], rt_ref[...]], axis=0)
    turned_ref[0] = writes
    turned_ref[1] = reads
    for lo in range(0, cols, BLOCK):
        here = pl.ds(lo, BLOCK)
        state = jnp.zeros((STATE, BLOCK), F32)
        adjoint = state
        for b in range(blocks):
            at = at_block(b)
            part = slice(b * BLOCK, (b + 1) * BLOCK)
            state += dot(writes[:, part], qq_ref[0, at, here]) * wide_ref[2 + b : 3 + b, here]
            adjoint += dot(reads[:, part], qq_ref[1, at, here]) * wide_ref[b : b + 1, here]
        e_ref[here, :] = jnp.where(place < 2, state, adjoint).astype(BF16)
        f_ref[here, :] = jnp.where(lax.rem(place, 2) == 0, state, adjoint).astype(BF16)
    heads = small_ref.shape[1]
    total = jnp.concatenate(
        [small_ref[5:6], jnp.zeros((1, STATE - heads), F32)], axis=1
    )
    parts = [part.astype(F32) for part in pieces(total, 3)]
    totals = jnp.concatenate(parts + [jnp.zeros((13, STATE), F32)], axis=0).astype(BF16)
    e_ref[pl.ds(cols, 16), :] = totals
    f_ref[pl.ds(cols, 16), :] = totals


def kernel_within(
    x_ref, g_ref, dy_ref, skip_ref, turned_ref, qq_ref, al_ref, be_ref, wide_ref,
    gate_ref, gate_f_ref, in_ref, in_f_ref, dr_ref, dw_ref, keys_ref, p_ref, q_ref, skip_out_ref,
    al_e, be_e, skip_e,
):
    rows, cols = x_ref.shape
    heads = skip_ref.shape[1]
    for lo in range(0, cols, TILE):
        wide = expander(heads, lo, TILE)
        here = pl.ds(lo, TILE)
        al_e[:, here] = split_dot_right(al_ref[...], wide, 2)
        be_e[:, here] = split_dot_right(be_ref[...], wide, 2)
        skip_e[:, here] = split_dot_right(jnp.broadcast_to(skip_ref[...], (8, heads)), wide, 3)
    nt = ((1,), (1,))
    wt = [turned_ref[0, :, at_block(b)] for b in range(2)]
    rt = [turned_ref[1, :, at_block(b)] for b in range(2)]
    w = [v.astype(F32).T.astype(BF16) for v in wt]
    r = [v.astype(F32).T.astype(BF16) for v in rt]
    for b in range(2):
        keys_ref[0, at_block(b), :] = w[b]
        keys_ref[1, at_block(b), :] = r[b]
    i = lax.broadcasted_iota(jnp.int32, (BLOCK, BLOCK), 0)
    j = lax.broadcasted_iota(jnp.int32, (BLOCK, BLOCK), 1)
    i00 = jnp.where(i >= j, dot(r[0], wt[0]), 0.0).astype(BF16)
    i11 = jnp.where(i >= j, dot(r[1], wt[1]), 0.0).astype(BF16)
    i10 = dot(r[1], wt[0]).astype(BF16)
    t00 = jnp.where(i <= j, dot(w[0], rt[0]), 0.0).astype(BF16)
    t11 = jnp.where(i <= j, dot(w[1], rt[1]), 0.0).astype(BF16)
    t10 = dot(w[0], rt[1]).astype(BF16)
    m00 = jnp.zeros((BLOCK, BLOCK), F32)
    m11 = m00
    m10 = m00
    p = [jnp.zeros((BLOCK, heads), F32)] * 2
    q = [jnp.zeros((BLOCK, heads), F32)] * 2
    skips = jnp.zeros((8, heads), F32)
    for lo in range(0, cols, BLOCK):
        here = pl.ds(lo, BLOCK)
        sel = selector(heads, lo, BLOCK)
        link = wide_ref[4:5, here]
        xb = [qq_ref[0, at_block(b), here] for b in range(2)]
        ua = [qq_ref[1, at_block(b), here] for b in range(2)]
        m00 += dot(ua[0], xb[0], nt)
        m11 += dot(ua[1], xb[1], nt)
        m10 += dot(ua[1], (xb[0].astype(F32) * link).astype(BF16), nt)
        v = [dot(i00, xb[0]), dot(i11, xb[1]) + link * dot(i10, xb[0])]
        z = [dot(t00, ua[0]) + link * dot(t10, ua[1]), dot(t11, ua[1])]
        skip = skip_e[0:1, here]
        for b in range(2):
            at = at_block(b)
            p[b] += split_dot_right(ua[b].astype(F32) * v[b], sel, 2)
            q[b] += split_dot_right(xb[b].astype(F32) * z[b], sel, 2)
            g = g_ref[at, here].astype(F32)
            dy = dy_ref[at, here].astype(F32)
            x = x_ref[at, here].astype(F32)
            sig = logistic(g)
            u = dy * g * sig
            up = dy * sig * (1.0 + g * (1.0 - sig))
            al = al_e[at, here]
            be = be_e[at, here]
            gate_ref[at, here] = (up * (al * v[b] + skip * x)).astype(BF16)
            gate_f_ref[at, here] = (up * al * wide_ref[b : b + 1, here]).astype(BF16)
            in_ref[at, here] = (be * z[b] + skip * u).astype(BF16)
            in_f_ref[at, here] = (be * wide_ref[2 + b : 3 + b, here]).astype(BF16)
            ux = jnp.sum((u * x).reshape(BLOCK // 8, 8, BLOCK), axis=0)
            skips += split_dot_right(ux, sel, 3)
    for b in range(2):
        p_ref[at_block(b), :] = p[b]
        q_ref[at_block(b), :] = q[b]
    skip_out_ref[...] = skips
    m00 = jnp.where(i >= j, m00, 0.0).astype(BF16)
    m11 = jnp.where(i >= j, m11, 0.0).astype(BF16)
    m10 = m10.astype(BF16)
    dr_ref[:, at_block(0)] = dot(wt[0], m00, nt)
    dr_ref[:, at_block(1)] = dot(wt[0], m10, nt) + dot(wt[1], m11, nt)
    dw_ref[:, at_block(0)] = dot(rt[0], m00) + dot(rt[1], m10)
    dw_ref[:, at_block(1)] = dot(rt[1], m11)


def kernel_after(first_ref, token_ref, out_ref):
    del first_ref, token_ref, out_ref


def head_sums(buffer_ref, key, weight_ref, index, heads):
    cols = weight_ref.shape[2]
    parts, select = [], []
    for lo in range(0, cols, TILE):
        tile = jnp.concatenate(
            [buffer_ref[pl.ds(lo + k, BLOCK), :] for k in range(0, TILE, BLOCK)], axis=1
        )
        product = weight_ref[index, :, pl.ds(lo, TILE)].astype(F32) * dot(key, tile)
        sel = selector(heads, lo, TILE)
        for part in pieces(product, 2):
            parts.append(part)
            select.append(sel)
    return dot(jnp.concatenate(parts, axis=1), jnp.concatenate(select, axis=0))


def pair_sums(one_ref, two_ref, cols, heads):
    out = jnp.zeros((8, heads), F32)
    for lo in range(0, cols, BLOCK):
        here = pl.ds(lo, BLOCK)
        product = one_ref[here, :].astype(F32) * two_ref[here, :].astype(F32)
        product = jnp.sum(product.reshape(STATE // 8, 8, BLOCK), axis=0)
        out += split_dot_right(product, selector(heads, lo, BLOCK), 2)
    return out


def kernel_early(e_ref, f_ref, keys_ref, qq_ref, small_ref, pe_ref, pf_ref, cross_ref):
    cols = qq_ref.shape[2]
    heads = small_ref.shape[1]
    place = lax.axis_index("context")
    mine = (place >= 2).astype(jnp.int32)
    side = lax.rem(place, 2)
    pe_ref[...] = head_sums(e_ref, keys_ref[mine], qq_ref, mine, heads)
    pf_ref[...] = head_sums(f_ref, keys_ref[side], qq_ref, side, heads)
    cross_ref[...] = pair_sums(e_ref, f_ref, cols, heads)


def total_of(ref, cols, heads):
    parts = ref[pl.ds(cols, 16), :].astype(F32)
    return (parts[0:1] + parts[1:2] + parts[2:3])[:, :heads]


def kernel_steps(
    h_ref, e_ref, f_ref, keys_ref, qq_ref, pe_ref, pf_ref, cross_ref, p_ref, q_ref,
    small_ref, z_ref, rate_ref, skips_ref,
    step_ref, sums_ref,
):
    rows, cols = qq_ref.shape[1:]
    heads = small_ref.shape[1]
    place = lax.axis_index("context")
    mine = (place >= 2).astype(jnp.int32)
    inner = (place == 1) | (place == 2)
    te, tf, th = (total_of(ref, cols, heads) for ref in (e_ref, f_ref, h_ref))
    ph = head_sums(h_ref, keys_ref[mine], qq_ref, mine, heads)
    cross = cross_ref[...] + te * pair_sums(h_ref, f_ref, cols, heads)
    cross = jnp.where(inner, jnp.sum(cross, axis=0, keepdims=True), 0.0)
    pe = pe_ref[...]
    pf = pf_ref[...]
    px = jnp.where(inner, pe + te * ph, pf + tf * (ph + th * pe))
    py = jnp.where(inner, pf, 0.0)
    row = lax.broadcasted_iota(jnp.int32, (rows, heads), 0)
    p = jnp.where(mine == 1, px, py) * jnp.where(row < BLOCK, small_ref[0:1], small_ref[1:2])
    q = jnp.where(mine == 1, py, px) * jnp.where(row < BLOCK, small_ref[2:3], small_ref[3:4])
    ends = jnp.sum(q, axis=0, keepdims=True) + small_ref[5:6] * cross
    q = q + q_ref[...]
    flow = split_dot_left(triangle(rows, False), p + p_ref[...] - q, 3) + ends
    z = z_ref[...]
    step = softplus(z)
    rate = jnp.exp(rate_ref[...])
    grad = (q / step - rate * flow) / (1.0 + jnp.exp(-z))
    step_ref[...] = grad.T
    sum_rate = jnp.sum(flow * step, axis=0, keepdims=True) * -rate
    sum_bias = jnp.sum(grad, axis=0, keepdims=True)
    sum_skip = jnp.sum(skips_ref[...], axis=0, keepdims=True)
    index = lax.broadcasted_iota(jnp.int32, (8, heads), 0)
    sums_ref[...] = jnp.where(
        index == 0, sum_rate, jnp.where(index == 1, sum_skip, jnp.where(index == 2, sum_bias, 0.0))
    )


def kernel_keys(
    e_ref, f_ref, h_ref, qq_ref, wide_ref, dr_ref, dw_ref, after_ref,
    keep_ref, send_ref, both_ref,
    coef_e,
):
    del after_ref
    cols = qq_ref.shape[2]
    half = STATE // 2
    heads = cols // HEAD_DIM
    nt = ((1,), (1,))
    place = lax.axis_index("context")
    inner = (place == 1) | (place == 2)
    te, tf, th = (total_of(ref, cols, heads) for ref in (e_ref, f_ref, h_ref))
    coef = jnp.concatenate(
        [jnp.where(inner, 1.0, tf * th), jnp.where(inner, te, tf)] + [jnp.zeros_like(te)] * 6,
        axis=0,
    )
    for lo in range(0, cols, TILE):
        coef_e[:, pl.ds(lo, TILE)] = split_dot_right(coef, expander(heads, lo, TILE), 3)
    dr = [dr_ref[:, at_block(b)] for b in range(2)]
    dw = [dw_ref[:, at_block(b)] for b in range(2)]
    for lo in range(0, cols, BLOCK):
        here = pl.ds(lo, BLOCK)
        got_f = f_ref[here, :].astype(F32)
        x = (
            e_ref[here, :].astype(F32) * coef_e[0:1, here]
            + h_ref[here, :].astype(F32) * coef_e[1:2, here]
            + jnp.where(inner, 0.0, got_f)
        )
        y = jnp.where(inner, got_f, 0.0)
        s = jnp.where(place >= 2, x, y)
        a = jnp.where(place >= 2, y, x)
        both_ref[0, :, here] = a.astype(BF16)
        both_ref[1, :, here] = s.astype(BF16)
        for b in range(2):
            at = at_block(b)
            scaled_s = (s * wide_ref[b : b + 1, here]).astype(BF16)
            scaled_a = (a * wide_ref[2 + b : 3 + b, here]).astype(BF16)
            dr[b] += dot(scaled_s, qq_ref[1, at, here], nt)
            dw[b] += dot(scaled_a, qq_ref[0, at, here], nt)
    for b in range(2):
        keep_ref[pl.ds(0, half), at_block(b)] = dw[b][:half]
        keep_ref[pl.ds(half, half), at_block(b)] = dr[b][:half]
        send_ref[pl.ds(0, half), at_block(b)] = dw[b][half:].astype(BF16)
        send_ref[pl.ds(half, half), at_block(b)] = dr[b][half:].astype(BF16)


def kernel_outer(
    both_ref, keys_ref, gate_ref, gate_f_ref, in_ref, in_f_ref, step_ref,
    grad_in_ref, grad_gate_ref, grad_step_ref,
):
    grad_step_ref[...] = step_ref[...]
    rows, cols = gate_ref.shape
    for lo in range(0, cols, BLOCK):
        here = pl.ds(lo, BLOCK)
        for b in range(2):
            at = at_block(b)
            v = dot(keys_ref[1, at, :], both_ref[1, :, here])
            z = dot(keys_ref[0, at, :], both_ref[0, :, here])
            grad_gate_ref[at, here] = (
                gate_ref[at, here].astype(F32) + gate_f_ref[at, here].astype(F32) * v
            ).astype(BF16)
            grad_in_ref[at, here] = (
                in_ref[at, here].astype(F32) + in_f_ref[at, here].astype(F32) * z
            ).astype(BF16)


def kernel_add(a_ref, b_ref, c_ref, d_ref, out_ref):
    out_ref[...] = (a_ref[...] + b_ref[...]) + (c_ref[...] + d_ref[...])


def kernel_finish(
    keep_ref, got_ref, a_ref, b_ref, c_ref, d_ref, w_ref, r_ref, rate_ref, skip_ref, bias_ref
):
    half = w_ref.shape[0]
    w_ref[...] = keep_ref[pl.ds(0, half), :] + got_ref[pl.ds(0, half), :].astype(F32)
    r_ref[...] = keep_ref[pl.ds(half, half), :] + got_ref[pl.ds(half, half), :].astype(F32)
    sums = (a_ref[...] + b_ref[...]) + (c_ref[...] + d_ref[...])
    rate_ref[...] = sums[0:1]
    skip_ref[...] = sums[1:2]
    bias_ref[...] = sums[2:3]


V = pltpu.VMEM
ANY = pl.ANY


def call(kernel, outs, args, scratch=(), us=3.0, spaces=None, out_spaces=None, alias=None):
    spaces = spaces or [V] * len(args)
    out_spaces = out_spaces or [V] * len(outs)
    return pl.pallas_call(
        kernel,
        out_shape=[jax.ShapeDtypeStruct(s, d) for s, d in outs],
        in_specs=[pl.BlockSpec(memory_space=s) for s in spaces],
        out_specs=[pl.BlockSpec(memory_space=s) for s in out_spaces],
        scratch_shapes=list(scratch),
        input_output_aliases=alias or {},
        compiler_params=pltpu.CompilerParams(vmem_limit_bytes=36 * 1024 * 1024),
        cost_estimate=pl.CostEstimate(
            flops=int(us * 1e9), bytes_accessed=int(us * 1e6), transcendentals=0
        ),
    )(*args)


def exchange(array, axis, mask):
    count = lax.axis_size(axis)
    pairs = [(i, i ^ mask) for i in range(count) if i ^ mask < count]
    return lax.ppermute(array, axis, pairs)


def body(
    head_inputs,
    gate_inputs,
    step_raw,
    state_write,
    state_read,
    log_rate,
    skip_gain,
    step_bias,
    grad_gated,
):
    x, g, dy = head_inputs[0], gate_inputs[0], grad_gated[0]
    raw = step_raw[0].T
    heads, rows = raw.shape
    cols = x.shape[1]
    half = state_write.shape[2]
    w, r = state_write[0].T, state_read[0].T
    wt, rt = exchange(w, "tensor", 1), exchange(r, "tensor", 1)
    rate, skip, bias = (v.reshape(1, heads) for v in (log_rate, skip_gain, step_bias))
    payload = ((cols + 16, STATE), BF16)
    big = ((rows, cols), BF16)
    pair = ((2, rows, cols), BF16)
    thin = ((rows, heads), F32)
    tiny = ((8, heads), F32)
    one = ((1, heads), F32)
    key = ((half, rows), BF16)
    x, g, dy, w, r, skip, qq, z, rate, al, be, wide, small = call(
        kernel_scale,
        [big, big, big, key, key, one, pair, thin, one, thin, thin, ((8, cols), F32), tiny],
        [
            pltpu.with_memory_space_constraint(v, pltpu.HBM)
            for v in (x, g, dy, raw, bias, rate, skip, w, r)
        ],
        [V((heads, rows), F32), V((1, heads), F32), pltpu.SemaphoreType.DMA((12,))],
        spaces=[pltpu.HBM] * 9,
    )
    turned, send_e, send_f = call(
        kernel_states,
        [((2, STATE, rows), BF16), payload, payload],
        [w, wt, r, rt, qq, wide, small],
    )
    got_e = exchange(send_e, "context", 3)
    got_f = exchange(send_f, "context", 1)
    gate, gate_f, inp, inp_f, dr, dw, keys, p, q, skips = call(
        kernel_within,
        [big] * 4 + [((STATE, rows), F32)] * 2 + [((2, rows, STATE), BF16), thin, thin, tiny],
        [x, g, dy, skip, turned, qq, al, be, wide],
        [V((rows, cols), F32)] * 2 + [V((8, cols), F32)],
        us=4.0,
    )
    (got_e,) = call(
        kernel_after, [payload], [got_e, skips],
        spaces=[ANY, ANY], out_spaces=[ANY], alias={0: 0}, us=0.01,
    )
    got_h = exchange(got_e, "context", 1)
    pe, pf, cross = call(
        kernel_early, [thin, thin, tiny], [got_e, got_f, keys, qq, small], us=2.0
    )
    grad_step, sums = call(
        kernel_steps,
        [((heads, rows), F32), tiny],
        [got_h, got_e, got_f, keys, qq, pe, pf, cross, p, q, small, z, rate, skips],
        us=1.0,
    )
    others = [exchange(sums, "context", mask) for mask in (1, 2, 3)]
    keep, send, ends = call(
        kernel_keys,
        [((STATE, rows), F32), ((STATE, rows), BF16), ((2, STATE, cols), BF16)],
        [got_e, got_f, got_h, qq, wide, dr, dw, sums],
        [V((8, cols), F32)],
        us=1.0,
        spaces=[V] * 7 + [ANY],
    )
    grad_in, grad_gate, grad_step = call(
        kernel_outer, [big, big, ((heads, rows), F32)],
        [ends, keys, gate, gate_f, inp, inp_f, grad_step], us=2.0,
    )
    (sums,) = call(kernel_add, [tiny], [sums] + others, us=0.1)
    got = exchange(send, "tensor", 1)
    others = [exchange(sums, "dp", mask) for mask in (1, 2, 3)]
    grad_w, grad_r, sum_rate, sum_skip, sum_bias = call(
        kernel_finish,
        [((half, rows), F32)] * 2 + [one] * 3,
        [keep, got, sums] + others,
        us=0.2,
    )
    return (
        grad_in[None],
        grad_gate[None],
        grad_w.T[None],
        grad_r.T[None],
        grad_step.T[None],
        sum_rate.reshape(heads),
        sum_skip.reshape(heads),
        sum_bias.reshape(heads),
    )


def solution(mesh):
    wide = P("dp", "context", "tensor")
    head = P("tensor")
    return jax.shard_map(
        body,
        mesh=mesh,
        in_specs=(wide,) * 5 + (head,) * 3 + (wide,),
        out_specs=(wide,) * 5 + (head,) * 3,
        check_vma=False,
    )
```

```python
import functools
import math

import jax
import jax.numpy as jnp
from jax import lax
from jax.experimental import pallas as pl
from jax.experimental.pallas import tpu as pltpu
from jax.sharding import PartitionSpec as P

HEAD_DIM = 64
STATE = 128
BLOCK = 128
LOG2E = math.log2(math.e)
F32 = jnp.float32
BF16 = jnp.bfloat16
TILE = 256


def dot(a, b, dims=((1,), (0,))):
    return lax.dot_general(a, b, (dims, ((), ())), preferred_element_type=F32)


def pieces(v, count):
    out = []
    for _ in range(count):
        part = v.astype(BF16)
        out.append(part)
        v = v - part.astype(F32)
    return out


def split_dot_left(exact, v, count):
    return sum(dot(exact, part) for part in pieces(v, count))


def split_dot_right(v, exact, count):
    return sum(dot(part, exact) for part in pieces(v, count))


def expander(heads, lo, size):
    head = lax.broadcasted_iota(jnp.int32, (heads, size), 0)
    column = lax.broadcasted_iota(jnp.int32, (heads, size), 1) + lo
    return ((column >= head * HEAD_DIM) & (column < (head + 1) * HEAD_DIM)).astype(BF16)


def selector(heads, lo, size):
    head = lax.broadcasted_iota(jnp.int32, (size, heads), 1)
    column = lax.broadcasted_iota(jnp.int32, (size, heads), 0) + lo
    return ((column >= head * HEAD_DIM) & (column < (head + 1) * HEAD_DIM)).astype(BF16)


def triangle(rows, lower):
    i = lax.broadcasted_iota(jnp.int32, (rows, rows), 0)
    j = lax.broadcasted_iota(jnp.int32, (rows, rows), 1)
    return ((i >= j) if lower else (i <= j)).astype(BF16)


def softplus(z):
    return jnp.maximum(z, 0.0) + jnp.log(1.0 + jnp.exp(-jnp.abs(z)))


def logistic(v):
    return 0.5 + 0.5 * jnp.tanh(0.5 * v)


def at_block(b):
    return pl.ds(b * BLOCK, BLOCK)


def kernel_scale(
    x_in, g_in, dy_in, raw_in, bias_in, rate_in, skip_in, w_in, r_in,
    x_ref, g_ref, dy_ref, w_ref, r_ref, skip_ref, qq_ref, z_ref, rate_ref, al_ref, be_ref,
    wide_ref, small_ref,
    raw_ref, bias_ref, sems,
):
    rows, cols = x_ref.shape
    heads = raw_ref.shape[0]
    blocks = rows // BLOCK
    thin = [
        (raw_in, raw_ref), (bias_in, bias_ref), (rate_in, rate_ref),
        (skip_in, skip_ref), (w_in, w_ref), (r_in, r_ref),
    ]
    copies = [pltpu.make_async_copy(s, d, sems.at[i]) for i, (s, d) in enumerate(thin)]
    large = []
    for b in range(blocks):
        large.append([
            pltpu.make_async_copy(s.at[at_block(b)], d.at[at_block(b)], sems.at[6 + 3 * b + i])
            for i, (s, d) in enumerate([(g_in, g_ref), (dy_in, dy_ref), (x_in, x_ref)])
        ])
    for copy in copies[:3] + large[0] + large[1] + copies[3:]:
        copy.start()
    for copy in copies[:3]:
        copy.wait()
    z = raw_ref[...].T + bias_ref[...]
    z_ref[...] = z
    step = softplus(z)
    log2_decay = step * (-LOG2E * jnp.exp(rate_ref[...]))
    run = split_dot_left(triangle(rows, True), log2_decay, 3)
    mid0 = run[BLOCK // 2 - 1 : BLOCK // 2]
    mid1 = run[BLOCK + BLOCK // 2 - 1 : BLOCK + BLOCK // 2]
    end = run[rows - 1 : rows]
    row = lax.broadcasted_iota(jnp.int32, (rows, heads), 0)
    rel = run - jnp.where(row < BLOCK, mid0, mid1)
    for copy in large[0]:
        copy.wait()
    al = jnp.exp2(rel)
    be = jnp.exp2(-rel) * step
    al_ref[...] = al
    be_ref[...] = be
    small = jnp.exp2(
        jnp.concatenate([mid0, mid1, end - mid0, end - mid1, mid1 - mid0, end, end, end], axis=0)
    )
    small_ref[...] = small
    small_parts = pieces(small, 3)
    al_parts = pieces(al, 2)
    be_parts = pieces(be, 2)
    for lo in range(0, cols, TILE):
        wide = expander(heads, lo, TILE)
        wide_ref[:, pl.ds(lo, TILE)] = sum(dot(part, wide) for part in small_parts)
    for b in range(blocks):
        if b:
            for copy in large[b]:
                copy.wait()
        at = at_block(b)
        part = slice(b * BLOCK, (b + 1) * BLOCK)
        for lo in range(0, cols, TILE):
            here = pl.ds(lo, TILE)
            wide = expander(heads, lo, TILE)
            al_tile = sum(dot(v[part], wide) for v in al_parts)
            be_tile = sum(dot(v[part], wide) for v in be_parts)
            g = g_ref[at, here].astype(F32)
            u = dy_ref[at, here].astype(F32) * g * logistic(g)
            qq_ref[1, at, here] = (u * al_tile).astype(BF16)
            qq_ref[0, at, here] = (x_ref[at, here].astype(F32) * be_tile).astype(BF16)
    for copy in copies[3:]:
        copy.wait()


def kernel_states(
    w_ref, wt_ref, r_ref, rt_ref, qq_ref, wide_ref, small_ref, turned_ref, e_ref, f_ref
):
    cols = qq_ref.shape[2]
    blocks = qq_ref.shape[1] // BLOCK
    place = lax.axis_index("context")
    writes = jnp.concatenate([w_ref[...], wt_ref[...]], axis=0)
    reads = jnp.concatenate([r_ref[...], rt_ref[...]], axis=0)
    turned_ref[0] = writes
    turned_ref[1] = reads
    for lo in range(0, cols, BLOCK):
        here = pl.ds(lo, BLOCK)
        state = jnp.zeros((STATE, BLOCK), F32)
        adjoint = state
        for b in range(blocks):
            at = at_block(b)
            part = slice(b * BLOCK, (b + 1) * BLOCK)
            state += dot(writes[:, part], qq_ref[0, at, here]) * wide_ref[2 + b : 3 + b, here]
            adjoint += dot(reads[:, part], qq_ref[1, at, here]) * wide_ref[b : b + 1, here]
        e_ref[here, :] = jnp.where(place < 2, state, adjoint).astype(BF16)
        f_ref[here, :] = jnp.where(lax.rem(place, 2) == 0, state, adjoint).astype(BF16)
    heads = small_ref.shape[1]
    total = jnp.concatenate(
        [small_ref[5:6], jnp.zeros((1, STATE - heads), F32)], axis=1
    )
    parts = [part.astype(F32) for part in pieces(total, 3)]
    totals = jnp.concatenate(parts + [jnp.zeros((13, STATE), F32)], axis=0).astype(BF16)
    e_ref[pl.ds(cols, 16), :] = totals
    f_ref[pl.ds(cols, 16), :] = totals


def kernel_within(
    x_ref, g_ref, dy_ref, skip_ref, turned_ref, qq_ref, al_ref, be_ref, wide_ref, z_ref, rate_ref,
    small_ref,
    gate_ref, gate_f_ref, in_ref, in_f_ref, dr_ref, dw_ref, keys_ref, p_ref, q_ref, probe_ref,
    local_ref,
    al_e, be_e, skip_e,
):
    rows, cols = x_ref.shape
    heads = skip_ref.shape[1]
    for lo in range(0, cols, TILE):
        wide = expander(heads, lo, TILE)
        here = pl.ds(lo, TILE)
        al_e[:, here] = split_dot_right(al_ref[...], wide, 2)
        be_e[:, here] = split_dot_right(be_ref[...], wide, 2)
        skip_e[:, here] = split_dot_right(jnp.broadcast_to(skip_ref[...], (8, heads)), wide, 3)
    nt = ((1,), (1,))
    wt = [turned_ref[0, :, at_block(b)] for b in range(2)]
    rt = [turned_ref[1, :, at_block(b)] for b in range(2)]
    w = [v.astype(F32).T.astype(BF16) for v in wt]
    r = [v.astype(F32).T.astype(BF16) for v in rt]
    for b in range(2):
        keys_ref[0, at_block(b), :] = w[b]
        keys_ref[1, at_block(b), :] = r[b]
    i = lax.broadcasted_iota(jnp.int32, (BLOCK, BLOCK), 0)
    j = lax.broadcasted_iota(jnp.int32, (BLOCK, BLOCK), 1)
    i00 = jnp.where(i >= j, dot(r[0], wt[0]), 0.0).astype(BF16)
    i11 = jnp.where(i >= j, dot(r[1], wt[1]), 0.0).astype(BF16)
    i10 = dot(r[1], wt[0]).astype(BF16)
    t00 = jnp.where(i <= j, dot(w[0], rt[0]), 0.0).astype(BF16)
    t11 = jnp.where(i <= j, dot(w[1], rt[1]), 0.0).astype(BF16)
    t10 = dot(w[0], rt[1]).astype(BF16)
    m00 = jnp.zeros((BLOCK, BLOCK), F32)
    m11 = m00
    m10 = m00
    p = [jnp.zeros((BLOCK, heads), F32)] * 2
    q = [jnp.zeros((BLOCK, heads), F32)] * 2
    skips = jnp.zeros((8, heads), F32)
    for lo in range(0, cols, BLOCK):
        here = pl.ds(lo, BLOCK)
        sel = selector(heads, lo, BLOCK)
        link = wide_ref[4:5, here]
        xb = [qq_ref[0, at_block(b), here] for b in range(2)]
        ua = [qq_ref[1, at_block(b), here] for b in range(2)]
        m00 += dot(ua[0], xb[0], nt)
        m11 += dot(ua[1], xb[1], nt)
        m10 += dot(ua[1], (xb[0].astype(F32) * link).astype(BF16), nt)
        v = [dot(i00, xb[0]), dot(i11, xb[1]) + link * dot(i10, xb[0])]
        z = [dot(t00, ua[0]) + link * dot(t10, ua[1]), dot(t11, ua[1])]
        skip = skip_e[0:1, here]
        for b in range(2):
            at = at_block(b)
            p[b] += split_dot_right(ua[b].astype(F32) * v[b], sel, 2)
            q[b] += split_dot_right(xb[b].astype(F32) * z[b], sel, 2)
            g = g_ref[at, here].astype(F32)
            dy = dy_ref[at, here].astype(F32)
            x = x_ref[at, here].astype(F32)
            sig = logistic(g)
            u = dy * g * sig
            up = dy * sig * (1.0 + g * (1.0 - sig))
            al = al_e[at, here]
            be = be_e[at, here]
            gate_ref[at, here] = (up * (al * v[b] + skip * x)).astype(BF16)
            gate_f_ref[at, here] = (up * al * wide_ref[b : b + 1, here]).astype(BF16)
            in_ref[at, here] = (be * z[b] + skip * u).astype(BF16)
            in_f_ref[at, here] = (be * wide_ref[2 + b : 3 + b, here]).astype(BF16)
            ux = jnp.sum((u * x).reshape(BLOCK // 8, 8, BLOCK), axis=0)
            skips += split_dot_right(ux, sel, 3)
    z = z_ref[...]
    rate = jnp.exp(rate_ref[...])
    step = softplus(z)
    slope = 1.0 / (1.0 + jnp.exp(-z))
    lower = triangle(rows, True)
    decayed = split_dot_left(lower, -rate * step, 3)
    climbed = rate * split_dot_left(lower, slope, 3)
    direct = slope / step
    decay_end = decayed[rows - 1 : rows]
    climb_end = climbed[rows - 1 : rows]
    weights = [
        [decay_end - decayed, direct + climbed - climb_end],
        [decayed, -climbed],
    ]
    for side in range(2):
        turned = [wt, rt][side]
        for n in range(2):
            parts = pieces(weights[side][n], 2)
            for lo in range(0, cols, TILE):
                here = pl.ds(lo, TILE)
                wide = expander(heads, lo, TILE)
                total = jnp.zeros((STATE, TILE), F32)
                for b in range(2):
                    part = slice(b * BLOCK, (b + 1) * BLOCK)
                    weight = sum(dot(v[part], wide) for v in parts)
                    scaled = qq_ref[side, at_block(b), here].astype(F32) * weight
                    row = (2 if side == 0 else 0) + b
                    total += dot(turned[b], scaled.astype(BF16)) * wide_ref[row : row + 1, here]
                probe_ref[side, n, :, here] = total
    p = jnp.concatenate(p, axis=0)
    q = jnp.concatenate(q, axis=0)
    p_ref[...] = p
    q_ref[...] = q
    local = [
        jnp.sum(v, axis=0, keepdims=True)
        for v in (decayed * (p - q), skips, direct * q - climbed * (p - q))
    ]
    kept = small_ref[5:6]
    local += [decay_end * kept, -climb_end * kept] + [jnp.zeros_like(kept)] * 3
    local_ref[...] = jnp.concatenate(local, axis=0)
    m00 = jnp.where(i >= j, m00, 0.0).astype(BF16)
    m11 = jnp.where(i >= j, m11, 0.0).astype(BF16)
    m10 = m10.astype(BF16)
    dr_ref[:, at_block(0)] = dot(wt[0], m00, nt)
    dr_ref[:, at_block(1)] = dot(wt[0], m10, nt) + dot(wt[1], m11, nt)
    dw_ref[:, at_block(0)] = dot(rt[0], m00) + dot(rt[1], m10)
    dw_ref[:, at_block(1)] = dot(rt[1], m11)


def total_of(ref, cols, heads):
    parts = ref[pl.ds(cols, 16), :].astype(F32)
    return (parts[0:1] + parts[1:2] + parts[2:3])[:, :heads]


def kernel_sums(
    e_ref, f_ref, h_ref, probe_ref, local_ref,
    sums_ref, both_ref, cross_ref,
    coef_e,
):
    cols = both_ref.shape[2]
    heads = local_ref.shape[1]
    place = lax.axis_index("context")
    inner = (place == 1) | (place == 2)
    mine = (place >= 2).astype(jnp.int32)
    te, tf, th = (total_of(ref, cols, heads) for ref in (e_ref, f_ref, h_ref))
    coef = jnp.concatenate(
        [jnp.where(inner, 1.0, tf * th), jnp.where(inner, te, tf)] + [jnp.zeros_like(te)] * 6,
        axis=0,
    )
    coef_parts = pieces(coef, 3)
    for lo in range(0, cols, TILE):
        wide = expander(heads, lo, TILE)
        coef_e[:, pl.ds(lo, TILE)] = sum(dot(part, wide) for part in coef_parts)

    def folded(v):
        return jnp.sum(v.reshape(STATE // 8, 8, BLOCK), axis=0)

    rows, select = [], []
    for lo in range(0, cols, BLOCK):
        here = pl.ds(lo, BLOCK)
        got_f = f_ref[here, :].astype(F32)
        x = (
            e_ref[here, :].astype(F32) * coef_e[0:1, here]
            + h_ref[here, :].astype(F32) * coef_e[1:2, here]
            + jnp.where(inner, 0.0, got_f)
        )
        y = jnp.where(inner, got_f, 0.0)
        both_ref[mine, :, here] = x.astype(BF16)
        both_ref[1 - mine, :, here] = y.astype(BF16)
        products = [
            folded(x * probe_ref[mine, n, :, here] + y * probe_ref[1 - mine, n, :, here])
            for n in range(2)
        ] + [folded(x * y), jnp.zeros((8, BLOCK), F32)]
        for part in pieces(jnp.concatenate(products, axis=0), 2):
            rows.append(part)
            select.append(selector(heads, lo, BLOCK))
    out = dot(jnp.concatenate(rows, axis=1), jnp.concatenate(select, axis=0))
    rate, bias, cross = (
        jnp.sum(out[8 * n : 8 * n + 8], axis=0, keepdims=True) for n in range(3)
    )
    local = local_ref[...]
    rate = rate + local[0:1] + local[3:4] * cross
    bias = bias + local[2:3] + local[4:5] * cross
    index = lax.broadcasted_iota(jnp.int32, (8, heads), 0)
    sums_ref[...] = jnp.where(
        index == 0, rate, jnp.where(index == 1, local[1:2], jnp.where(index == 2, bias, 0.0))
    )
    cross_ref[...] = jnp.broadcast_to(cross, (8, heads))


def kernel_keys(both_ref, qq_ref, wide_ref, dr_ref, dw_ref, keep_ref, send_ref):
    cols = qq_ref.shape[2]
    half = STATE // 2
    nt = ((1,), (1,))
    for b in range(2):
        at = at_block(b)
        dr = dr_ref[:, at]
        dw = dw_ref[:, at]
        for lo in range(0, cols, TILE):
            here = pl.ds(lo, TILE)
            s = (both_ref[1, :, here].astype(F32) * wide_ref[b : b + 1, here]).astype(BF16)
            a = (both_ref[0, :, here].astype(F32) * wide_ref[2 + b : 3 + b, here]).astype(BF16)
            dr += dot(s, qq_ref[1, at, here], nt)
            dw += dot(a, qq_ref[0, at, here], nt)
        keep_ref[pl.ds(0, half), at] = dw[:half]
        keep_ref[pl.ds(half, half), at] = dr[:half]
        send_ref[pl.ds(0, half), at] = dw[half:].astype(BF16)
        send_ref[pl.ds(half, half), at] = dr[half:].astype(BF16)


def kernel_outer(
    both_ref, keys_ref, qq_ref, gate_ref, gate_f_ref, in_ref, in_f_ref,
    cross_ref, p_ref, q_ref, small_ref, z_ref, rate_ref,
    grad_in_out, grad_gate_out, grad_step_out,
    grad_in_ref, grad_gate_ref, step_ref, sems,
):
    rows, cols = gate_ref.shape
    heads = small_ref.shape[1]
    copies = []

    def leave(src, dst):
        copies.append(pltpu.make_async_copy(src, dst, sems.at[len(copies)]))
        copies[-1].start()

    sums = []
    for b in range(2):
        at = at_block(b)
        parts = [[], []]
        select = []
        for lo in range(0, cols, TILE):
            here = pl.ds(lo, TILE)
            v = dot(keys_ref[1, at, :], both_ref[1, :, here])
            z = dot(keys_ref[0, at, :], both_ref[0, :, here])
            grad_gate_ref[at, here] = (
                gate_ref[at, here].astype(F32) + gate_f_ref[at, here].astype(F32) * v
            ).astype(BF16)
            grad_in_ref[at, here] = (
                in_ref[at, here].astype(F32) + in_f_ref[at, here].astype(F32) * z
            ).astype(BF16)
            for side, got in enumerate((z, v)):
                parts[side] += pieces(qq_ref[side, at, here].astype(F32) * got, 2)
            select += [selector(heads, lo, TILE)] * 2
        leave(grad_gate_ref.at[at], grad_gate_out.at[at])
        leave(grad_in_ref.at[at], grad_in_out.at[at])
        select = jnp.concatenate(select, axis=0)
        sums.append([
            dot(jnp.concatenate(parts[side], axis=1), select)
            * small_ref[(2 if side == 0 else 0) + b : (3 if side == 0 else 1) + b]
            for side in range(2)
        ])
    q, p = (jnp.concatenate([sums[b][side] for b in range(2)], axis=0) for side in range(2))
    ends = jnp.sum(q, axis=0, keepdims=True) + small_ref[5:6] * cross_ref[0:1]
    q = q + q_ref[...]
    flow = split_dot_left(triangle(rows, False), p + p_ref[...] - q, 3) + ends
    z = z_ref[...]
    grad = (q / softplus(z) - jnp.exp(rate_ref[...]) * flow) / (1.0 + jnp.exp(-z))
    step_ref[...] = grad.T
    leave(step_ref, grad_step_out)
    for copy in copies:
        copy.wait()


def kernel_add(a_ref, b_ref, c_ref, d_ref, out_ref):
    out_ref[...] = (a_ref[...] + b_ref[...]) + (c_ref[...] + d_ref[...])


def kernel_finish(
    keep_ref, got_ref, a_ref, b_ref, c_ref, d_ref, w_ref, r_ref, rate_ref, skip_ref, bias_ref
):
    half = w_ref.shape[0]
    w_ref[...] = keep_ref[pl.ds(0, half), :] + got_ref[pl.ds(0, half), :].astype(F32)
    r_ref[...] = keep_ref[pl.ds(half, half), :] + got_ref[pl.ds(half, half), :].astype(F32)
    sums = (a_ref[...] + b_ref[...]) + (c_ref[...] + d_ref[...])
    rate_ref[...] = sums[0:1]
    skip_ref[...] = sums[1:2]
    bias_ref[...] = sums[2:3]


V = pltpu.VMEM
ANY = pl.ANY


def call(kernel, outs, args, scratch=(), us=3.0, spaces=None, out_spaces=None, alias=None):
    spaces = spaces or [V] * len(args)
    out_spaces = out_spaces or [V] * len(outs)
    return pl.pallas_call(
        kernel,
        out_shape=[jax.ShapeDtypeStruct(s, d) for s, d in outs],
        in_specs=[pl.BlockSpec(memory_space=s) for s in spaces],
        out_specs=[pl.BlockSpec(memory_space=s) for s in out_spaces],
        scratch_shapes=list(scratch),
        input_output_aliases=alias or {},
        compiler_params=pltpu.CompilerParams(vmem_limit_bytes=36 * 1024 * 1024),
        cost_estimate=pl.CostEstimate(
            flops=int(us * 1e9), bytes_accessed=int(us * 1e6), transcendentals=0
        ),
    )(*args)


def exchange(array, axis, mask):
    count = lax.axis_size(axis)
    pairs = [(i, i ^ mask) for i in range(count) if i ^ mask < count]
    return lax.ppermute(array, axis, pairs)


def body(
    head_inputs,
    gate_inputs,
    step_raw,
    state_write,
    state_read,
    log_rate,
    skip_gain,
    step_bias,
    grad_gated,
):
    x, g, dy = head_inputs[0], gate_inputs[0], grad_gated[0]
    raw = step_raw[0].T
    heads, rows = raw.shape
    cols = x.shape[1]
    half = state_write.shape[2]
    w, r = state_write[0].T, state_read[0].T
    wt, rt = exchange(w, "tensor", 1), exchange(r, "tensor", 1)
    rate, skip, bias = (v.reshape(1, heads) for v in (log_rate, skip_gain, step_bias))
    payload = ((cols + 16, STATE), BF16)
    big = ((rows, cols), BF16)
    pair = ((2, rows, cols), BF16)
    thin = ((rows, heads), F32)
    tiny = ((8, heads), F32)
    one = ((1, heads), F32)
    key = ((half, rows), BF16)
    x, g, dy, w, r, skip, qq, z, rate, al, be, wide, small = call(
        kernel_scale,
        [big, big, big, key, key, one, pair, thin, one, thin, thin, ((8, cols), F32), tiny],
        [
            pltpu.with_memory_space_constraint(v, pltpu.HBM)
            for v in (x, g, dy, raw, bias, rate, skip, w, r)
        ],
        [V((heads, rows), F32), V((1, heads), F32), pltpu.SemaphoreType.DMA((12,))],
        spaces=[pltpu.HBM] * 9,
    )
    turned, send_e, send_f = call(
        kernel_states,
        [((2, STATE, rows), BF16), payload, payload],
        [w, wt, r, rt, qq, wide, small],
    )
    got_e = exchange(send_e, "context", 3)
    got_f = exchange(send_f, "context", 1)
    got_h = exchange(send_e, "context", 2)
    state = ((2, STATE, cols), BF16)
    gate, gate_f, inp, inp_f, dr, dw, keys, p, q, probe, local = call(
        kernel_within,
        [big] * 4 + [((STATE, rows), F32)] * 2
        + [((2, rows, STATE), BF16), thin, thin, ((2, 2, STATE, cols), F32), tiny],
        [x, g, dy, skip, turned, qq, al, be, wide, z, rate, small],
        [V((rows, cols), F32)] * 2 + [V((8, cols), F32)],
        us=4.0,
    )
    sums, both, cross = call(
        kernel_sums, [tiny, state, tiny], [got_e, got_f, got_h, probe, local],
        [V((8, cols), F32)], us=0.5,
    )
    others = [exchange(sums, "context", mask) for mask in (3, 2, 1)]
    keep, send = call(
        kernel_keys, [((STATE, rows), F32), ((STATE, rows), BF16)],
        [both, qq, wide, dr, dw], us=1.0,
    )
    grad_in, grad_gate, grad_step = call(
        kernel_outer, [big, big, ((heads, rows), F32)],
        [both, keys, qq, gate, gate_f, inp, inp_f, cross, p, q, small, z, rate],
        [V((rows, cols), BF16)] * 2 + [V((heads, rows), F32), pltpu.SemaphoreType.DMA((5,))],
        us=2.0, out_spaces=[pltpu.HBM] * 3,
    )
    (sums,) = call(kernel_add, [tiny], [sums] + others, us=0.1)
    got = exchange(send, "tensor", 1)
    others = [exchange(sums, "dp", mask) for mask in (1, 3, 2)]
    grad_w, grad_r, sum_rate, sum_skip, sum_bias = call(
        kernel_finish,
        [((half, rows), F32)] * 2 + [one] * 3,
        [keep, got, sums] + others,
        us=0.2,
    )
    return (
        grad_in[None],
        grad_gate[None],
        grad_w.T[None],
        grad_r.T[None],
        grad_step.T[None],
        sum_rate.reshape(heads),
        sum_skip.reshape(heads),
        sum_bias.reshape(heads),
    )


def solution(mesh):
    wide = P("dp", "context", "tensor")
    head = P("tensor")
    return jax.shard_map(
        body,
        mesh=mesh,
        in_specs=(wide,) * 5 + (head,) * 3 + (wide,),
        out_specs=(wide,) * 5 + (head,) * 3,
        check_vma=False,
    )
```

```python
import functools
import math

import jax
import jax.numpy as jnp
from jax import lax
from jax.experimental import pallas as pl
from jax.experimental.pallas import tpu as pltpu
from jax.sharding import PartitionSpec as P

HEAD_DIM = 64
STATE = 128
BLOCK = 128
LOG2E = math.log2(math.e)
F32 = jnp.float32
BF16 = jnp.bfloat16
TILE = 256


def dot(a, b, dims=((1,), (0,))):
    return lax.dot_general(a, b, (dims, ((), ())), preferred_element_type=F32)


def pieces(v, count):
    out = []
    for _ in range(count):
        part = v.astype(BF16)
        out.append(part)
        v = v - part.astype(F32)
    return out


def split_dot_left(exact, v, count):
    return sum(dot(exact, part) for part in pieces(v, count))


def split_dot_right(v, exact, count):
    return sum(dot(part, exact) for part in pieces(v, count))


def expander(heads, lo, size):
    head = lax.broadcasted_iota(jnp.int32, (heads, size), 0)
    column = lax.broadcasted_iota(jnp.int32, (heads, size), 1) + lo
    return ((column >= head * HEAD_DIM) & (column < (head + 1) * HEAD_DIM)).astype(BF16)


def selector(heads, lo, size):
    head = lax.broadcasted_iota(jnp.int32, (size, heads), 1)
    column = lax.broadcasted_iota(jnp.int32, (size, heads), 0) + lo
    return ((column >= head * HEAD_DIM) & (column < (head + 1) * HEAD_DIM)).astype(BF16)


def triangle(rows, lower):
    i = lax.broadcasted_iota(jnp.int32, (rows, rows), 0)
    j = lax.broadcasted_iota(jnp.int32, (rows, rows), 1)
    return ((i >= j) if lower else (i <= j)).astype(BF16)


def softplus(z):
    return jnp.maximum(z, 0.0) + jnp.log(1.0 + jnp.exp(-jnp.abs(z)))


def logistic(v):
    return 0.5 + 0.5 * jnp.tanh(0.5 * v)


def at_block(b):
    return pl.ds(b * BLOCK, BLOCK)


def kernel_scale(
    x_in, g_in, dy_in, raw_in, bias_in, rate_in, skip_in, w_in, r_in,
    x_ref, g_ref, dy_ref, w_ref, r_ref, skip_ref, qq_ref, z_ref, rate_ref, al_ref, be_ref,
    wide_ref, small_ref,
    raw_ref, bias_ref, sems,
):
    rows, cols = x_ref.shape
    heads = raw_ref.shape[0]
    blocks = rows // BLOCK
    thin = [
        (raw_in, raw_ref), (bias_in, bias_ref), (rate_in, rate_ref),
        (skip_in, skip_ref), (w_in, w_ref), (r_in, r_ref),
    ]
    copies = [pltpu.make_async_copy(s, d, sems.at[i]) for i, (s, d) in enumerate(thin)]
    large = []
    for b in range(blocks):
        large.append([
            pltpu.make_async_copy(s.at[at_block(b)], d.at[at_block(b)], sems.at[6 + 3 * b + i])
            for i, (s, d) in enumerate([(g_in, g_ref), (dy_in, dy_ref), (x_in, x_ref)])
        ])
    for copy in copies[:3] + large[0] + large[1] + copies[3:]:
        copy.start()
    for copy in copies[:3]:
        copy.wait()
    z = raw_ref[...].T + bias_ref[...]
    z_ref[...] = z
    step = softplus(z)
    log2_decay = step * (-LOG2E * jnp.exp(rate_ref[...]))
    run = split_dot_left(triangle(rows, True), log2_decay, 3)
    mid0 = run[BLOCK // 2 - 1 : BLOCK // 2]
    mid1 = run[BLOCK + BLOCK // 2 - 1 : BLOCK + BLOCK // 2]
    end = run[rows - 1 : rows]
    row = lax.broadcasted_iota(jnp.int32, (rows, heads), 0)
    rel = run - jnp.where(row < BLOCK, mid0, mid1)
    for copy in large[0]:
        copy.wait()
    al = jnp.exp2(rel)
    be = jnp.exp2(-rel) * step
    al_ref[...] = al
    be_ref[...] = be
    small = jnp.exp2(
        jnp.concatenate([mid0, mid1, end - mid0, end - mid1, mid1 - mid0, end, end, end], axis=0)
    )
    small_ref[...] = small
    small_parts = pieces(small, 3)
    al_parts = pieces(al, 2)
    be_parts = pieces(be, 2)
    for lo in range(0, cols, TILE):
        wide = expander(heads, lo, TILE)
        wide_ref[:, pl.ds(lo, TILE)] = sum(dot(part, wide) for part in small_parts)
    for b in range(blocks):
        if b:
            for copy in large[b]:
                copy.wait()
        at = at_block(b)
        part = slice(b * BLOCK, (b + 1) * BLOCK)
        for lo in range(0, cols, TILE):
            here = pl.ds(lo, TILE)
            wide = expander(heads, lo, TILE)
            al_tile = sum(dot(v[part], wide) for v in al_parts)
            be_tile = sum(dot(v[part], wide) for v in be_parts)
            g = g_ref[at, here].astype(F32)
            u = dy_ref[at, here].astype(F32) * g * logistic(g)
            qq_ref[1, at, here] = (u * al_tile).astype(BF16)
            qq_ref[0, at, here] = (x_ref[at, here].astype(F32) * be_tile).astype(BF16)
    for copy in copies[3:]:
        copy.wait()


def kernel_states(
    w_ref, wt_ref, r_ref, rt_ref, qq_ref, wide_ref, small_ref,
    turned_ref, up_ref, down_ref, h_ref,
):
    cols = qq_ref.shape[2]
    blocks = qq_ref.shape[1] // BLOCK
    place = lax.axis_index("context")
    writes = jnp.concatenate([w_ref[...], wt_ref[...]], axis=0)
    reads = jnp.concatenate([r_ref[...], rt_ref[...]], axis=0)
    turned_ref[0] = writes
    turned_ref[1] = reads
    for lo in range(0, cols, BLOCK):
        here = pl.ds(lo, BLOCK)
        state = jnp.zeros((STATE, BLOCK), F32)
        adjoint = state
        for b in range(blocks):
            at = at_block(b)
            part = slice(b * BLOCK, (b + 1) * BLOCK)
            state += dot(writes[:, part], qq_ref[0, at, here]) * wide_ref[2 + b : 3 + b, here]
            adjoint += dot(reads[:, part], qq_ref[1, at, here]) * wide_ref[b : b + 1, here]
        state = state.astype(BF16)
        adjoint = adjoint.astype(BF16)
        up_ref[here, :] = jnp.where(place < 3, state, adjoint)
        down_ref[here, :] = jnp.where(place < 1, state, adjoint)
        h_ref[here, :] = jnp.where(place < 2, state, adjoint)
    heads = small_ref.shape[1]
    total = jnp.concatenate(
        [small_ref[5:6], jnp.zeros((1, STATE - heads), F32)], axis=1
    )
    parts = [part.astype(F32) for part in pieces(total, 3)]
    totals = jnp.concatenate(parts + [jnp.zeros((13, STATE), F32)], axis=0).astype(BF16)
    for ref in (up_ref, down_ref, h_ref):
        ref[pl.ds(cols, 16), :] = totals


def kernel_within(
    x_ref, g_ref, dy_ref, skip_ref, turned_ref, qq_ref, al_ref, be_ref, wide_ref, z_ref, rate_ref,
    small_ref,
    gate_ref, gate_f_ref, in_ref, in_f_ref, dr_ref, dw_ref, keys_ref, p_ref, q_ref, probe_ref,
    local_ref,
    spread_ref,
):
    rows, cols = x_ref.shape
    heads = skip_ref.shape[1]
    z = z_ref[...]
    rate = jnp.exp(rate_ref[...])
    step = softplus(z)
    slope = 1.0 / (1.0 + jnp.exp(-z))
    lower = triangle(rows, True)
    decayed = split_dot_left(lower, -rate * step, 3)
    climbed = rate * split_dot_left(lower, slope, 3)
    direct = slope / step
    decay_end = decayed[rows - 1 : rows]
    climb_end = climbed[rows - 1 : rows]
    thin = jnp.concatenate(
        [
            al_ref[...], be_ref[...],
            decay_end - decayed, direct + climbed - climb_end, decayed, -climbed,
            jnp.broadcast_to(skip_ref[...], (8, heads)),
        ],
        axis=0,
    )
    thin = jnp.concatenate(pieces(thin, 2), axis=1)
    nt = ((1,), (1,))
    wt = [turned_ref[0, :, at_block(b)] for b in range(2)]
    rt = [turned_ref[1, :, at_block(b)] for b in range(2)]
    w = [v.astype(F32).T.astype(BF16) for v in wt]
    r = [v.astype(F32).T.astype(BF16) for v in rt]
    for b in range(2):
        keys_ref[0, at_block(b), :] = w[b]
        keys_ref[1, at_block(b), :] = r[b]
    i = lax.broadcasted_iota(jnp.int32, (BLOCK, BLOCK), 0)
    j = lax.broadcasted_iota(jnp.int32, (BLOCK, BLOCK), 1)
    i00 = jnp.where(i >= j, dot(r[0], wt[0]), 0.0).astype(BF16)
    i11 = jnp.where(i >= j, dot(r[1], wt[1]), 0.0).astype(BF16)
    i10 = dot(r[1], wt[0]).astype(BF16)
    t00 = jnp.where(i <= j, dot(w[0], rt[0]), 0.0).astype(BF16)
    t11 = jnp.where(i <= j, dot(w[1], rt[1]), 0.0).astype(BF16)
    t10 = dot(w[0], rt[1]).astype(BF16)
    m00 = jnp.zeros((BLOCK, BLOCK), F32)
    m11 = m00
    m10 = m00
    p_parts, q_parts = [[], []], [[], []]
    skip_parts, selects, skip_selects = [], [], []
    for lo in range(0, cols, TILE):
        here = pl.ds(lo, TILE)
        wide = expander(heads, lo, TILE)
        spread_ref[...] = dot(thin, jnp.concatenate([wide, wide], axis=0))
        sel = selector(heads, lo, TILE)
        selects += [sel] * 2
        skip_selects += [sel] * 3
        link = wide_ref[4:5, here]
        xb = [qq_ref[0, at_block(b), here] for b in range(2)]
        ua = [qq_ref[1, at_block(b), here] for b in range(2)]
        m00 += dot(ua[0], xb[0], nt)
        m11 += dot(ua[1], xb[1], nt)
        m10 += dot(ua[1], (xb[0].astype(F32) * link).astype(BF16), nt)
        v = [dot(i00, xb[0]), dot(i11, xb[1]) + link * dot(i10, xb[0])]
        z = [dot(t00, ua[0]) + link * dot(t10, ua[1]), dot(t11, ua[1])]
        skip = spread_ref[6 * rows : 6 * rows + 1, :]
        totals = [[0.0, 0.0], [0.0, 0.0]]
        products = 0.0
        for b in range(2):
            at = at_block(b)
            xf, uf = xb[b].astype(F32), ua[b].astype(F32)
            p_parts[b] += pieces(uf * v[b], 2)
            q_parts[b] += pieces(xf * z[b], 2)
            g = g_ref[at, here].astype(F32)
            dy = dy_ref[at, here].astype(F32)
            x = x_ref[at, here].astype(F32)
            sig = logistic(g)
            u = dy * g * sig
            up = dy * sig * (1.0 + g * (1.0 - sig))
            al = spread_ref[pl.ds(b * BLOCK, BLOCK), :]
            be = spread_ref[pl.ds(rows + b * BLOCK, BLOCK), :]
            gate_ref[at, here] = (up * (al * v[b] + skip * x)).astype(BF16)
            gate_f_ref[at, here] = (up * al * wide_ref[b : b + 1, here]).astype(BF16)
            in_ref[at, here] = (be * z[b] + skip * u).astype(BF16)
            in_f_ref[at, here] = (be * wide_ref[2 + b : 3 + b, here]).astype(BF16)
            products += jnp.sum((u * x).reshape(BLOCK // 8, 8, TILE), axis=0)
            for side, (turned, own) in enumerate(((wt[b], xf), (rt[b], uf))):
                row = (2 if side == 0 else 0) + b
                for n in range(2):
                    weight = spread_ref[pl.ds((2 + 2 * side + n) * rows + b * BLOCK, BLOCK), :]
                    totals[side][n] += (
                        dot(turned, (own * weight).astype(BF16)) * wide_ref[row : row + 1, here]
                    )
        for side in range(2):
            for n in range(2):
                probe_ref[side, n, :, here] = totals[side][n]
        skip_parts += pieces(products, 3)
    selects = jnp.concatenate(selects, axis=0)
    p, q = (
        jnp.concatenate([dot(jnp.concatenate(v, axis=1), selects) for v in parts], axis=0)
        for parts in (p_parts, q_parts)
    )
    skips = dot(jnp.concatenate(skip_parts, axis=1), jnp.concatenate(skip_selects, axis=0))
    p_ref[...] = p
    q_ref[...] = q
    local = [
        jnp.sum(v, axis=0, keepdims=True)
        for v in (decayed * (p - q), skips, direct * q - climbed * (p - q))
    ]
    kept = small_ref[5:6]
    local += [decay_end * kept, -climb_end * kept] + [jnp.zeros_like(kept)] * 3
    local_ref[...] = jnp.concatenate(local, axis=0)
    m00 = jnp.where(i >= j, m00, 0.0).astype(BF16)
    m11 = jnp.where(i >= j, m11, 0.0).astype(BF16)
    m10 = m10.astype(BF16)
    dr_ref[:, at_block(0)] = dot(wt[0], m00, nt)
    dr_ref[:, at_block(1)] = dot(wt[0], m10, nt) + dot(wt[1], m11, nt)
    dw_ref[:, at_block(0)] = dot(rt[0], m00) + dot(rt[1], m10)
    dw_ref[:, at_block(1)] = dot(rt[1], m11)


def total_of(ref, cols, heads):
    parts = ref[pl.ds(cols, 16), :].astype(F32)
    return (parts[0:1] + parts[1:2] + parts[2:3])[:, :heads]


def kernel_sums(
    up_ref, down_ref, h_ref, probe_ref, local_ref,
    sums_ref, both_ref, cross_ref,
    coef_e,
):
    cols = both_ref.shape[2]
    heads = local_ref.shape[1]
    place = lax.axis_index("context")
    inner = (place == 1) | (place == 2)
    mine = (place >= 2).astype(jnp.int32)
    even = lax.rem(place, 2) == 0
    t_up, t_down, th = (total_of(ref, cols, heads) for ref in (up_ref, down_ref, h_ref))
    te, tf = jnp.where(even, t_up, t_down), jnp.where(even, t_down, t_up)
    coef = jnp.concatenate(
        [jnp.where(inner, 1.0, tf * th), jnp.where(inner, te, tf)] + [jnp.zeros_like(te)] * 6,
        axis=0,
    )
    coef_parts = pieces(coef, 3)
    for lo in range(0, cols, TILE):
        wide = expander(heads, lo, TILE)
        coef_e[:, pl.ds(lo, TILE)] = sum(dot(part, wide) for part in coef_parts)

    def folded(v):
        return jnp.sum(v.reshape(STATE // 8, 8, BLOCK), axis=0)

    rows, select = [], []
    for lo in range(0, cols, BLOCK):
        here = pl.ds(lo, BLOCK)
        up, down = up_ref[here, :].astype(F32), down_ref[here, :].astype(F32)
        got_f = jnp.where(even, down, up)
        x = (
            jnp.where(even, up, down) * coef_e[0:1, here]
            + h_ref[here, :].astype(F32) * coef_e[1:2, here]
            + jnp.where(inner, 0.0, got_f)
        )
        y = jnp.where(inner, got_f, 0.0)
        both_ref[mine, :, here] = x.astype(BF16)
        both_ref[1 - mine, :, here] = y.astype(BF16)
        products = [
            folded(x * probe_ref[mine, n, :, here] + y * probe_ref[1 - mine, n, :, here])
            for n in range(2)
        ] + [folded(x * y), jnp.zeros((8, BLOCK), F32)]
        for part in pieces(jnp.concatenate(products, axis=0), 2):
            rows.append(part)
            select.append(selector(heads, lo, BLOCK))
    out = dot(jnp.concatenate(rows, axis=1), jnp.concatenate(select, axis=0))
    rate, bias, cross = (
        jnp.sum(out[8 * n : 8 * n + 8], axis=0, keepdims=True) for n in range(3)
    )
    local = local_ref[...]
    rate = rate + local[0:1] + local[3:4] * cross
    bias = bias + local[2:3] + local[4:5] * cross
    index = lax.broadcasted_iota(jnp.int32, (8, heads), 0)
    sums_ref[...] = jnp.where(
        index == 0, rate, jnp.where(index == 1, local[1:2], jnp.where(index == 2, bias, 0.0))
    )
    cross_ref[...] = jnp.broadcast_to(cross, (8, heads))


def kernel_keys(both_ref, qq_ref, wide_ref, dr_ref, dw_ref, keep_ref, send_ref):
    cols = qq_ref.shape[2]
    half = STATE // 2
    nt = ((1,), (1,))
    for b in range(2):
        at = at_block(b)
        dr = dr_ref[:, at]
        dw = dw_ref[:, at]
        for lo in range(0, cols, TILE):
            here = pl.ds(lo, TILE)
            s = (both_ref[1, :, here].astype(F32) * wide_ref[b : b + 1, here]).astype(BF16)
            a = (both_ref[0, :, here].astype(F32) * wide_ref[2 + b : 3 + b, here]).astype(BF16)
            dr += dot(s, qq_ref[1, at, here], nt)
            dw += dot(a, qq_ref[0, at, here], nt)
        keep_ref[pl.ds(0, half), at] = dw[:half]
        keep_ref[pl.ds(half, half), at] = dr[:half]
        send_ref[pl.ds(0, half), at] = dw[half:].astype(BF16)
        send_ref[pl.ds(half, half), at] = dr[half:].astype(BF16)


def kernel_outer(
    both_ref, keys_ref, qq_ref, gate_ref, gate_f_ref, in_ref, in_f_ref,
    cross_ref, p_ref, q_ref, small_ref, z_ref, rate_ref,
    grad_in_out, grad_gate_out, grad_step_out,
    grad_in_ref, grad_gate_ref, step_ref, sems,
):
    rows, cols = gate_ref.shape
    heads = small_ref.shape[1]
    copies = []

    def leave(src, dst):
        copies.append(pltpu.make_async_copy(src, dst, sems.at[len(copies)]))
        copies[-1].start()

    sums = []
    for b in range(2):
        at = at_block(b)
        parts = [[], []]
        select = []
        for lo in range(0, cols, TILE):
            here = pl.ds(lo, TILE)
            v = dot(keys_ref[1, at, :], both_ref[1, :, here])
            z = dot(keys_ref[0, at, :], both_ref[0, :, here])
            grad_gate_ref[at, here] = (
                gate_ref[at, here].astype(F32) + gate_f_ref[at, here].astype(F32) * v
            ).astype(BF16)
            grad_in_ref[at, here] = (
                in_ref[at, here].astype(F32) + in_f_ref[at, here].astype(F32) * z
            ).astype(BF16)
            for side, got in enumerate((z, v)):
                parts[side] += pieces(qq_ref[side, at, here].astype(F32) * got, 2)
            select += [selector(heads, lo, TILE)] * 2
        leave(grad_gate_ref.at[at], grad_gate_out.at[at])
        leave(grad_in_ref.at[at], grad_in_out.at[at])
        select = jnp.concatenate(select, axis=0)
        sums.append([
            dot(jnp.concatenate(parts[side], axis=1), select)
            * small_ref[(2 if side == 0 else 0) + b : (3 if side == 0 else 1) + b]
            for side in range(2)
        ])
    q, p = (jnp.concatenate([sums[b][side] for b in range(2)], axis=0) for side in range(2))
    ends = jnp.sum(q, axis=0, keepdims=True) + small_ref[5:6] * cross_ref[0:1]
    q = q + q_ref[...]
    flow = split_dot_left(triangle(rows, False), p + p_ref[...] - q, 3) + ends
    z = z_ref[...]
    grad = (q / softplus(z) - jnp.exp(rate_ref[...]) * flow) / (1.0 + jnp.exp(-z))
    step_ref[...] = grad.T
    leave(step_ref, grad_step_out)
    for copy in copies:
        copy.wait()


def kernel_add(a_ref, b_ref, c_ref, d_ref, out_ref):
    out_ref[...] = (a_ref[...] + b_ref[...]) + (c_ref[...] + d_ref[...])


def kernel_finish(
    keep_ref, got_ref, a_ref, b_ref, c_ref, d_ref, w_ref, r_ref, rate_ref, skip_ref, bias_ref
):
    half = w_ref.shape[0]
    w_ref[...] = keep_ref[pl.ds(0, half), :] + got_ref[pl.ds(0, half), :].astype(F32)
    r_ref[...] = keep_ref[pl.ds(half, half), :] + got_ref[pl.ds(half, half), :].astype(F32)
    sums = (a_ref[...] + b_ref[...]) + (c_ref[...] + d_ref[...])
    rate_ref[...] = sums[0:1]
    skip_ref[...] = sums[1:2]
    bias_ref[...] = sums[2:3]


V = pltpu.VMEM
ANY = pl.ANY


def call(kernel, outs, args, scratch=(), us=3.0, spaces=None, out_spaces=None, alias=None):
    spaces = spaces or [V] * len(args)
    out_spaces = out_spaces or [V] * len(outs)
    return pl.pallas_call(
        kernel,
        out_shape=[jax.ShapeDtypeStruct(s, d) for s, d in outs],
        in_specs=[pl.BlockSpec(memory_space=s) for s in spaces],
        out_specs=[pl.BlockSpec(memory_space=s) for s in out_spaces],
        scratch_shapes=list(scratch),
        input_output_aliases=alias or {},
        compiler_params=pltpu.CompilerParams(vmem_limit_bytes=36 * 1024 * 1024),
        cost_estimate=pl.CostEstimate(
            flops=int(us * 1e9), bytes_accessed=int(us * 1e6), transcendentals=0
        ),
    )(*args)


def exchange(array, axis, mask):
    count = lax.axis_size(axis)
    pairs = [(i, i ^ mask) for i in range(count) if i ^ mask < count]
    return lax.ppermute(array, axis, pairs)


def cycle(array, axis, by):
    count = lax.axis_size(axis)
    return lax.ppermute(array, axis, [(i, (i + by) % count) for i in range(count)])


def body(
    head_inputs,
    gate_inputs,
    step_raw,
    state_write,
    state_read,
    log_rate,
    skip_gain,
    step_bias,
    grad_gated,
):
    x, g, dy = head_inputs[0], gate_inputs[0], grad_gated[0]
    raw = step_raw[0].T
    heads, rows = raw.shape
    cols = x.shape[1]
    half = state_write.shape[2]
    w, r = state_write[0].T, state_read[0].T
    wt, rt = exchange(w, "tensor", 1), exchange(r, "tensor", 1)
    rate, skip, bias = (v.reshape(1, heads) for v in (log_rate, skip_gain, step_bias))
    payload = ((cols + 16, STATE), BF16)
    big = ((rows, cols), BF16)
    pair = ((2, rows, cols), BF16)
    thin = ((rows, heads), F32)
    tiny = ((8, heads), F32)
    one = ((1, heads), F32)
    key = ((half, rows), BF16)
    x, g, dy, w, r, skip, qq, z, rate, al, be, wide, small = call(
        kernel_scale,
        [big, big, big, key, key, one, pair, thin, one, thin, thin, ((8, cols), F32), tiny],
        [
            pltpu.with_memory_space_constraint(v, pltpu.HBM)
            for v in (x, g, dy, raw, bias, rate, skip, w, r)
        ],
        [V((heads, rows), F32), V((1, heads), F32), pltpu.SemaphoreType.DMA((12,))],
        spaces=[pltpu.HBM] * 9,
    )
    turned, send_up, send_down, send_h = call(
        kernel_states,
        [((2, STATE, rows), BF16), payload, payload, payload],
        [w, wt, r, rt, qq, wide, small],
    )
    got_up, got_down = cycle(send_up, "context", 1), cycle(send_down, "context", -1)
    got_h = exchange(send_h, "context", 2)
    state = ((2, STATE, cols), BF16)
    gate, gate_f, inp, inp_f, dr, dw, keys, p, q, probe, local = call(
        kernel_within,
        [big] * 4 + [((STATE, rows), F32)] * 2
        + [((2, rows, STATE), BF16), thin, thin, ((2, 2, STATE, cols), F32), tiny],
        [x, g, dy, skip, turned, qq, al, be, wide, z, rate, small],
        [V((6 * rows + 8, TILE), F32)],
        us=4.0,
    )
    sums, both, cross = call(
        kernel_sums, [tiny, state, tiny], [got_up, got_down, got_h, probe, local],
        [V((8, cols), F32)], us=0.5,
    )
    others = [exchange(sums, "context", mask) for mask in (1, 2, 3)]
    keep, send = call(
        kernel_keys, [((STATE, rows), F32), ((STATE, rows), BF16)],
        [both, qq, wide, dr, dw], us=1.0,
    )
    grad_in, grad_gate, grad_step = call(
        kernel_outer, [big, big, ((heads, rows), F32)],
        [both, keys, qq, gate, gate_f, inp, inp_f, cross, p, q, small, z, rate],
        [V((rows, cols), BF16)] * 2 + [V((heads, rows), F32), pltpu.SemaphoreType.DMA((5,))],
        us=2.0, out_spaces=[pltpu.HBM] * 3,
    )
    (sums,) = call(kernel_add, [tiny], [sums] + others, us=0.1)
    got = exchange(send, "tensor", 1)
    others = [exchange(sums, "dp", mask) for mask in (1, 2, 3)]
    grad_w, grad_r, sum_rate, sum_skip, sum_bias = call(
        kernel_finish,
        [((half, rows), F32)] * 2 + [one] * 3,
        [keep, got, sums] + others,
        us=0.2,
    )
    return (
        grad_in[None],
        grad_gate[None],
        grad_w.T[None],
        grad_r.T[None],
        grad_step.T[None],
        sum_rate.reshape(heads),
        sum_skip.reshape(heads),
        sum_bias.reshape(heads),
    )


def solution(mesh):
    wide = P("dp", "context", "tensor")
    head = P("tensor")
    return jax.shard_map(
        body,
        mesh=mesh,
        in_specs=(wide,) * 5 + (head,) * 3 + (wide,),
        out_specs=(wide,) * 5 + (head,) * 3,
        check_vma=False,
    )
```

```python
import functools
import math

import jax
import jax.numpy as jnp
from jax import lax
from jax.experimental import pallas as pl
from jax.experimental.pallas import tpu as pltpu
from jax.sharding import PartitionSpec as P

HEAD_DIM = 64
STATE = 128
BLOCK = 128
LOG2E = math.log2(math.e)
F32 = jnp.float32
BF16 = jnp.bfloat16
TILE = 256


def dot(a, b, dims=((1,), (0,))):
    return lax.dot_general(a, b, (dims, ((), ())), preferred_element_type=F32)


def pieces(v, count):
    out = []
    for _ in range(count):
        part = v.astype(BF16)
        out.append(part)
        v = v - part.astype(F32)
    return out


def split_dot_left(exact, v, count):
    return sum(dot(exact, part) for part in pieces(v, count))


def split_dot_right(v, exact, count):
    return sum(dot(part, exact) for part in pieces(v, count))


def expander(heads, lo, size):
    head = lax.broadcasted_iota(jnp.int32, (heads, size), 0)
    column = lax.broadcasted_iota(jnp.int32, (heads, size), 1) + lo
    return ((column >= head * HEAD_DIM) & (column < (head + 1) * HEAD_DIM)).astype(BF16)


def selector(heads, lo, size):
    head = lax.broadcasted_iota(jnp.int32, (size, heads), 1)
    column = lax.broadcasted_iota(jnp.int32, (size, heads), 0) + lo
    return ((column >= head * HEAD_DIM) & (column < (head + 1) * HEAD_DIM)).astype(BF16)


def triangle(rows, lower):
    i = lax.broadcasted_iota(jnp.int32, (rows, rows), 0)
    j = lax.broadcasted_iota(jnp.int32, (rows, rows), 1)
    return ((i >= j) if lower else (i <= j)).astype(BF16)


def softplus(z):
    return jnp.maximum(z, 0.0) + jnp.log(1.0 + jnp.exp(-jnp.abs(z)))


def logistic(v):
    return 0.5 + 0.5 * jnp.tanh(0.5 * v)


def at_block(b):
    return pl.ds(b * BLOCK, BLOCK)


def kernel_scale(
    x_in, g_in, dy_in, raw_in, bias_in, rate_in, skip_in, w_in, r_in,
    x_ref, g_ref, dy_ref, w_ref, r_ref, skip_ref, qq_ref, z_ref, rate_ref, al_ref, be_ref,
    wide_ref, small_ref,
    raw_ref, bias_ref, sems,
):
    rows, cols = x_ref.shape
    heads = raw_ref.shape[0]
    blocks = rows // BLOCK
    thin = [
        (raw_in, raw_ref), (bias_in, bias_ref), (rate_in, rate_ref),
        (skip_in, skip_ref), (w_in, w_ref), (r_in, r_ref),
    ]
    copies = [pltpu.make_async_copy(s, d, sems.at[i]) for i, (s, d) in enumerate(thin)]
    large = []
    for b in range(blocks):
        large.append([
            pltpu.make_async_copy(s.at[at_block(b)], d.at[at_block(b)], sems.at[6 + 3 * b + i])
            for i, (s, d) in enumerate([(g_in, g_ref), (dy_in, dy_ref), (x_in, x_ref)])
        ])
    for copy in copies[:3] + large[0] + large[1] + copies[3:]:
        copy.start()
    for copy in copies[:3]:
        copy.wait()
    z = raw_ref[...].T + bias_ref[...]
    z_ref[...] = z
    step = softplus(z)
    log2_decay = step * (-LOG2E * jnp.exp(rate_ref[...]))
    run = split_dot_left(triangle(rows, True), log2_decay, 3)
    mid0 = run[BLOCK // 2 - 1 : BLOCK // 2]
    mid1 = run[BLOCK + BLOCK // 2 - 1 : BLOCK + BLOCK // 2]
    end = run[rows - 1 : rows]
    row = lax.broadcasted_iota(jnp.int32, (rows, heads), 0)
    rel = run - jnp.where(row < BLOCK, mid0, mid1)
    for copy in large[0]:
        copy.wait()
    al = jnp.exp2(rel)
    be = jnp.exp2(-rel) * step
    al_ref[...] = al
    be_ref[...] = be
    small = jnp.exp2(
        jnp.concatenate([mid0, mid1, end - mid0, end - mid1, mid1 - mid0, end, end, end], axis=0)
    )
    small_ref[...] = small
    small_parts = pieces(small, 3)
    halves = [
        jnp.concatenate(
            pieces(jnp.concatenate([v[b * BLOCK : (b + 1) * BLOCK] for v in (al, be)], axis=0), 2),
            axis=1,
        )
        for b in range(blocks)
    ]
    for lo in range(0, cols, TILE):
        wide = expander(heads, lo, TILE)
        wide_ref[:, pl.ds(lo, TILE)] = sum(dot(part, wide) for part in small_parts)
    for b in range(blocks):
        if b:
            for copy in large[b]:
                copy.wait()
        at = at_block(b)
        for lo in range(0, cols, TILE):
            here = pl.ds(lo, TILE)
            wide = expander(heads, lo, TILE)
            spread = dot(halves[b], jnp.concatenate([wide, wide], axis=0))
            al_tile, be_tile = spread[:BLOCK], spread[BLOCK:]
            g = g_ref[at, here].astype(F32)
            u = dy_ref[at, here].astype(F32) * g * logistic(g)
            qq_ref[1, at, here] = (u * al_tile).astype(BF16)
            qq_ref[0, at, here] = (x_ref[at, here].astype(F32) * be_tile).astype(BF16)
    for copy in copies[3:]:
        copy.wait()


def kernel_states(
    w_ref, wt_ref, r_ref, rt_ref, qq_ref, wide_ref,
    turned_ref, up_ref, down_ref, h_ref,
):
    cols = qq_ref.shape[2]
    blocks = qq_ref.shape[1] // BLOCK
    place = lax.axis_index("context")
    writes = jnp.concatenate([w_ref[...], wt_ref[...]], axis=0)
    reads = jnp.concatenate([r_ref[...], rt_ref[...]], axis=0)
    turned_ref[0] = writes
    turned_ref[1] = reads
    for lo in range(0, cols, TILE):
        here = pl.ds(lo, TILE)
        state = jnp.zeros((STATE, TILE), F32)
        adjoint = state
        for b in range(blocks):
            at = at_block(b)
            part = slice(b * BLOCK, (b + 1) * BLOCK)
            state += dot(writes[:, part], qq_ref[0, at, here]) * wide_ref[2 + b : 3 + b, here]
            adjoint += dot(reads[:, part], qq_ref[1, at, here]) * wide_ref[b : b + 1, here]
        state = state.astype(BF16)
        adjoint = adjoint.astype(BF16)
        up = jnp.where(place < 3, state, adjoint)
        down = jnp.where(place < 1, state, adjoint)
        mid = jnp.where(place < 2, state, adjoint)
        for k in range(0, TILE, BLOCK):
            there = pl.ds(lo + k, BLOCK)
            up_ref[there, :] = up[:, k : k + BLOCK]
            down_ref[there, :] = down[:, k : k + BLOCK]
            h_ref[there, :] = mid[:, k : k + BLOCK]
    total = jnp.concatenate(
        [wide_ref[5:6, pl.ds(lo, BLOCK)] for lo in range(0, cols, BLOCK)], axis=0
    )
    totals = jnp.concatenate([part.astype(F32) for part in pieces(total, 2)], axis=0).astype(BF16)
    for ref in (up_ref, down_ref, h_ref):
        ref[pl.ds(cols, 16), :] = totals


def kernel_within(
    x_ref, g_ref, dy_ref, skip_ref, turned_ref, qq_ref, al_ref, be_ref, wide_ref, z_ref, rate_ref,
    small_ref,
    gate_ref, gate_f_ref, in_ref, in_f_ref, dr_ref, dw_ref, keys_ref, p_ref, q_ref, probe_ref,
    local_ref,
    spread_ref,
):
    rows, cols = x_ref.shape
    heads = skip_ref.shape[1]
    z = z_ref[...]
    rate = jnp.exp(rate_ref[...])
    step = softplus(z)
    slope = 1.0 / (1.0 + jnp.exp(-z))
    lower = triangle(rows, True)
    decayed = split_dot_left(lower, -rate * step, 3)
    climbed = rate * split_dot_left(lower, slope, 3)
    direct = slope / step
    decay_end = decayed[rows - 1 : rows]
    climb_end = climbed[rows - 1 : rows]
    thin = jnp.concatenate(
        [
            al_ref[...], be_ref[...],
            decay_end - decayed, direct + climbed - climb_end, decayed, -climbed,
            jnp.broadcast_to(skip_ref[...], (8, heads)),
        ],
        axis=0,
    )
    thin = jnp.concatenate(pieces(thin, 2), axis=1)
    nt = ((1,), (1,))
    wt = [turned_ref[0, :, at_block(b)] for b in range(2)]
    rt = [turned_ref[1, :, at_block(b)] for b in range(2)]
    w = [v.astype(F32).T.astype(BF16) for v in wt]
    r = [v.astype(F32).T.astype(BF16) for v in rt]
    for b in range(2):
        keys_ref[0, at_block(b), :] = w[b]
        keys_ref[1, at_block(b), :] = r[b]
    i = lax.broadcasted_iota(jnp.int32, (BLOCK, BLOCK), 0)
    j = lax.broadcasted_iota(jnp.int32, (BLOCK, BLOCK), 1)
    i00 = jnp.where(i >= j, dot(r[0], wt[0]), 0.0).astype(BF16)
    i11 = jnp.where(i >= j, dot(r[1], wt[1]), 0.0).astype(BF16)
    i10 = dot(r[1], wt[0]).astype(BF16)
    t00 = jnp.where(i <= j, dot(w[0], rt[0]), 0.0).astype(BF16)
    t11 = jnp.where(i <= j, dot(w[1], rt[1]), 0.0).astype(BF16)
    t10 = dot(w[0], rt[1]).astype(BF16)
    m00 = jnp.zeros((BLOCK, BLOCK), F32)
    m11 = m00
    m10 = m00
    p_parts, q_parts = [[], []], [[], []]
    skip_parts, selects, skip_selects = [], [], []
    for lo in range(0, cols, TILE):
        here = pl.ds(lo, TILE)
        wide = expander(heads, lo, TILE)
        spread_ref[...] = dot(thin, jnp.concatenate([wide, wide], axis=0))
        sel = selector(heads, lo, TILE)
        selects += [sel] * 2
        skip_selects += [sel] * 3
        link = wide_ref[4:5, here]
        xb = [qq_ref[0, at_block(b), here] for b in range(2)]
        ua = [qq_ref[1, at_block(b), here] for b in range(2)]
        m00 += dot(ua[0], xb[0], nt)
        m11 += dot(ua[1], xb[1], nt)
        m10 += dot(ua[1], (xb[0].astype(F32) * link).astype(BF16), nt)
        v = [dot(i00, xb[0]), dot(i11, xb[1]) + link * dot(i10, xb[0])]
        z = [dot(t00, ua[0]) + link * dot(t10, ua[1]), dot(t11, ua[1])]
        skip = spread_ref[6 * rows : 6 * rows + 1, :]
        totals = [[0.0, 0.0], [0.0, 0.0]]
        products = 0.0
        for b in range(2):
            at = at_block(b)
            xf, uf = xb[b].astype(F32), ua[b].astype(F32)
            p_parts[b] += pieces(uf * v[b], 2)
            q_parts[b] += pieces(xf * z[b], 2)
            g = g_ref[at, here].astype(F32)
            dy = dy_ref[at, here].astype(F32)
            x = x_ref[at, here].astype(F32)
            sig = logistic(g)
            u = dy * g * sig
            up = dy * sig * (1.0 + g * (1.0 - sig))
            al = spread_ref[pl.ds(b * BLOCK, BLOCK), :]
            be = spread_ref[pl.ds(rows + b * BLOCK, BLOCK), :]
            gate_ref[at, here] = (up * (al * v[b] + skip * x)).astype(BF16)
            gate_f_ref[at, here] = (up * al * wide_ref[b : b + 1, here]).astype(BF16)
            in_ref[at, here] = (be * z[b] + skip * u).astype(BF16)
            in_f_ref[at, here] = (be * wide_ref[2 + b : 3 + b, here]).astype(BF16)
            products += jnp.sum((u * x).reshape(BLOCK // 8, 8, TILE), axis=0)
            for side, (turned, own) in enumerate(((wt[b], xf), (rt[b], uf))):
                row = (2 if side == 0 else 0) + b
                for n in range(2):
                    weight = spread_ref[pl.ds((2 + 2 * side + n) * rows + b * BLOCK, BLOCK), :]
                    totals[side][n] += (
                        dot(turned, (own * weight).astype(BF16)) * wide_ref[row : row + 1, here]
                    )
        for side in range(2):
            for n in range(2):
                probe_ref[side, n, :, here] = totals[side][n]
        skip_parts += pieces(products, 3)
    selects = jnp.concatenate(selects, axis=0)
    p, q = (
        jnp.concatenate([dot(jnp.concatenate(v, axis=1), selects) for v in parts], axis=0)
        for parts in (p_parts, q_parts)
    )
    skips = dot(jnp.concatenate(skip_parts, axis=1), jnp.concatenate(skip_selects, axis=0))
    p_ref[...] = p
    q_ref[...] = q
    local = [
        jnp.sum(v, axis=0, keepdims=True)
        for v in (decayed * (p - q), skips, direct * q - climbed * (p - q))
    ]
    kept = small_ref[5:6]
    local += [decay_end * kept, -climb_end * kept] + [jnp.zeros_like(kept)] * 3
    local_ref[...] = jnp.concatenate(local, axis=0)
    m00 = jnp.where(i >= j, m00, 0.0).astype(BF16)
    m11 = jnp.where(i >= j, m11, 0.0).astype(BF16)
    m10 = m10.astype(BF16)
    dr_ref[:, at_block(0)] = dot(wt[0], m00, nt)
    dr_ref[:, at_block(1)] = dot(wt[0], m10, nt) + dot(wt[1], m11, nt)
    dw_ref[:, at_block(0)] = dot(rt[0], m00) + dot(rt[1], m10)
    dw_ref[:, at_block(1)] = dot(rt[1], m11)


def total_of(ref, cols):
    parts = ref[pl.ds(cols, 16), :].astype(F32)
    return parts[:8] + parts[8:]


def kernel_sums(
    up_ref, down_ref, h_ref, probe_ref, local_ref,
    sums_ref, both_ref, cross_ref,
):
    cols = both_ref.shape[2]
    heads = local_ref.shape[1]
    place = lax.axis_index("context")
    inner = (place == 1) | (place == 2)
    mine = (place >= 2).astype(jnp.int32)
    even = lax.rem(place, 2) == 0
    t_up, t_down, th = (total_of(ref, cols) for ref in (up_ref, down_ref, h_ref))
    te, tf = jnp.where(even, t_up, t_down), jnp.where(even, t_down, t_up)
    coef_e = jnp.where(inner, 1.0, tf * th)
    coef_f = jnp.where(inner, jnp.zeros_like(te), 1.0)
    coef_h = jnp.where(inner, te, tf)
    coef_up = jnp.where(even, coef_e, coef_f)
    coef_down = jnp.where(even, coef_f, coef_e)
    y_up = jnp.where(inner & ~even, 1.0, 0.0)
    y_down = jnp.where(inner & even, 1.0, 0.0)

    def folded(v):
        return jnp.sum(v.reshape(STATE // 8, 8, BLOCK), axis=0)

    rows, select = [], []
    for lo in range(0, cols, BLOCK):
        here = pl.ds(lo, BLOCK)
        k = lo // BLOCK
        up, down = up_ref[here, :].astype(F32), down_ref[here, :].astype(F32)
        x = (
            up * coef_up[k : k + 1]
            + down * coef_down[k : k + 1]
            + h_ref[here, :].astype(F32) * coef_h[k : k + 1]
        )
        y = up * y_up + down * y_down
        both_ref[mine, :, here] = x.astype(BF16)
        both_ref[1 - mine, :, here] = y.astype(BF16)
        products = [
            folded(x * probe_ref[mine, n, :, here] + y * probe_ref[1 - mine, n, :, here])
            for n in range(2)
        ] + [folded(x * y), jnp.zeros((8, BLOCK), F32)]
        for part in pieces(jnp.concatenate(products, axis=0), 2):
            rows.append(part)
            select.append(selector(heads, lo, BLOCK))
    out = dot(jnp.concatenate(rows, axis=1), jnp.concatenate(select, axis=0))
    rate, bias, cross = (
        jnp.sum(out[8 * n : 8 * n + 8], axis=0, keepdims=True) for n in range(3)
    )
    local = local_ref[...]
    rate = rate + local[0:1] + local[3:4] * cross
    bias = bias + local[2:3] + local[4:5] * cross
    index = lax.broadcasted_iota(jnp.int32, (8, heads), 0)
    sums_ref[...] = jnp.where(
        index == 0, rate, jnp.where(index == 1, local[1:2], jnp.where(index == 2, bias, 0.0))
    )
    cross_ref[...] = jnp.broadcast_to(cross, (8, heads))


def kernel_keys(both_ref, qq_ref, wide_ref, dr_ref, dw_ref, keep_ref, send_ref):
    cols = qq_ref.shape[2]
    half = STATE // 2
    nt = ((1,), (1,))
    for b in range(2):
        at = at_block(b)
        dr = dr_ref[:, at]
        dw = dw_ref[:, at]
        for lo in range(0, cols, TILE):
            here = pl.ds(lo, TILE)
            s = (both_ref[1, :, here].astype(F32) * wide_ref[b : b + 1, here]).astype(BF16)
            a = (both_ref[0, :, here].astype(F32) * wide_ref[2 + b : 3 + b, here]).astype(BF16)
            dr += dot(s, qq_ref[1, at, here], nt)
            dw += dot(a, qq_ref[0, at, here], nt)
        keep_ref[pl.ds(0, half), at] = dw[:half]
        keep_ref[pl.ds(half, half), at] = dr[:half]
        send_ref[pl.ds(0, half), at] = dw[half:].astype(BF16)
        send_ref[pl.ds(half, half), at] = dr[half:].astype(BF16)


def kernel_outer(
    both_ref, keys_ref, qq_ref, gate_ref, gate_f_ref, in_ref, in_f_ref,
    cross_ref, p_ref, q_ref, small_ref, z_ref, rate_ref,
    grad_in_out, grad_gate_out, grad_step_out,
    grad_in_ref, grad_gate_ref, step_ref, sems,
):
    rows, cols = gate_ref.shape
    heads = small_ref.shape[1]
    copies = []

    def leave(src, dst):
        copies.append(pltpu.make_async_copy(src, dst, sems.at[len(copies)]))
        copies[-1].start()

    sums = []
    for b in range(2):
        at = at_block(b)
        parts = [[], []]
        select = []
        for lo in range(0, cols, TILE):
            here = pl.ds(lo, TILE)
            v = dot(keys_ref[1, at, :], both_ref[1, :, here])
            z = dot(keys_ref[0, at, :], both_ref[0, :, here])
            grad_gate_ref[at, here] = (
                gate_ref[at, here].astype(F32) + gate_f_ref[at, here].astype(F32) * v
            ).astype(BF16)
            grad_in_ref[at, here] = (
                in_ref[at, here].astype(F32) + in_f_ref[at, here].astype(F32) * z
            ).astype(BF16)
            for side, got in enumerate((z, v)):
                parts[side] += pieces(qq_ref[side, at, here].astype(F32) * got, 2)
            select += [selector(heads, lo, TILE)] * 2
        leave(grad_gate_ref.at[at], grad_gate_out.at[at])
        leave(grad_in_ref.at[at], grad_in_out.at[at])
        select = jnp.concatenate(select, axis=0)
        sums.append([
            dot(jnp.concatenate(parts[side], axis=1), select)
            * small_ref[(2 if side == 0 else 0) + b : (3 if side == 0 else 1) + b]
            for side in range(2)
        ])
    q, p = (jnp.concatenate([sums[b][side] for b in range(2)], axis=0) for side in range(2))
    ends = jnp.sum(q, axis=0, keepdims=True) + small_ref[5:6] * cross_ref[0:1]
    q = q + q_ref[...]
    flow = split_dot_left(triangle(rows, False), p + p_ref[...] - q, 3) + ends
    z = z_ref[...]
    grad = (q / softplus(z) - jnp.exp(rate_ref[...]) * flow) / (1.0 + jnp.exp(-z))
    step_ref[...] = grad.T
    leave(step_ref, grad_step_out)
    for copy in copies:
        copy.wait()


def kernel_add(a_ref, b_ref, c_ref, d_ref, out_ref):
    out_ref[...] = (a_ref[...] + b_ref[...]) + (c_ref[...] + d_ref[...])


def kernel_finish(
    keep_ref, got_ref, a_ref, b_ref, c_ref, d_ref, w_ref, r_ref, rate_ref, skip_ref, bias_ref
):
    half = w_ref.shape[0]
    w_ref[...] = keep_ref[pl.ds(0, half), :] + got_ref[pl.ds(0, half), :].astype(F32)
    r_ref[...] = keep_ref[pl.ds(half, half), :] + got_ref[pl.ds(half, half), :].astype(F32)
    sums = (a_ref[...] + b_ref[...]) + (c_ref[...] + d_ref[...])
    rate_ref[...] = sums[0:1]
    skip_ref[...] = sums[1:2]
    bias_ref[...] = sums[2:3]


V = pltpu.VMEM
ANY = pl.ANY


def call(kernel, outs, args, scratch=(), us=3.0, spaces=None, out_spaces=None, alias=None):
    spaces = spaces or [V] * len(args)
    out_spaces = out_spaces or [V] * len(outs)
    return pl.pallas_call(
        kernel,
        out_shape=[jax.ShapeDtypeStruct(s, d) for s, d in outs],
        in_specs=[pl.BlockSpec(memory_space=s) for s in spaces],
        out_specs=[pl.BlockSpec(memory_space=s) for s in out_spaces],
        scratch_shapes=list(scratch),
        input_output_aliases=alias or {},
        compiler_params=pltpu.CompilerParams(vmem_limit_bytes=36 * 1024 * 1024),
        cost_estimate=pl.CostEstimate(
            flops=int(us * 1e9), bytes_accessed=int(us * 1e6), transcendentals=0
        ),
    )(*args)


def exchange(array, axis, mask):
    count = lax.axis_size(axis)
    pairs = [(i, i ^ mask) for i in range(count) if i ^ mask < count]
    return lax.ppermute(array, axis, pairs)


def cycle(array, axis, by):
    count = lax.axis_size(axis)
    return lax.ppermute(array, axis, [(i, (i + by) % count) for i in range(count)])


def body(
    head_inputs,
    gate_inputs,
    step_raw,
    state_write,
    state_read,
    log_rate,
    skip_gain,
    step_bias,
    grad_gated,
):
    x, g, dy = head_inputs[0], gate_inputs[0], grad_gated[0]
    raw = step_raw[0].T
    heads, rows = raw.shape
    cols = x.shape[1]
    half = state_write.shape[2]
    w, r = state_write[0].T, state_read[0].T
    wt, rt = exchange(w, "tensor", 1), exchange(r, "tensor", 1)
    rate, skip, bias = (v.reshape(1, heads) for v in (log_rate, skip_gain, step_bias))
    payload = ((cols + 16, STATE), BF16)
    big = ((rows, cols), BF16)
    pair = ((2, rows, cols), BF16)
    thin = ((rows, heads), F32)
    tiny = ((8, heads), F32)
    one = ((1, heads), F32)
    key = ((half, rows), BF16)
    x, g, dy, w, r, skip, qq, z, rate, al, be, wide, small = call(
        kernel_scale,
        [big, big, big, key, key, one, pair, thin, one, thin, thin, ((8, cols), F32), tiny],
        [
            pltpu.with_memory_space_constraint(v, pltpu.HBM)
            for v in (x, g, dy, raw, bias, rate, skip, w, r)
        ],
        [V((heads, rows), F32), V((1, heads), F32), pltpu.SemaphoreType.DMA((12,))],
        spaces=[pltpu.HBM] * 9,
    )
    turned, send_up, send_down, send_h = call(
        kernel_states,
        [((2, STATE, rows), BF16), payload, payload, payload],
        [w, wt, r, rt, qq, wide],
    )
    got_up, got_down = cycle(send_up, "context", 1), cycle(send_down, "context", -1)
    got_h = exchange(send_h, "context", 2)
    state = ((2, STATE, cols), BF16)
    gate, gate_f, inp, inp_f, dr, dw, keys, p, q, probe, local = call(
        kernel_within,
        [big] * 4 + [((STATE, rows), F32)] * 2
        + [((2, rows, STATE), BF16), thin, thin, ((2, 2, STATE, cols), F32), tiny],
        [x, g, dy, skip, turned, qq, al, be, wide, z, rate, small],
        [V((6 * rows + 8, TILE), F32)],
        us=4.0,
    )
    sums, both, cross = call(
        kernel_sums, [tiny, state, tiny], [got_up, got_down, got_h, probe, local], us=0.5,
    )
    others = [exchange(sums, "context", mask) for mask in (1, 2, 3)]
    keep, send = call(
        kernel_keys, [((STATE, rows), F32), ((STATE, rows), BF16)],
        [both, qq, wide, dr, dw], us=1.0,
    )
    grad_in, grad_gate, grad_step = call(
        kernel_outer, [big, big, ((heads, rows), F32)],
        [both, keys, qq, gate, gate_f, inp, inp_f, cross, p, q, small, z, rate],
        [V((rows, cols), BF16)] * 2 + [V((heads, rows), F32), pltpu.SemaphoreType.DMA((5,))],
        us=2.0, out_spaces=[pltpu.HBM] * 3,
    )
    (sums,) = call(kernel_add, [tiny], [sums] + others, us=0.1)
    got = exchange(send, "tensor", 1)
    others = [exchange(sums, "dp", mask) for mask in (1, 2, 3)]
    grad_w, grad_r, sum_rate, sum_skip, sum_bias = call(
        kernel_finish,
        [((half, rows), F32)] * 2 + [one] * 3,
        [keep, got, sums] + others,
        us=0.2,
    )
    return (
        grad_in[None],
        grad_gate[None],
        grad_w.T[None],
        grad_r.T[None],
        grad_step.T[None],
        sum_rate.reshape(heads),
        sum_skip.reshape(heads),
        sum_bias.reshape(heads),
    )


def solution(mesh):
    wide = P("dp", "context", "tensor")
    head = P("tensor")
    return jax.shard_map(
        body,
        mesh=mesh,
        in_specs=(wide,) * 5 + (head,) * 3 + (wide,),
        out_specs=(wide,) * 5 + (head,) * 3,
        check_vma=False,
    )
```

```python
import functools
import math

import jax
import jax.numpy as jnp
from jax import lax
from jax.experimental import pallas as pl
from jax.experimental.pallas import tpu as pltpu
from jax.sharding import PartitionSpec as P

HEAD_DIM = 64
STATE = 128
BLOCK = 128
LOG2E = math.log2(math.e)
F32 = jnp.float32
BF16 = jnp.bfloat16
TILE = 256


def dot(a, b, dims=((1,), (0,))):
    return lax.dot_general(a, b, (dims, ((), ())), preferred_element_type=F32)


def pieces(v, count):
    out = []
    for _ in range(count):
        part = v.astype(BF16)
        out.append(part)
        v = v - part.astype(F32)
    return out


def split_dot_left(exact, v, count):
    return sum(dot(exact, part) for part in pieces(v, count))


def split_dot_right(v, exact, count):
    return sum(dot(part, exact) for part in pieces(v, count))


def expander(heads, lo, size):
    head = lax.broadcasted_iota(jnp.int32, (heads, size), 0)
    column = lax.broadcasted_iota(jnp.int32, (heads, size), 1) + lo
    return ((column >= head * HEAD_DIM) & (column < (head + 1) * HEAD_DIM)).astype(BF16)


def selector(heads, lo, size):
    head = lax.broadcasted_iota(jnp.int32, (size, heads), 1)
    column = lax.broadcasted_iota(jnp.int32, (size, heads), 0) + lo
    return ((column >= head * HEAD_DIM) & (column < (head + 1) * HEAD_DIM)).astype(BF16)


def triangle(rows, lower):
    i = lax.broadcasted_iota(jnp.int32, (rows, rows), 0)
    j = lax.broadcasted_iota(jnp.int32, (rows, rows), 1)
    return ((i >= j) if lower else (i <= j)).astype(BF16)


def softplus(z):
    return jnp.maximum(z, 0.0) + jnp.log(1.0 + jnp.exp(-jnp.abs(z)))


def logistic(v):
    return 0.5 + 0.5 * jnp.tanh(0.5 * v)


def at_block(b):
    return pl.ds(b * BLOCK, BLOCK)


def kernel_scale(
    x_in, g_in, dy_in, raw_in, bias_in, rate_in, skip_in, w_in, r_in,
    x_ref, g_ref, dy_ref, w_ref, r_ref, skip_ref, qq_ref, z_ref, rate_ref, al_ref, be_ref,
    wide_ref, small_ref,
    raw_ref, bias_ref, sems,
):
    rows, cols = x_ref.shape
    heads = raw_ref.shape[0]
    blocks = rows // BLOCK
    thin = [
        (raw_in, raw_ref), (bias_in, bias_ref), (rate_in, rate_ref),
        (skip_in, skip_ref), (w_in, w_ref), (r_in, r_ref),
    ]
    copies = [pltpu.make_async_copy(s, d, sems.at[i]) for i, (s, d) in enumerate(thin)]
    large = []
    for b in range(blocks):
        large.append([
            pltpu.make_async_copy(s.at[at_block(b)], d.at[at_block(b)], sems.at[6 + 3 * b + i])
            for i, (s, d) in enumerate([(g_in, g_ref), (dy_in, dy_ref), (x_in, x_ref)])
        ])
    for copy in copies[:3] + large[0] + large[1] + copies[3:]:
        copy.start()
    for copy in copies[:3]:
        copy.wait()
    z = raw_ref[...].T + bias_ref[...]
    z_ref[...] = z
    step = softplus(z)
    log2_decay = step * (-LOG2E * jnp.exp(rate_ref[...]))
    run = split_dot_left(triangle(rows, True), log2_decay, 3)
    mid0 = run[BLOCK // 2 - 1 : BLOCK // 2]
    mid1 = run[BLOCK + BLOCK // 2 - 1 : BLOCK + BLOCK // 2]
    end = run[rows - 1 : rows]
    row = lax.broadcasted_iota(jnp.int32, (rows, heads), 0)
    rel = run - jnp.where(row < BLOCK, mid0, mid1)
    for copy in large[0]:
        copy.wait()
    al = jnp.exp2(rel)
    be = jnp.exp2(-rel) * step
    al_ref[...] = al
    be_ref[...] = be
    small = jnp.exp2(
        jnp.concatenate([mid0, mid1, end - mid0, end - mid1, mid1 - mid0, end, end, end], axis=0)
    )
    small_ref[...] = small
    small_parts = pieces(small, 3)
    halves = [
        jnp.concatenate(
            pieces(jnp.concatenate([v[b * BLOCK : (b + 1) * BLOCK] for v in (al, be)], axis=0), 2),
            axis=1,
        )
        for b in range(blocks)
    ]
    for lo in range(0, cols, TILE):
        wide = expander(heads, lo, TILE)
        wide_ref[:, pl.ds(lo, TILE)] = sum(dot(part, wide) for part in small_parts)
    for b in range(blocks):
        if b:
            for copy in large[b]:
                copy.wait()
        at = at_block(b)
        for lo in range(0, cols, TILE):
            here = pl.ds(lo, TILE)
            wide = expander(heads, lo, TILE)
            spread = dot(halves[b], jnp.concatenate([wide, wide], axis=0))
            al_tile, be_tile = spread[:BLOCK], spread[BLOCK:]
            g = g_ref[at, here].astype(F32)
            u = dy_ref[at, here].astype(F32) * g * logistic(g)
            qq_ref[1, at, here] = (u * al_tile).astype(BF16)
            qq_ref[0, at, here] = (x_ref[at, here].astype(F32) * be_tile).astype(BF16)
    for copy in copies[3:]:
        copy.wait()


def kernel_states(
    w_ref, wt_ref, r_ref, rt_ref, qq_ref, wide_ref,
    turned_ref, up_ref, down_ref, h_ref,
):
    cols = qq_ref.shape[2]
    blocks = qq_ref.shape[1] // BLOCK
    place = lax.axis_index("context")
    writes = jnp.concatenate([w_ref[...], wt_ref[...]], axis=0)
    reads = jnp.concatenate([r_ref[...], rt_ref[...]], axis=0)
    turned_ref[0] = writes
    turned_ref[1] = reads
    for lo in range(0, cols, TILE):
        here = pl.ds(lo, TILE)
        state = jnp.zeros((STATE, TILE), F32)
        adjoint = state
        for b in range(blocks):
            at = at_block(b)
            part = slice(b * BLOCK, (b + 1) * BLOCK)
            state += dot(writes[:, part], qq_ref[0, at, here]) * wide_ref[2 + b : 3 + b, here]
            adjoint += dot(reads[:, part], qq_ref[1, at, here]) * wide_ref[b : b + 1, here]
        state = state.astype(BF16)
        adjoint = adjoint.astype(BF16)
        up = jnp.where(place < 3, state, adjoint)
        down = jnp.where(place < 1, state, adjoint)
        mid = jnp.where(place < 2, state, adjoint)
        for k in range(0, TILE, BLOCK):
            there = pl.ds(lo + k, BLOCK)
            up_ref[there, :] = up[:, k : k + BLOCK]
            down_ref[there, :] = down[:, k : k + BLOCK]
            h_ref[there, :] = mid[:, k : k + BLOCK]
    total = jnp.concatenate(
        [wide_ref[5:6, pl.ds(lo, BLOCK)] for lo in range(0, cols, BLOCK)], axis=0
    )
    totals = jnp.concatenate([part.astype(F32) for part in pieces(total, 2)], axis=0).astype(BF16)
    for ref in (up_ref, down_ref, h_ref):
        ref[pl.ds(cols, 16), :] = totals


def kernel_within(
    x_ref, g_ref, dy_ref, skip_ref, turned_ref, qq_ref, al_ref, be_ref, wide_ref, z_ref, rate_ref,
    small_ref,
    gate_ref, gate_f_ref, in_ref, in_f_ref, dr_ref, dw_ref, keys_ref, p_ref, q_ref, probe_ref,
    local_ref,
    spread_ref,
):
    rows, cols = x_ref.shape
    heads = skip_ref.shape[1]
    z = z_ref[...]
    rate = jnp.exp(rate_ref[...])
    step = softplus(z)
    slope = 1.0 / (1.0 + jnp.exp(-z))
    lower = triangle(rows, True)
    decayed = split_dot_left(lower, -rate * step, 3)
    climbed = rate * split_dot_left(lower, slope, 3)
    direct = slope / step
    decay_end = decayed[rows - 1 : rows]
    climb_end = climbed[rows - 1 : rows]
    thin = jnp.concatenate(
        [
            al_ref[...], be_ref[...],
            decay_end - decayed, direct + climbed - climb_end, decayed, -climbed,
            jnp.broadcast_to(skip_ref[...], (8, heads)),
        ],
        axis=0,
    )
    thin = jnp.concatenate(pieces(thin, 2), axis=1)
    nt = ((1,), (1,))
    wt = [turned_ref[0, :, at_block(b)] for b in range(2)]
    rt = [turned_ref[1, :, at_block(b)] for b in range(2)]
    w = [v.astype(F32).T.astype(BF16) for v in wt]
    r = [v.astype(F32).T.astype(BF16) for v in rt]
    for b in range(2):
        keys_ref[0, at_block(b), :] = w[b]
        keys_ref[1, at_block(b), :] = r[b]
    i = lax.broadcasted_iota(jnp.int32, (BLOCK, BLOCK), 0)
    j = lax.broadcasted_iota(jnp.int32, (BLOCK, BLOCK), 1)
    i00 = jnp.where(i >= j, dot(r[0], wt[0]), 0.0).astype(BF16)
    i11 = jnp.where(i >= j, dot(r[1], wt[1]), 0.0).astype(BF16)
    i10 = dot(r[1], wt[0]).astype(BF16)
    t00 = jnp.where(i <= j, dot(w[0], rt[0]), 0.0).astype(BF16)
    t11 = jnp.where(i <= j, dot(w[1], rt[1]), 0.0).astype(BF16)
    t10 = dot(w[0], rt[1]).astype(BF16)
    m00 = jnp.zeros((BLOCK, BLOCK), F32)
    m11 = m00
    m10 = m00
    p_parts, q_parts = [[], []], [[], []]
    skip_parts, selects, skip_selects = [], [], []
    for lo in range(0, cols, TILE):
        here = pl.ds(lo, TILE)
        wide = expander(heads, lo, TILE)
        spread_ref[...] = dot(thin, jnp.concatenate([wide, wide], axis=0))
        selects += [wide] * 2
        skip_selects += [wide] * 3
        link = wide_ref[4:5, here]
        xb = [qq_ref[0, at_block(b), here] for b in range(2)]
        ua = [qq_ref[1, at_block(b), here] for b in range(2)]
        m00 += dot(ua[0], xb[0], nt)
        m11 += dot(ua[1], xb[1], nt)
        m10 += dot(ua[1], (xb[0].astype(F32) * link).astype(BF16), nt)
        v = [dot(i00, xb[0]), dot(i11, xb[1]) + link * dot(i10, xb[0])]
        z = [dot(t00, ua[0]) + link * dot(t10, ua[1]), dot(t11, ua[1])]
        skip = spread_ref[6 * rows : 6 * rows + 1, :]
        totals = [[0.0, 0.0], [0.0, 0.0]]
        products = 0.0
        for b in range(2):
            at = at_block(b)
            xf, uf = xb[b].astype(F32), ua[b].astype(F32)
            p_parts[b] += pieces(uf * v[b], 2)
            q_parts[b] += pieces(xf * z[b], 2)
            g = g_ref[at, here].astype(F32)
            dy = dy_ref[at, here].astype(F32)
            x = x_ref[at, here].astype(F32)
            sig = logistic(g)
            u = dy * g * sig
            up = dy * sig * (1.0 + g * (1.0 - sig))
            al = spread_ref[pl.ds(b * BLOCK, BLOCK), :]
            be = spread_ref[pl.ds(rows + b * BLOCK, BLOCK), :]
            gate_ref[at, here] = (up * (al * v[b] + skip * x)).astype(BF16)
            gate_f_ref[at, here] = (up * al * wide_ref[b : b + 1, here]).astype(BF16)
            in_ref[at, here] = (be * z[b] + skip * u).astype(BF16)
            in_f_ref[at, here] = (be * wide_ref[2 + b : 3 + b, here]).astype(BF16)
            products += jnp.sum((u * x).reshape(BLOCK // 8, 8, TILE), axis=0)
            for side, (turned, own) in enumerate(((wt[b], xf), (rt[b], uf))):
                row = (2 if side == 0 else 0) + b
                for n in range(2):
                    weight = spread_ref[pl.ds((2 + 2 * side + n) * rows + b * BLOCK, BLOCK), :]
                    totals[side][n] += (
                        dot(turned, (own * weight).astype(BF16)) * wide_ref[row : row + 1, here]
                    )
        for side in range(2):
            for n in range(2):
                probe_ref[side, n, :, here] = totals[side][n]
        skip_parts += pieces(products, 3)
    selects = jnp.concatenate(selects, axis=1)
    p, q = (
        jnp.concatenate([dot(jnp.concatenate(v, axis=1), selects, nt) for v in parts], axis=0)
        for parts in (p_parts, q_parts)
    )
    skips = dot(jnp.concatenate(skip_parts, axis=1), jnp.concatenate(skip_selects, axis=1), nt)
    p_ref[...] = p
    q_ref[...] = q
    local = [
        jnp.sum(v, axis=0, keepdims=True)
        for v in (decayed * (p - q), skips, direct * q - climbed * (p - q))
    ]
    kept = small_ref[5:6]
    local += [decay_end * kept, -climb_end * kept] + [jnp.zeros_like(kept)] * 3
    local_ref[...] = jnp.concatenate(local, axis=0)
    m00 = jnp.where(i >= j, m00, 0.0).astype(BF16)
    m11 = jnp.where(i >= j, m11, 0.0).astype(BF16)
    m10 = m10.astype(BF16)
    dr_ref[:, at_block(0)] = dot(wt[0], m00, nt)
    dr_ref[:, at_block(1)] = dot(wt[0], m10, nt) + dot(wt[1], m11, nt)
    dw_ref[:, at_block(0)] = dot(rt[0], m00) + dot(rt[1], m10)
    dw_ref[:, at_block(1)] = dot(rt[1], m11)


def total_of(ref, cols):
    parts = ref[pl.ds(cols, 16), :].astype(F32)
    return parts[:8] + parts[8:]


def kernel_sums(
    up_ref, down_ref, h_ref, probe_ref, local_ref,
    sums_ref, both_ref, cross_ref,
):
    cols = both_ref.shape[2]
    heads = local_ref.shape[1]
    place = lax.axis_index("context")
    inner = (place == 1) | (place == 2)
    mine = (place >= 2).astype(jnp.int32)
    even = lax.rem(place, 2) == 0
    t_up, t_down, th = (total_of(ref, cols) for ref in (up_ref, down_ref, h_ref))
    te, tf = jnp.where(even, t_up, t_down), jnp.where(even, t_down, t_up)
    coef_e = jnp.where(inner, 1.0, tf * th)
    coef_f = jnp.where(inner, jnp.zeros_like(te), 1.0)
    coef_h = jnp.where(inner, te, tf)
    coef_up = jnp.where(even, coef_e, coef_f)
    coef_down = jnp.where(even, coef_f, coef_e)
    y_up = jnp.where(inner & ~even, 1.0, 0.0)
    y_down = jnp.where(inner & even, 1.0, 0.0)

    def folded(v):
        return jnp.sum(v.reshape(STATE // 8, 8, BLOCK), axis=0)

    rows, select = [], []
    for lo in range(0, cols, BLOCK):
        here = pl.ds(lo, BLOCK)
        k = lo // BLOCK
        up, down = up_ref[here, :].astype(F32), down_ref[here, :].astype(F32)
        x = (
            up * coef_up[k : k + 1]
            + down * coef_down[k : k + 1]
            + h_ref[here, :].astype(F32) * coef_h[k : k + 1]
        )
        y = up * y_up + down * y_down
        both_ref[mine, :, here] = x.astype(BF16)
        both_ref[1 - mine, :, here] = y.astype(BF16)
        products = [
            folded(x * probe_ref[mine, n, :, here] + y * probe_ref[1 - mine, n, :, here])
            for n in range(2)
        ] + [folded(x * y), jnp.zeros((8, BLOCK), F32)]
        for part in pieces(jnp.concatenate(products, axis=0), 2):
            rows.append(part)
            select.append(expander(heads, lo, BLOCK))
    out = dot(jnp.concatenate(rows, axis=1), jnp.concatenate(select, axis=1), ((1,), (1,)))
    rate, bias, cross = (
        jnp.sum(out[8 * n : 8 * n + 8], axis=0, keepdims=True) for n in range(3)
    )
    local = local_ref[...]
    rate = rate + local[0:1] + local[3:4] * cross
    bias = bias + local[2:3] + local[4:5] * cross
    index = lax.broadcasted_iota(jnp.int32, (8, heads), 0)
    sums_ref[...] = jnp.where(
        index == 0, rate, jnp.where(index == 1, local[1:2], jnp.where(index == 2, bias, 0.0))
    )
    cross_ref[...] = jnp.broadcast_to(cross, (8, heads))


def kernel_keys(both_ref, qq_ref, wide_ref, dr_ref, dw_ref, keep_ref, send_ref):
    cols = qq_ref.shape[2]
    half = STATE // 2
    nt = ((1,), (1,))
    for b in range(2):
        at = at_block(b)
        dr = dr_ref[:, at]
        dw = dw_ref[:, at]
        for lo in range(0, cols, TILE):
            here = pl.ds(lo, TILE)
            s = (both_ref[1, :, here].astype(F32) * wide_ref[b : b + 1, here]).astype(BF16)
            a = (both_ref[0, :, here].astype(F32) * wide_ref[2 + b : 3 + b, here]).astype(BF16)
            dr += dot(s, qq_ref[1, at, here], nt)
            dw += dot(a, qq_ref[0, at, here], nt)
        keep_ref[pl.ds(0, half), at] = dw[:half]
        keep_ref[pl.ds(half, half), at] = dr[:half]
        send_ref[pl.ds(0, half), at] = dw[half:].astype(BF16)
        send_ref[pl.ds(half, half), at] = dr[half:].astype(BF16)


def kernel_outer(
    both_ref, keys_ref, qq_ref, gate_ref, gate_f_ref, in_ref, in_f_ref,
    cross_ref, p_ref, q_ref, small_ref, z_ref, rate_ref,
    grad_in_out, grad_gate_out, grad_step_out,
    grad_in_ref, grad_gate_ref, step_ref, sems,
):
    rows, cols = gate_ref.shape
    heads = small_ref.shape[1]
    copies = []

    def leave(src, dst):
        copies.append(pltpu.make_async_copy(src, dst, sems.at[len(copies)]))
        copies[-1].start()

    sums = []
    for b in range(2):
        at = at_block(b)
        parts = [[], []]
        select = []
        for lo in range(0, cols, TILE):
            here = pl.ds(lo, TILE)
            v = dot(keys_ref[1, at, :], both_ref[1, :, here])
            z = dot(keys_ref[0, at, :], both_ref[0, :, here])
            grad_gate_ref[at, here] = (
                gate_ref[at, here].astype(F32) + gate_f_ref[at, here].astype(F32) * v
            ).astype(BF16)
            grad_in_ref[at, here] = (
                in_ref[at, here].astype(F32) + in_f_ref[at, here].astype(F32) * z
            ).astype(BF16)
            for side, got in enumerate((z, v)):
                parts[side] += pieces(qq_ref[side, at, here].astype(F32) * got, 2)
            select += [expander(heads, lo, TILE)] * 2
        leave(grad_gate_ref.at[at], grad_gate_out.at[at])
        leave(grad_in_ref.at[at], grad_in_out.at[at])
        select = jnp.concatenate(select, axis=1)
        sums.append([
            dot(jnp.concatenate(parts[side], axis=1), select, ((1,), (1,)))
            * small_ref[(2 if side == 0 else 0) + b : (3 if side == 0 else 1) + b]
            for side in range(2)
        ])
    q, p = (jnp.concatenate([sums[b][side] for b in range(2)], axis=0) for side in range(2))
    ends = jnp.sum(q, axis=0, keepdims=True) + small_ref[5:6] * cross_ref[0:1]
    q = q + q_ref[...]
    flow = split_dot_left(triangle(rows, False), p + p_ref[...] - q, 3) + ends
    z = z_ref[...]
    grad = (q / softplus(z) - jnp.exp(rate_ref[...]) * flow) / (1.0 + jnp.exp(-z))
    step_ref[...] = grad.T
    leave(step_ref, grad_step_out)
    for copy in copies:
        copy.wait()


def kernel_add(a_ref, b_ref, c_ref, d_ref, out_ref):
    out_ref[...] = (a_ref[...] + b_ref[...]) + (c_ref[...] + d_ref[...])


def kernel_finish(
    keep_ref, got_ref, a_ref, b_ref, c_ref, d_ref, w_ref, r_ref, rate_ref, skip_ref, bias_ref
):
    half = w_ref.shape[0]
    w_ref[...] = keep_ref[pl.ds(0, half), :] + got_ref[pl.ds(0, half), :].astype(F32)
    r_ref[...] = keep_ref[pl.ds(half, half), :] + got_ref[pl.ds(half, half), :].astype(F32)
    sums = (a_ref[...] + b_ref[...]) + (c_ref[...] + d_ref[...])
    rate_ref[...] = sums[0:1]
    skip_ref[...] = sums[1:2]
    bias_ref[...] = sums[2:3]


V = pltpu.VMEM
ANY = pl.ANY


def call(kernel, outs, args, scratch=(), us=3.0, spaces=None, out_spaces=None, alias=None):
    spaces = spaces or [V] * len(args)
    out_spaces = out_spaces or [V] * len(outs)
    return pl.pallas_call(
        kernel,
        out_shape=[jax.ShapeDtypeStruct(s, d) for s, d in outs],
        in_specs=[pl.BlockSpec(memory_space=s) for s in spaces],
        out_specs=[pl.BlockSpec(memory_space=s) for s in out_spaces],
        scratch_shapes=list(scratch),
        input_output_aliases=alias or {},
        compiler_params=pltpu.CompilerParams(vmem_limit_bytes=36 * 1024 * 1024),
        cost_estimate=pl.CostEstimate(
            flops=int(us * 1e9), bytes_accessed=int(us * 1e6), transcendentals=0
        ),
    )(*args)


def exchange(array, axis, mask):
    count = lax.axis_size(axis)
    pairs = [(i, i ^ mask) for i in range(count) if i ^ mask < count]
    return lax.ppermute(array, axis, pairs)


def cycle(array, axis, by):
    count = lax.axis_size(axis)
    return lax.ppermute(array, axis, [(i, (i + by) % count) for i in range(count)])


def body(
    head_inputs,
    gate_inputs,
    step_raw,
    state_write,
    state_read,
    log_rate,
    skip_gain,
    step_bias,
    grad_gated,
):
    x, g, dy = head_inputs[0], gate_inputs[0], grad_gated[0]
    raw = step_raw[0].T
    heads, rows = raw.shape
    cols = x.shape[1]
    half = state_write.shape[2]
    w, r = state_write[0].T, state_read[0].T
    wt, rt = exchange(w, "tensor", 1), exchange(r, "tensor", 1)
    rate, skip, bias = (v.reshape(1, heads) for v in (log_rate, skip_gain, step_bias))
    payload = ((cols + 16, STATE), BF16)
    big = ((rows, cols), BF16)
    pair = ((2, rows, cols), BF16)
    thin = ((rows, heads), F32)
    tiny = ((8, heads), F32)
    one = ((1, heads), F32)
    key = ((half, rows), BF16)
    x, g, dy, w, r, skip, qq, z, rate, al, be, wide, small = call(
        kernel_scale,
        [big, big, big, key, key, one, pair, thin, one, thin, thin, ((8, cols), F32), tiny],
        [
            pltpu.with_memory_space_constraint(v, pltpu.HBM)
            for v in (x, g, dy, raw, bias, rate, skip, w, r)
        ],
        [V((heads, rows), F32), V((1, heads), F32), pltpu.SemaphoreType.DMA((12,))],
        spaces=[pltpu.HBM] * 9,
    )
    turned, send_up, send_down, send_h = call(
        kernel_states,
        [((2, STATE, rows), BF16), payload, payload, payload],
        [w, wt, r, rt, qq, wide],
    )
    got_up, got_down = cycle(send_up, "context", 1), cycle(send_down, "context", -1)
    got_h = exchange(send_h, "context", 2)
    state = ((2, STATE, cols), BF16)
    gate, gate_f, inp, inp_f, dr, dw, keys, p, q, probe, local = call(
        kernel_within,
        [big] * 4 + [((STATE, rows), F32)] * 2
        + [((2, rows, STATE), BF16), thin, thin, ((2, 2, STATE, cols), F32), tiny],
        [x, g, dy, skip, turned, qq, al, be, wide, z, rate, small],
        [V((6 * rows + 8, TILE), F32)],
        us=4.0,
    )
    sums, both, cross = call(
        kernel_sums, [tiny, state, tiny], [got_up, got_down, got_h, probe, local], us=0.5,
    )
    others = [exchange(sums, "context", mask) for mask in (1, 2, 3)]
    keep, send = call(
        kernel_keys, [((STATE, rows), F32), ((STATE, rows), BF16)],
        [both, qq, wide, dr, dw], us=1.0,
    )
    grad_in, grad_gate, grad_step = call(
        kernel_outer, [big, big, ((heads, rows), F32)],
        [both, keys, qq, gate, gate_f, inp, inp_f, cross, p, q, small, z, rate],
        [V((rows, cols), BF16)] * 2 + [V((heads, rows), F32), pltpu.SemaphoreType.DMA((5,))],
        us=2.0, out_spaces=[pltpu.HBM] * 3,
    )
    (sums,) = call(kernel_add, [tiny], [sums] + others, us=0.1)
    got = exchange(send, "tensor", 1)
    others = [exchange(sums, "dp", mask) for mask in (1, 2, 3)]
    grad_w, grad_r, sum_rate, sum_skip, sum_bias = call(
        kernel_finish,
        [((half, rows), F32)] * 2 + [one] * 3,
        [keep, got, sums] + others,
        us=0.2,
    )
    return (
        grad_in[None],
        grad_gate[None],
        grad_w.T[None],
        grad_r.T[None],
        grad_step.T[None],
        sum_rate.reshape(heads),
        sum_skip.reshape(heads),
        sum_bias.reshape(heads),
    )


def solution(mesh):
    wide = P("dp", "context", "tensor")
    head = P("tensor")
    return jax.shard_map(
        body,
        mesh=mesh,
        in_specs=(wide,) * 5 + (head,) * 3 + (wide,),
        out_specs=(wide,) * 5 + (head,) * 3,
        check_vma=False,
    )
```

```python
import functools
import math

import jax
import jax.numpy as jnp
from jax import lax
from jax.experimental import pallas as pl
from jax.experimental.pallas import tpu as pltpu
from jax.sharding import PartitionSpec as P

HEAD_DIM = 64
STATE = 128
BLOCK = 128
LOG2E = math.log2(math.e)
F32 = jnp.float32
BF16 = jnp.bfloat16
TILE = 256


def dot(a, b, dims=((1,), (0,))):
    return lax.dot_general(a, b, (dims, ((), ())), preferred_element_type=F32)


def pieces(v, count):
    out = []
    for _ in range(count):
        part = v.astype(BF16)
        out.append(part)
        v = v - part.astype(F32)
    return out


def split_dot_left(exact, v, count):
    return sum(dot(exact, part) for part in pieces(v, count))


def split_dot_right(v, exact, count):
    return sum(dot(part, exact) for part in pieces(v, count))


def expander(heads, lo, size):
    head = lax.broadcasted_iota(jnp.int32, (heads, size), 0)
    column = lax.broadcasted_iota(jnp.int32, (heads, size), 1) + lo
    return ((column >= head * HEAD_DIM) & (column < (head + 1) * HEAD_DIM)).astype(BF16)


def selector(heads, lo, size):
    head = lax.broadcasted_iota(jnp.int32, (size, heads), 1)
    column = lax.broadcasted_iota(jnp.int32, (size, heads), 0) + lo
    return ((column >= head * HEAD_DIM) & (column < (head + 1) * HEAD_DIM)).astype(BF16)


def triangle(rows, lower):
    i = lax.broadcasted_iota(jnp.int32, (rows, rows), 0)
    j = lax.broadcasted_iota(jnp.int32, (rows, rows), 1)
    return ((i >= j) if lower else (i <= j)).astype(BF16)


def softplus(z):
    return jnp.maximum(z, 0.0) + jnp.log(1.0 + jnp.exp(-jnp.abs(z)))


def logistic(v):
    return 0.5 + 0.5 * jnp.tanh(0.5 * v)


def at_block(b):
    return pl.ds(b * BLOCK, BLOCK)


def kernel_scale(
    x_in, g_in, dy_in, raw_in, bias_in, rate_in, skip_in, w_in, r_in,
    x_ref, g_ref, dy_ref, w_ref, r_ref, skip_ref, qq_ref, z_ref, rate_ref, al_ref, be_ref,
    wide_ref, small_ref,
    raw_ref, bias_ref, sems,
):
    rows, cols = x_ref.shape
    heads = raw_ref.shape[0]
    blocks = rows // BLOCK
    thin = [
        (raw_in, raw_ref), (bias_in, bias_ref), (rate_in, rate_ref),
        (skip_in, skip_ref), (w_in, w_ref), (r_in, r_ref),
    ]
    copies = [pltpu.make_async_copy(s, d, sems.at[i]) for i, (s, d) in enumerate(thin)]
    large = []
    for b in range(blocks):
        large.append([
            pltpu.make_async_copy(s.at[at_block(b)], d.at[at_block(b)], sems.at[6 + 3 * b + i])
            for i, (s, d) in enumerate([(g_in, g_ref), (dy_in, dy_ref), (x_in, x_ref)])
        ])
    for copy in copies[:3] + large[0] + large[1] + copies[3:]:
        copy.start()
    for copy in copies[:3]:
        copy.wait()
    z = raw_ref[...].T + bias_ref[...]
    z_ref[...] = z
    step = softplus(z)
    log2_decay = step * (-LOG2E * jnp.exp(rate_ref[...]))
    run = split_dot_left(triangle(rows, True), log2_decay, 3)
    mid0 = run[BLOCK // 2 - 1 : BLOCK // 2]
    mid1 = run[BLOCK + BLOCK // 2 - 1 : BLOCK + BLOCK // 2]
    end = run[rows - 1 : rows]
    row = lax.broadcasted_iota(jnp.int32, (rows, heads), 0)
    rel = run - jnp.where(row < BLOCK, mid0, mid1)
    for copy in large[0]:
        copy.wait()
    al = jnp.exp2(rel)
    be = jnp.exp2(-rel) * step
    al_ref[...] = al
    be_ref[...] = be
    small = jnp.exp2(
        jnp.concatenate([mid0, mid1, end - mid0, end - mid1, mid1 - mid0, end, end, end], axis=0)
    )
    small_ref[...] = small
    small_parts = pieces(small, 3)
    halves = [
        jnp.concatenate(
            pieces(jnp.concatenate([v[b * BLOCK : (b + 1) * BLOCK] for v in (al, be)], axis=0), 2),
            axis=1,
        )
        for b in range(blocks)
    ]
    for lo in range(0, cols, TILE):
        wide = expander(heads, lo, TILE)
        wide_ref[:, pl.ds(lo, TILE)] = sum(dot(part, wide) for part in small_parts)
    for b in range(blocks):
        if b:
            for copy in large[b]:
                copy.wait()
        at = at_block(b)
        for lo in range(0, cols, TILE):
            here = pl.ds(lo, TILE)
            wide = expander(heads, lo, TILE)
            spread = dot(halves[b], jnp.concatenate([wide, wide], axis=0))
            al_tile, be_tile = spread[:BLOCK], spread[BLOCK:]
            g = g_ref[at, here].astype(F32)
            u = dy_ref[at, here].astype(F32) * g * logistic(g)
            qq_ref[1, at, here] = (u * al_tile).astype(BF16)
            qq_ref[0, at, here] = (x_ref[at, here].astype(F32) * be_tile).astype(BF16)
    for copy in copies[3:]:
        copy.wait()


def kernel_states(
    w_ref, wt_ref, r_ref, rt_ref, qq_ref, wide_ref,
    turned_ref, up_ref, down_ref, h_ref,
):
    cols = qq_ref.shape[2]
    blocks = qq_ref.shape[1] // BLOCK
    place = lax.axis_index("context")
    writes = jnp.concatenate([w_ref[...], wt_ref[...]], axis=0)
    reads = jnp.concatenate([r_ref[...], rt_ref[...]], axis=0)
    turned_ref[0] = writes
    turned_ref[1] = reads
    for lo in range(0, cols, TILE):
        here = pl.ds(lo, TILE)
        state = jnp.zeros((STATE, TILE), F32)
        adjoint = state
        for b in range(blocks):
            at = at_block(b)
            part = slice(b * BLOCK, (b + 1) * BLOCK)
            state += dot(writes[:, part], qq_ref[0, at, here]) * wide_ref[2 + b : 3 + b, here]
            adjoint += dot(reads[:, part], qq_ref[1, at, here]) * wide_ref[b : b + 1, here]
        state = state.astype(BF16)
        adjoint = adjoint.astype(BF16)
        up = jnp.where(place < 3, state, adjoint)
        down = jnp.where(place < 1, state, adjoint)
        mid = jnp.where(place < 2, state, adjoint)
        for k in range(0, TILE, BLOCK):
            there = pl.ds(lo + k, BLOCK)
            up_ref[there, :] = up[:, k : k + BLOCK]
            down_ref[there, :] = down[:, k : k + BLOCK]
            h_ref[there, :] = mid[:, k : k + BLOCK]
    total = jnp.concatenate(
        [wide_ref[5:6, pl.ds(lo, BLOCK)] for lo in range(0, cols, BLOCK)], axis=0
    )
    totals = jnp.concatenate([part.astype(F32) for part in pieces(total, 2)], axis=0).astype(BF16)
    for ref in (up_ref, down_ref, h_ref):
        ref[pl.ds(cols, 16), :] = totals


def kernel_within(
    x_ref, g_ref, dy_ref, skip_ref, turned_ref, qq_ref, al_ref, be_ref, wide_ref, z_ref, rate_ref,
    small_ref,
    gate_ref, gate_f_ref, in_ref, in_f_ref, dr_ref, dw_ref, keys_ref, p_ref, q_ref, probe_ref,
    local_ref,
    spread_ref,
):
    rows, cols = x_ref.shape
    heads = skip_ref.shape[1]
    z = z_ref[...]
    rate = jnp.exp(rate_ref[...])
    step = softplus(z)
    slope = 1.0 / (1.0 + jnp.exp(-z))
    lower = triangle(rows, True)
    decayed = split_dot_left(lower, -rate * step, 3)
    climbed = rate * split_dot_left(lower, slope, 3)
    direct = slope / step
    decay_end = decayed[rows - 1 : rows]
    climb_end = climbed[rows - 1 : rows]
    thin = jnp.concatenate(
        [
            al_ref[...], be_ref[...],
            decay_end - decayed, direct + climbed - climb_end, decayed, -climbed,
            jnp.broadcast_to(skip_ref[...], (8, heads)),
        ],
        axis=0,
    )
    thin = jnp.concatenate(pieces(thin, 2), axis=1)
    nt = ((1,), (1,))
    wt = [turned_ref[0, :, at_block(b)] for b in range(2)]
    rt = [turned_ref[1, :, at_block(b)] for b in range(2)]
    w = [v.astype(F32).T.astype(BF16) for v in wt]
    r = [v.astype(F32).T.astype(BF16) for v in rt]
    for b in range(2):
        keys_ref[0, at_block(b), :] = w[b]
        keys_ref[1, at_block(b), :] = r[b]
    i = lax.broadcasted_iota(jnp.int32, (BLOCK, BLOCK), 0)
    j = lax.broadcasted_iota(jnp.int32, (BLOCK, BLOCK), 1)
    i00 = jnp.where(i >= j, dot(r[0], wt[0]), 0.0).astype(BF16)
    i11 = jnp.where(i >= j, dot(r[1], wt[1]), 0.0).astype(BF16)
    i10 = dot(r[1], wt[0]).astype(BF16)
    t00 = jnp.where(i <= j, dot(w[0], rt[0]), 0.0).astype(BF16)
    t11 = jnp.where(i <= j, dot(w[1], rt[1]), 0.0).astype(BF16)
    t10 = dot(w[0], rt[1]).astype(BF16)
    m00 = jnp.zeros((BLOCK, BLOCK), F32)
    m11 = m00
    m10 = m00
    p_parts, q_parts = [[], []], [[], []]
    skip_parts, selects, skip_selects = [], [], []
    for lo in range(0, cols, TILE):
        here = pl.ds(lo, TILE)
        wide = expander(heads, lo, TILE)
        spread_ref[...] = dot(thin, jnp.concatenate([wide, wide], axis=0))
        sel = selector(heads, lo, TILE)
        selects += [sel] * 2
        skip_selects += [sel] * 3
        link = wide_ref[4:5, here]
        xb = [qq_ref[0, at_block(b), here] for b in range(2)]
        ua = [qq_ref[1, at_block(b), here] for b in range(2)]
        m00 += dot(ua[0], xb[0], nt)
        m11 += dot(ua[1], xb[1], nt)
        m10 += dot(ua[1], (xb[0].astype(F32) * link).astype(BF16), nt)
        v = [dot(i00, xb[0]), dot(i11, xb[1]) + link * dot(i10, xb[0])]
        z = [dot(t00, ua[0]) + link * dot(t10, ua[1]), dot(t11, ua[1])]
        skip = spread_ref[6 * rows : 6 * rows + 1, :]
        totals = [[0.0, 0.0], [0.0, 0.0]]
        products = 0.0
        for b in range(2):
            at = at_block(b)
            xf, uf = xb[b].astype(F32), ua[b].astype(F32)
            p_parts[b] += pieces(uf * v[b], 2)
            q_parts[b] += pieces(xf * z[b], 2)
            g = g_ref[at, here].astype(F32)
            dy = dy_ref[at, here].astype(F32)
            x = x_ref[at, here].astype(F32)
            sig = logistic(g)
            u = dy * g * sig
            up = dy * sig * (1.0 + g * (1.0 - sig))
            al = spread_ref[pl.ds(b * BLOCK, BLOCK), :]
            be = spread_ref[pl.ds(rows + b * BLOCK, BLOCK), :]
            gate_ref[at, here] = (up * (al * v[b] + skip * x)).astype(BF16)
            gate_f_ref[at, here] = (up * al * wide_ref[b : b + 1, here]).astype(BF16)
            in_ref[at, here] = (be * z[b] + skip * u).astype(BF16)
            in_f_ref[at, here] = (be * wide_ref[2 + b : 3 + b, here]).astype(BF16)
            products += jnp.sum((u * x).reshape(BLOCK // 8, 8, TILE), axis=0)
            for side, (turned, own) in enumerate(((wt[b], xf), (rt[b], uf))):
                row = (2 if side == 0 else 0) + b
                for n in range(2):
                    weight = spread_ref[pl.ds((2 + 2 * side + n) * rows + b * BLOCK, BLOCK), :]
                    totals[side][n] += (
                        dot(turned, (own * weight).astype(BF16)) * wide_ref[row : row + 1, here]
                    )
        for side in range(2):
            for n in range(2):
                probe_ref[side, n, :, here] = totals[side][n].astype(BF16)
        skip_parts += pieces(products, 3)
    selects = jnp.concatenate(selects, axis=0)
    p, q = (
        jnp.concatenate([dot(jnp.concatenate(v, axis=1), selects) for v in parts], axis=0)
        for parts in (p_parts, q_parts)
    )
    skips = dot(jnp.concatenate(skip_parts, axis=1), jnp.concatenate(skip_selects, axis=0))
    p_ref[...] = p
    q_ref[...] = q
    local = [
        jnp.sum(v, axis=0, keepdims=True)
        for v in (decayed * (p - q), skips, direct * q - climbed * (p - q))
    ]
    kept = small_ref[5:6]
    local += [decay_end * kept, -climb_end * kept] + [jnp.zeros_like(kept)] * 3
    local_ref[...] = jnp.concatenate(local, axis=0)
    m00 = jnp.where(i >= j, m00, 0.0).astype(BF16)
    m11 = jnp.where(i >= j, m11, 0.0).astype(BF16)
    m10 = m10.astype(BF16)
    dr_ref[:, at_block(0)] = dot(wt[0], m00, nt)
    dr_ref[:, at_block(1)] = dot(wt[0], m10, nt) + dot(wt[1], m11, nt)
    dw_ref[:, at_block(0)] = dot(rt[0], m00) + dot(rt[1], m10)
    dw_ref[:, at_block(1)] = dot(rt[1], m11)


def total_of(ref, cols):
    parts = ref[pl.ds(cols, 16), :].astype(F32)
    return parts[:8] + parts[8:]


def kernel_sums(
    up_ref, down_ref, h_ref, probe_ref, local_ref,
    sums_ref, both_ref, cross_ref,
):
    cols = both_ref.shape[2]
    heads = local_ref.shape[1]
    place = lax.axis_index("context")
    inner = (place == 1) | (place == 2)
    mine = (place >= 2).astype(jnp.int32)
    even = lax.rem(place, 2) == 0
    t_up, t_down, th = (total_of(ref, cols) for ref in (up_ref, down_ref, h_ref))
    te, tf = jnp.where(even, t_up, t_down), jnp.where(even, t_down, t_up)
    coef_e = jnp.where(inner, 1.0, tf * th)
    coef_f = jnp.where(inner, jnp.zeros_like(te), 1.0)
    coef_h = jnp.where(inner, te, tf)
    coef_up = jnp.where(even, coef_e, coef_f)
    coef_down = jnp.where(even, coef_f, coef_e)
    y_up = jnp.where(inner & ~even, 1.0, 0.0)
    y_down = jnp.where(inner & even, 1.0, 0.0)

    def folded(v):
        return jnp.sum(v.reshape(STATE // 8, 8, BLOCK), axis=0)

    rows, select = [], []
    for lo in range(0, cols, BLOCK):
        here = pl.ds(lo, BLOCK)
        k = lo // BLOCK
        up, down = up_ref[here, :].astype(F32), down_ref[here, :].astype(F32)
        x = (
            up * coef_up[k : k + 1]
            + down * coef_down[k : k + 1]
            + h_ref[here, :].astype(F32) * coef_h[k : k + 1]
        )
        y = up * y_up + down * y_down
        both_ref[mine, :, here] = x.astype(BF16)
        both_ref[1 - mine, :, here] = y.astype(BF16)
        products = [
            folded(x * probe_ref[mine, n, :, here] + y * probe_ref[1 - mine, n, :, here])
            for n in range(2)
        ] + [folded(x * y), jnp.zeros((8, BLOCK), F32)]
        for part in pieces(jnp.concatenate(products, axis=0), 2):
            rows.append(part)
            select.append(selector(heads, lo, BLOCK))
    out = dot(jnp.concatenate(rows, axis=1), jnp.concatenate(select, axis=0))
    rate, bias, cross = (
        jnp.sum(out[8 * n : 8 * n + 8], axis=0, keepdims=True) for n in range(3)
    )
    local = local_ref[...]
    rate = rate + local[0:1] + local[3:4] * cross
    bias = bias + local[2:3] + local[4:5] * cross
    index = lax.broadcasted_iota(jnp.int32, (8, heads), 0)
    sums_ref[...] = jnp.where(
        index == 0, rate, jnp.where(index == 1, local[1:2], jnp.where(index == 2, bias, 0.0))
    )
    cross_ref[...] = jnp.broadcast_to(cross, (8, heads))


def kernel_keys(both_ref, qq_ref, wide_ref, dr_ref, dw_ref, keep_ref, send_ref):
    cols = qq_ref.shape[2]
    half = STATE // 2
    nt = ((1,), (1,))
    for b in range(2):
        at = at_block(b)
        dr = dr_ref[:, at]
        dw = dw_ref[:, at]
        for lo in range(0, cols, TILE):
            here = pl.ds(lo, TILE)
            s = (both_ref[1, :, here].astype(F32) * wide_ref[b : b + 1, here]).astype(BF16)
            a = (both_ref[0, :, here].astype(F32) * wide_ref[2 + b : 3 + b, here]).astype(BF16)
            dr += dot(s, qq_ref[1, at, here], nt)
            dw += dot(a, qq_ref[0, at, here], nt)
        keep_ref[pl.ds(0, half), at] = dw[:half]
        keep_ref[pl.ds(half, half), at] = dr[:half]
        send_ref[pl.ds(0, half), at] = dw[half:].astype(BF16)
        send_ref[pl.ds(half, half), at] = dr[half:].astype(BF16)


def kernel_outer(
    both_ref, keys_ref, qq_ref, gate_ref, gate_f_ref, in_ref, in_f_ref,
    cross_ref, p_ref, q_ref, small_ref, z_ref, rate_ref,
    grad_in_out, grad_gate_out, grad_step_out,
    grad_in_ref, grad_gate_ref, step_ref, sems,
):
    rows, cols = gate_ref.shape
    heads = small_ref.shape[1]
    copies = []

    def leave(src, dst):
        copies.append(pltpu.make_async_copy(src, dst, sems.at[len(copies)]))
        copies[-1].start()

    sums = []
    for b in range(2):
        at = at_block(b)
        parts = [[], []]
        select = []
        for lo in range(0, cols, TILE):
            here = pl.ds(lo, TILE)
            v = dot(keys_ref[1, at, :], both_ref[1, :, here])
            z = dot(keys_ref[0, at, :], both_ref[0, :, here])
            grad_gate_ref[at, here] = (
                gate_ref[at, here].astype(F32) + gate_f_ref[at, here].astype(F32) * v
            ).astype(BF16)
            grad_in_ref[at, here] = (
                in_ref[at, here].astype(F32) + in_f_ref[at, here].astype(F32) * z
            ).astype(BF16)
            for side, got in enumerate((z, v)):
                parts[side] += pieces(qq_ref[side, at, here].astype(F32) * got, 2)
            select += [selector(heads, lo, TILE)] * 2
        leave(grad_gate_ref.at[at], grad_gate_out.at[at])
        leave(grad_in_ref.at[at], grad_in_out.at[at])
        select = jnp.concatenate(select, axis=0)
        sums.append([
            dot(jnp.concatenate(parts[side], axis=1), select)
            * small_ref[(2 if side == 0 else 0) + b : (3 if side == 0 else 1) + b]
            for side in range(2)
        ])
    q, p = (jnp.concatenate([sums[b][side] for b in range(2)], axis=0) for side in range(2))
    ends = jnp.sum(q, axis=0, keepdims=True) + small_ref[5:6] * cross_ref[0:1]
    q = q + q_ref[...]
    flow = split_dot_left(triangle(rows, False), p + p_ref[...] - q, 3) + ends
    z = z_ref[...]
    grad = (q / softplus(z) - jnp.exp(rate_ref[...]) * flow) / (1.0 + jnp.exp(-z))
    step_ref[...] = grad.T
    leave(step_ref, grad_step_out)
    for copy in copies:
        copy.wait()


def kernel_add(a_ref, b_ref, c_ref, d_ref, out_ref):
    out_ref[...] = (a_ref[...] + b_ref[...]) + (c_ref[...] + d_ref[...])


def kernel_finish(
    keep_ref, got_ref, a_ref, b_ref, c_ref, d_ref, w_ref, r_ref, rate_ref, skip_ref, bias_ref
):
    half = w_ref.shape[0]
    w_ref[...] = keep_ref[pl.ds(0, half), :] + got_ref[pl.ds(0, half), :].astype(F32)
    r_ref[...] = keep_ref[pl.ds(half, half), :] + got_ref[pl.ds(half, half), :].astype(F32)
    sums = (a_ref[...] + b_ref[...]) + (c_ref[...] + d_ref[...])
    rate_ref[...] = sums[0:1]
    skip_ref[...] = sums[1:2]
    bias_ref[...] = sums[2:3]


V = pltpu.VMEM
ANY = pl.ANY


def call(kernel, outs, args, scratch=(), us=3.0, spaces=None, out_spaces=None, alias=None):
    spaces = spaces or [V] * len(args)
    out_spaces = out_spaces or [V] * len(outs)
    return pl.pallas_call(
        kernel,
        out_shape=[jax.ShapeDtypeStruct(s, d) for s, d in outs],
        in_specs=[pl.BlockSpec(memory_space=s) for s in spaces],
        out_specs=[pl.BlockSpec(memory_space=s) for s in out_spaces],
        scratch_shapes=list(scratch),
        input_output_aliases=alias or {},
        compiler_params=pltpu.CompilerParams(vmem_limit_bytes=36 * 1024 * 1024),
        cost_estimate=pl.CostEstimate(
            flops=int(us * 1e9), bytes_accessed=int(us * 1e6), transcendentals=0
        ),
    )(*args)


def exchange(array, axis, mask):
    count = lax.axis_size(axis)
    pairs = [(i, i ^ mask) for i in range(count) if i ^ mask < count]
    return lax.ppermute(array, axis, pairs)


def cycle(array, axis, by):
    count = lax.axis_size(axis)
    return lax.ppermute(array, axis, [(i, (i + by) % count) for i in range(count)])


def body(
    head_inputs,
    gate_inputs,
    step_raw,
    state_write,
    state_read,
    log_rate,
    skip_gain,
    step_bias,
    grad_gated,
):
    x, g, dy = head_inputs[0], gate_inputs[0], grad_gated[0]
    raw = step_raw[0].T
    heads, rows = raw.shape
    cols = x.shape[1]
    half = state_write.shape[2]
    w, r = state_write[0].T, state_read[0].T
    wt, rt = exchange(w, "tensor", 1), exchange(r, "tensor", 1)
    rate, skip, bias = (v.reshape(1, heads) for v in (log_rate, skip_gain, step_bias))
    payload = ((cols + 16, STATE), BF16)
    big = ((rows, cols), BF16)
    pair = ((2, rows, cols), BF16)
    thin = ((rows, heads), F32)
    tiny = ((8, heads), F32)
    one = ((1, heads), F32)
    key = ((half, rows), BF16)
    x, g, dy, w, r, skip, qq, z, rate, al, be, wide, small = call(
        kernel_scale,
        [big, big, big, key, key, one, pair, thin, one, thin, thin, ((8, cols), F32), tiny],
        [
            pltpu.with_memory_space_constraint(v, pltpu.HBM)
            for v in (x, g, dy, raw, bias, rate, skip, w, r)
        ],
        [V((heads, rows), F32), V((1, heads), F32), pltpu.SemaphoreType.DMA((12,))],
        spaces=[pltpu.HBM] * 9,
    )
    turned, send_up, send_down, send_h = call(
        kernel_states,
        [((2, STATE, rows), BF16), payload, payload, payload],
        [w, wt, r, rt, qq, wide],
    )
    got_up, got_down = cycle(send_up, "context", 1), cycle(send_down, "context", -1)
    got_h = exchange(send_h, "context", 2)
    state = ((2, STATE, cols), BF16)
    gate, gate_f, inp, inp_f, dr, dw, keys, p, q, probe, local = call(
        kernel_within,
        [big] * 4 + [((STATE, rows), F32)] * 2
        + [((2, rows, STATE), BF16), thin, thin, ((2, 2, STATE, cols), BF16), tiny],
        [x, g, dy, skip, turned, qq, al, be, wide, z, rate, small],
        [V((6 * rows + 8, TILE), F32)],
        us=4.0,
    )
    sums, both, cross = call(
        kernel_sums, [tiny, state, tiny], [got_up, got_down, got_h, probe, local], us=0.5,
    )
    others = [exchange(sums, "context", mask) for mask in (1, 2, 3)]
    keep, send = call(
        kernel_keys, [((STATE, rows), F32), ((STATE, rows), BF16)],
        [both, qq, wide, dr, dw], us=1.0,
    )
    grad_in, grad_gate, grad_step = call(
        kernel_outer, [big, big, ((heads, rows), F32)],
        [both, keys, qq, gate, gate_f, inp, inp_f, cross, p, q, small, z, rate],
        [V((rows, cols), BF16)] * 2 + [V((heads, rows), F32), pltpu.SemaphoreType.DMA((5,))],
        us=2.0, out_spaces=[pltpu.HBM] * 3,
    )
    (sums,) = call(kernel_add, [tiny], [sums] + others, us=0.1)
    got = exchange(send, "tensor", 1)
    others = [exchange(sums, "dp", mask) for mask in (1, 2, 3)]
    grad_w, grad_r, sum_rate, sum_skip, sum_bias = call(
        kernel_finish,
        [((half, rows), F32)] * 2 + [one] * 3,
        [keep, got, sums] + others,
        us=0.2,
    )
    return (
        grad_in[None],
        grad_gate[None],
        grad_w.T[None],
        grad_r.T[None],
        grad_step.T[None],
        sum_rate.reshape(heads),
        sum_skip.reshape(heads),
        sum_bias.reshape(heads),
    )


def solution(mesh):
    wide = P("dp", "context", "tensor")
    head = P("tensor")
    return jax.shard_map(
        body,
        mesh=mesh,
        in_specs=(wide,) * 5 + (head,) * 3 + (wide,),
        out_specs=(wide,) * 5 + (head,) * 3,
        check_vma=False,
    )
```
